32 devices in a mesh: crop: 4 (over y, x), row: 4 (over z), col: 2 (over core).
Axes of the slice: x: 2, y: 2, z: 4, core: 2. Of those that a mesh axis runs over, the one named last changes fastest.
Arguments:
- pair_acts: bfloat16 [4, 512, 512, 128], P('crop', 'row', 'col'), may hold values from -6 to 6
- residue_mask: int32 [4, 512], P('crop'), may hold values 0 or 1
- dist_bins: int32 [4, 512, 512], P('crop', 'row', 'col'), may hold values from 0 to 63
- w_in: float32 [128, 640], replicated, may hold values from -0.5 to 0.5
- w_out: float32 [128, 128], replicated, may hold values from -0.5 to 0.5
- w_t1: float32 [128, 512], replicated, may hold values from -0.5 to 0.5
- w_t2: float32 [512, 128], replicated, may hold values from -0.25 to 0.25
- w_dist: float32 [128, 64], replicated, may hold values from -0.5 to 0.5
- norm_params: float32 [6, 128], replicated, may hold values from -0.6 to 1.45
- dist_bias: float32 [64], replicated, may hold values from -3 to 3
- m_in: float32 [128, 640], replicated, may hold values from -2.2888184e-05 to 2.2888184e-05
- m_out: float32 [128, 128], replicated, may hold values from -2.2888184e-05 to 2.2888184e-05
- m_t1: float32 [128, 512], replicated, may hold values from -2.2888184e-05 to 2.2888184e-05
- m_t2: float32 [512, 128], replicated, may hold values from -2.2888184e-05 to 2.2888184e-05
- m_dist: float32 [128, 64], replicated, may hold values from -2.2888184e-05 to 2.2888184e-05
- m_norm: float32 [6, 128], replicated, may hold values from -7.6293945e-05 to 7.6293945e-05
- m_bias: float32 [64], replicated, may hold values from -7.6293945e-05 to 7.6293945e-05
- v_in: float32 [128, 640], replicated, may hold values from 1.6778523e-12 to 6.711409e-12
- v_out: float32 [128, 128], replicated, may hold values from 1.6778523e-12 to 6.711409e-12
- v_t1: float32 [128, 512], replicated, may hold values from 1.6778523e-12 to 6.711409e-12
- v_t2: float32 [512, 128], replicated, may hold values from 1.6778523e-12 to 6.711409e-12
- v_dist: float32 [128, 64], replicated, may hold values from 1.6778523e-12 to 6.711409e-12
- v_norm: float32 [6, 128], replicated, may hold values from 1.510067e-11 to 6.040268e-11
- v_bias: float32 [64], replicated, may hold values from 1.510067e-11 to 6.040268e-11
Outputs:
- new_w_in: float32 [128, 640], replicated
- new_w_out: float32 [128, 128], replicated
- new_w_t1: float32 [128, 512], replicated
- new_w_t2: float32 [512, 128], replicated
- new_w_dist: float32 [128, 64], replicated
- new_norm: float32 [6, 128], replicated
- new_bias: float32 [64], replicated
- new_m_in: float32 [128, 640], replicated
- new_m_out: float32 [128, 128], replicated
- new_m_t1: float32 [128, 512], replicated
- new_m_t2: float32 [512, 128], replicated
- new_m_dist: float32 [128, 64], replicated
- new_m_norm: float32 [6, 128], replicated
- new_m_bias: float32 [64], replicated
- new_v_in: float32 [128, 640], replicated
- new_v_out: float32 [128, 128], replicated
- new_v_t1: float32 [128, 512], replicated
- new_v_t2: float32 [512, 128], replicated
- new_v_dist: float32 [128, 64], replicated
- new_v_norm: float32 [6, 128], replicated
- new_v_bias: float32 [64], replicated
- loss_sum: float32 [], replicated
- pair_total: float32 [], replicated
- grad_norm: float32 [], replicated
The draws below stay inside these ranges and needn't reach their ends.
All inputs are finite; a program needn't handle non-finite values. No bound on the sum of `residue_mask` on one device may be relied on, other than what follows from the above.
Results may differ from the reference program's by a relative error of at most 0.006.
Values may be sent and summed in bfloat16 or wider, within the bound.
A program may use at most 640 MiB of HBM per device.

```python
import math
import jax
import jax.numpy as jnp
from jax import lax

C = 128
CH = 128
TR = 512
BINS = 64
L = 512
STEP = 10
CROPS = 4
PARAMS = 238400


def draw_norm_params(key, part):
    key = jax.random.fold_in(key, 1)
    key_gain, key_shift = jax.random.split(key)
    gain_rows = 1.0 + 0.15 * jnp.clip(jax.random.normal(key_gain, (6, C), jnp.float32), -3.0, 3.0)
    shift_rows = 0.2 * jnp.clip(jax.random.normal(key_shift, (6, C), jnp.float32), -3.0, 3.0)
    parity = (jnp.arange(6) % 2)[:, None]
    return jnp.where(parity == 0, gain_rows, shift_rows)


def touch_ends(entries, stream_key, least, top_value):
    spot = [jax.random.randint(jax.random.fold_in(stream_key, axis), (), 0, length) for axis, length in enumerate(entries.shape)]
    longest = entries.shape.index(max(entries.shape))
    beside = spot[:longest] + [(spot[longest] + 1) % entries.shape[longest]] + spot[longest + 1:]
    return entries.at[tuple(spot)].set(least).at[tuple(beside)].set(top_value)


def block_levels(stream_key, shape, shards, least, high):
    def one(axis_at, shards_of):
        steps = jax.random.uniform(jax.random.fold_in(jax.random.fold_in(stream_key, 6), axis_at), (shards_of,), jnp.float32, least / len(shards), high / len(shards))
        return jnp.repeat(jnp.exp(steps), shape[axis_at] // shards_of).reshape((-1,) + (1,) * (len(shape) - axis_at - 1))

    factor_of = one(*shards[0])
    for cut in shards[1:]:
        factor_of = factor_of * one(*cut)
    return factor_of


def scatter_about(rng, dims, deviation, most, pieces=(), dtype=jnp.bfloat16):
    factor_of = block_levels(rng, dims, pieces, -0.22, 0.18) if pieces else 1.0
    result = jax.random.normal(rng, dims, jnp.float32) * deviation * factor_of
    return jnp.minimum(jnp.maximum(result, -most), most).astype(dtype)


def setup_inputs(seed: int = 0) -> dict:
    keys = jax.random.split(jax.random.key(seed), 25)
    return {
        "pair_acts": scatter_about(keys[0], (CROPS, L, L, C), 1.0, 6.0, ((0, 4), (1, 4), (2, 2))),
        "residue_mask": touch_ends((jax.random.randint(keys[1], (CROPS, L), 0, 8) < 7).astype(jnp.int32), jax.random.fold_in(keys[1], 1), 0, 1),
        "dist_bins": touch_ends(jax.random.randint(keys[2], (CROPS, L, L), 0, BINS), jax.random.fold_in(keys[2], 1), 0, BINS - 1).astype(jnp.int32),
        "w_in": scatter_about(keys[3], (C, 4 * CH + C), C ** -0.5, 0.5, (), jnp.float32),
        "w_out": scatter_about(keys[4], (CH, C), CH ** -0.5, 0.5, (), jnp.float32),
        "w_t1": scatter_about(keys[5], (C, TR), C ** -0.5, 0.5, (), jnp.float32),
        "w_t2": scatter_about(keys[6], (TR, C), TR ** -0.5, 0.25, (), jnp.float32),
        "w_dist": scatter_about(keys[7], (C, BINS), C ** -0.5, 0.5, (), jnp.float32),
        "norm_params": draw_norm_params(jax.random.fold_in(keys[24], 71), 0),
        "dist_bias": scatter_about(keys[9], (BINS,), 0.5, 3.0, (), jnp.float32),
        "m_in": scatter_about(keys[10], (C, 4 * CH + C), (0.1 * 0.02 / PARAMS ** 0.5), 2.288818359375e-05, (), jnp.float32),
        "m_out": scatter_about(keys[11], (CH, C), (0.1 * 0.02 / PARAMS ** 0.5), 2.288818359375e-05, (), jnp.float32),
        "m_t1": scatter_about(keys[12], (C, TR), (0.1 * 0.02 / PARAMS ** 0.5), 2.288818359375e-05, (), jnp.float32),
        "m_t2": scatter_about(keys[13], (TR, C), (0.1 * 0.02 / PARAMS ** 0.5), 2.288818359375e-05, (), jnp.float32),
        "m_dist": scatter_about(keys[14], (C, BINS), (0.1 * 0.02 / PARAMS ** 0.5), 2.288818359375e-05, (), jnp.float32),
        "m_norm": scatter_about(keys[15], (6, C), (0.3 * 0.02 / PARAMS ** 0.5), 7.62939453125e-05, (), jnp.float32),
        "m_bias": scatter_about(keys[16], (BINS,), (0.3 * 0.02 / PARAMS ** 0.5), 7.62939453125e-05, (), jnp.float32),
        "v_in": jnp.clip(jnp.exp(jax.random.uniform(keys[17], (C, 4 * CH + C), jnp.float32, math.log(1.6778523015403835e-12), math.log(6.711409206161534e-12))), 1.6778523015403835e-12, 6.711409206161534e-12),
        "v_out": jnp.clip(jnp.exp(jax.random.uniform(keys[18], (CH, C), jnp.float32, math.log(1.6778523015403835e-12), math.log(6.711409206161534e-12))), 1.6778523015403835e-12, 6.711409206161534e-12),
        "v_t1": jnp.clip(jnp.exp(jax.random.uniform(keys[19], (C, TR), jnp.float32, math.log(1.6778523015403835e-12), math.log(6.711409206161534e-12))), 1.6778523015403835e-12, 6.711409206161534e-12),
        "v_t2": jnp.clip(jnp.exp(jax.random.uniform(keys[20], (TR, C), jnp.float32, math.log(1.6778523015403835e-12), math.log(6.711409206161534e-12))), 1.6778523015403835e-12, 6.711409206161534e-12),
        "v_dist": jnp.clip(jnp.exp(jax.random.uniform(keys[21], (C, BINS), jnp.float32, math.log(1.6778523015403835e-12), math.log(6.711409206161534e-12))), 1.6778523015403835e-12, 6.711409206161534e-12),
        "v_norm": jnp.clip(jnp.exp(jax.random.uniform(keys[22], (6, C), jnp.float32, math.log(1.510067071386345e-11), math.log(6.04026828554538e-11))), 1.510067071386345e-11, 6.04026828554538e-11),
        "v_bias": jnp.clip(jnp.exp(jax.random.uniform(keys[23], (BINS,), jnp.float32, math.log(1.510067071386345e-11), math.log(6.04026828554538e-11))), 1.510067071386345e-11, 6.04026828554538e-11),
    }


NORM_EPS = 1e-05
CLIP_NORM = 0.02
LEARN_RATE = 0.03
GAIN_RATE = 0.3
BETA_ONE = 0.9
BETA_TWO = 0.999
ADAM_EPS = 1e-08
WEIGHT_DECAY = 0.01

@jax.custom_vjp
def low(v):
    return lax.optimization_barrier(v.astype(jnp.bfloat16)).astype(jnp.float32)

@jax.custom_vjp
def low_back(v):
    return v

def low_keep(v):
    return (low(v), None)

def low_pass(kept, grad):
    return (grad,)

def back_keep(v):
    return (v, None)

def back_low(kept, grad):
    return (low(grad),)
low.defvjp(low_keep, low_pass)
low_back.defvjp(back_keep, back_low)

def layer_norm(values, gain, shift):
    center = values - lax.optimization_barrier(jnp.mean(values, -1, keepdims=True))
    spread = lax.optimization_barrier(jnp.mean(center * center, -1, keepdims=True))
    return center * lax.rsqrt(spread + NORM_EPS) * gain + shift

def linear(values, weight):
    return jnp.einsum('ijc,cd->ijd', values, weight, precision=lax.Precision.HIGHEST)

def crop_loss(params, acts, mask_vals, bins):
    w_in, w_out, w_t1, w_t2, w_dist, norm_params, dist_bias = params
    w_in, w_out, w_t1, w_t2, w_dist = [low(weight) for weight in (w_in, w_out, w_t1, w_t2, w_dist)]
    pair_mask = (mask_vals[:, None] * mask_vals[None, :])[..., None]
    pair_norm = low(layer_norm(acts, norm_params[0], norm_params[1]))
    projected = low_back(linear(pair_norm, w_in))
    left_proj = projected[..., :CH]
    left_gate = projected[..., CH:2 * CH]
    right_proj = projected[..., 2 * CH:3 * CH]
    right_gate = projected[..., 3 * CH:4 * CH]
    out_gate = projected[..., 4 * CH:]
    left_vals = low(pair_mask * jax.nn.sigmoid(left_gate) * left_proj)
    right_vals = low(pair_mask * jax.nn.sigmoid(right_gate) * right_proj)
    triangle = low_back(jnp.einsum('ikc,jkc->ijc', left_vals, right_vals, precision=lax.Precision.HIGHEST))
    tri_norm = low(layer_norm(triangle, norm_params[2], norm_params[3]))
    updated = acts + jax.nn.sigmoid(out_gate) * low_back(linear(tri_norm, w_out))
    trans_in = low(layer_norm(updated, norm_params[4], norm_params[5]))
    hidden = low(jax.nn.silu(low_back(linear(trans_in, w_t1))))
    final = updated + low_back(linear(hidden, w_t2))
    logits = low_back(linear(low(final), w_dist) + dist_bias)
    onehot = (bins[..., None] == jnp.arange(BINS)).astype(jnp.float32)
    entropy = jax.nn.logsumexp(logits, -1) - lax.optimization_barrier(jnp.sum(logits * onehot, -1))
    return jnp.sum(pair_mask[..., 0] * entropy)

def adamw_update(weight, first, second, grad, scale, rate):
    clipped = grad * scale
    first_new = BETA_ONE * first + (1.0 - BETA_ONE) * clipped
    second_new = BETA_TWO * second + (1.0 - BETA_TWO) * clipped * clipped
    first_hat = first_new / (1.0 - BETA_ONE ** STEP)
    second_hat = second_new / (1.0 - BETA_TWO ** STEP)
    stepped = weight - rate * (first_hat / (jnp.sqrt(second_hat) + ADAM_EPS) + WEIGHT_DECAY * weight)
    return (stepped, first_new, second_new)

def reference(pair_acts, residue_mask, dist_bins, w_in, w_out, w_t1, w_t2, w_dist, norm_params, dist_bias, m_in, m_out, m_t1, m_t2, m_dist, m_norm, m_bias, v_in, v_out, v_t1, v_t2, v_dist, v_norm, v_bias):
    mask_vals = residue_mask.astype(jnp.float32)
    per_crop = lax.optimization_barrier(jnp.sum(mask_vals, -1))
    pair_total = jnp.sum(per_crop * per_crop)
    acts = pair_acts.astype(jnp.float32)
    params = (w_in, w_out, w_t1, w_t2, w_dist, norm_params, dist_bias)

    def total(weights):

        def visit(carry, item):
            return (carry + jax.checkpoint(crop_loss)(weights, item[0], item[1], item[2]), None)
        summed, unused = lax.scan(visit, jnp.zeros((), jnp.float32), (acts, mask_vals, dist_bins))
        return summed
    loss_sum, pullback = jax.vjp(total, params)
    grads = pullback(jnp.ones((), jnp.float32) / pair_total)[0]
    squares = jnp.zeros((), jnp.float32)
    for grad in grads:
        squares = squares + jnp.sum(grad * grad)
    grad_norm = jnp.sqrt(squares)
    scale = CLIP_NORM / jnp.maximum(grad_norm, CLIP_NORM)
    firsts = (m_in, m_out, m_t1, m_t2, m_dist, m_norm, m_bias)
    seconds = (v_in, v_out, v_t1, v_t2, v_dist, v_norm, v_bias)
    rates = (LEARN_RATE, LEARN_RATE, LEARN_RATE, LEARN_RATE, LEARN_RATE, GAIN_RATE, GAIN_RATE)
    results = [adamw_update(params[index], firsts[index], seconds[index], grads[index], scale, rates[index]) for index in range(7)]
    return (results[0][0], results[1][0], results[2][0], results[3][0], results[4][0], results[5][0], results[6][0], results[0][1], results[1][1], results[2][1], results[3][1], results[4][1], results[5][1], results[6][1], results[0][2], results[1][2], results[2][2], results[3][2], results[4][2], results[5][2], results[6][2], loss_sum, pair_total, grad_norm)
```

```python
import functools

import jax
import jax.numpy as jnp
from jax import lax
from jax.experimental import pallas as pl
from jax.experimental.pallas import tpu as pltpu
from jax.sharding import PartitionSpec as P

STEP = 10


NORM_EPS = 1e-05
CLIP_NORM = 0.02
LEARN_RATE = 0.03
GAIN_RATE = 0.3
BETA_ONE = 0.9
BETA_TWO = 0.999
ADAM_EPS = 1e-08
WEIGHT_DECAY = 0.01


def standardize(values):
    center = values - jnp.mean(values, -1, keepdims=True)
    rstd = lax.rsqrt(jnp.mean(center * center, -1, keepdims=True) + NORM_EPS)
    return (center * rstd, rstd)


def standard_back(grad, normed, rstd):
    return rstd * (
        grad
        - jnp.mean(grad, -1, keepdims=True)
        - normed * jnp.mean(grad * normed, -1, keepdims=True)
    )


def linear(values, weight):
    return jnp.einsum("ijc,cd->ijd", values, weight, preferred_element_type=jnp.float32)


def weight_grad(values, grad):
    return jnp.einsum("ijc,ijd->cd", values, grad, preferred_element_type=jnp.float32)


def transposed(grad, weight):
    return jnp.einsum("ijd,cd->ijc", grad, weight, preferred_element_type=jnp.float32)


def adamw_update(weight, first, second, grad, scale, rate):
    clipped = grad * scale
    first_new = BETA_ONE * first + (1.0 - BETA_ONE) * clipped
    second_new = BETA_TWO * second + (1.0 - BETA_TWO) * clipped * clipped
    first_hat = first_new / (1.0 - BETA_ONE**STEP)
    second_hat = second_new / (1.0 - BETA_TWO**STEP)
    stepped = weight - rate * (
        first_hat / (jnp.sqrt(second_hat) + ADAM_EPS) + WEIGHT_DECAY * weight
    )
    return (stepped, first_new, second_new)


def on_device_general(
    pair_acts,
    residue_mask,
    dist_bins,
    w_in,
    w_out,
    w_t1,
    w_t2,
    w_dist,
    norm_params,
    dist_bias,
    m_in,
    m_out,
    m_t1,
    m_t2,
    m_dist,
    m_norm,
    m_bias,
    v_in,
    v_out,
    v_t1,
    v_t2,
    v_dist,
    v_norm,
    v_bias,
):
    tile_rows = pair_acts.shape[1]
    tile_cols = pair_acts.shape[2]
    width = w_out.shape[0]
    row_first = lax.axis_index("row") * tile_rows
    col_first = lax.axis_index("col") * tile_cols
    mask_vals = residue_mask[0].astype(jnp.float32)
    row_mask = lax.dynamic_slice_in_dim(mask_vals, row_first, tile_rows)
    col_mask = lax.dynamic_slice_in_dim(mask_vals, col_first, tile_cols)
    pair_mask = row_mask[:, None] * col_mask[None, :]
    mask_cube = pair_mask[..., None]
    pair_total = lax.psum(jnp.sum(pair_mask), ("crop", "row", "col"))
    low_in, low_out, low_t1, low_t2, low_dist = [
        weight.astype(jnp.bfloat16) for weight in (w_in, w_out, w_t1, w_t2, w_dist)
    ]
    acts = pair_acts[0].astype(jnp.float32)
    normed_one, rstd_one = standardize(acts)
    pair_norm = (normed_one * norm_params[0] + norm_params[1]).astype(jnp.bfloat16)
    projected = linear(pair_norm, low_in)
    left_proj = projected[..., :width]
    left_sig = jax.nn.sigmoid(projected[..., width : 2 * width])
    right_proj = projected[..., 2 * width : 3 * width]
    right_sig = jax.nn.sigmoid(projected[..., 3 * width : 4 * width])
    gate_sig = jax.nn.sigmoid(projected[..., 4 * width :])
    left_vals = (mask_cube * left_sig * left_proj).astype(jnp.bfloat16)
    right_vals = (mask_cube * right_sig * right_proj).astype(jnp.bfloat16)
    strips = lax.all_gather(right_vals, "row", axis=0, tiled=True)
    piece = strips
    triangle = jnp.transpose(
        lax.psum_scatter(
            jnp.einsum("jkc,ikc->jic", piece, left_vals, preferred_element_type=jnp.float32),
            "col",
            scatter_dimension=0,
            tiled=True,
        ),
        (1, 0, 2),
    )
    normed_two, rstd_two = standardize(triangle)
    tri_norm = (normed_two * norm_params[2] + norm_params[3]).astype(jnp.bfloat16)
    out_proj = linear(tri_norm, low_out)
    updated = acts + gate_sig * out_proj
    normed_three, rstd_three = standardize(updated)
    trans_in = (normed_three * norm_params[4] + norm_params[5]).astype(jnp.bfloat16)
    pre_act = linear(trans_in, low_t1)
    hidden = jax.nn.silu(pre_act).astype(jnp.bfloat16)
    final = updated + linear(hidden, low_t2)
    final_low = final.astype(jnp.bfloat16)
    logits = linear(final_low, low_dist) + dist_bias
    log_total = jax.nn.logsumexp(logits, -1)
    onehot = (dist_bins[0][..., None] == jnp.arange(w_dist.shape[1])).astype(jnp.float32)
    loss_local = jnp.sum(pair_mask * (log_total - jnp.sum(logits * onehot, -1)))
    d_logits = (mask_cube * (jnp.exp(logits - log_total[..., None]) - onehot) / pair_total).astype(
        jnp.bfloat16
    )
    grad_dist = weight_grad(final_low, d_logits)
    grad_bias = jnp.sum(d_logits.astype(jnp.float32), (0, 1))
    d_final = transposed(d_logits, low_dist)
    d_trans = d_final.astype(jnp.bfloat16)
    grad_t2 = weight_grad(hidden, d_trans)
    d_hidden = transposed(d_trans, low_t2)
    sig_pre = jax.nn.sigmoid(pre_act)
    d_pre = (d_hidden * sig_pre * (1.0 + pre_act * (1.0 - sig_pre))).astype(jnp.bfloat16)
    grad_t1 = weight_grad(trans_in, d_pre)
    d_trans_in = transposed(d_pre, low_t1)
    d_updated = d_final + standard_back(d_trans_in * norm_params[4], normed_three, rstd_three)
    d_out = (d_updated * gate_sig).astype(jnp.bfloat16)
    d_out_gate = d_updated * out_proj * gate_sig * (1.0 - gate_sig)
    grad_out = weight_grad(tri_norm, d_out)
    d_tri_norm = transposed(d_out, low_out)
    d_triangle = standard_back(d_tri_norm * norm_params[2], normed_two, rstd_two).astype(
        jnp.bfloat16
    )
    d_rows = lax.all_gather(d_triangle, "col", axis=1, tiled=True)
    d_left = jnp.einsum("ijc,jkc->ikc", d_rows, strips, preferred_element_type=jnp.float32)
    piece = d_rows
    d_right = lax.psum_scatter(
        jnp.einsum("ijc,ikc->jkc", piece, left_vals, preferred_element_type=jnp.float32).astype(
            jnp.bfloat16
        ),
        "row",
        scatter_dimension=0,
        tiled=True,
    ).astype(jnp.float32)
    d_proj = jnp.concatenate(
        [
            d_left * mask_cube * left_sig,
            d_left * mask_cube * left_proj * left_sig * (1.0 - left_sig),
            d_right * mask_cube * right_sig,
            d_right * mask_cube * right_proj * right_sig * (1.0 - right_sig),
            d_out_gate,
        ],
        -1,
    ).astype(jnp.bfloat16)
    grad_in = weight_grad(pair_norm, d_proj)
    d_pair_norm = transposed(d_proj, low_in)
    grad_norms = jnp.stack(
        [
            jnp.sum(d_pair_norm * normed_one, (0, 1)),
            jnp.sum(d_pair_norm, (0, 1)),
            jnp.sum(d_tri_norm * normed_two, (0, 1)),
            jnp.sum(d_tri_norm, (0, 1)),
            jnp.sum(d_trans_in * normed_three, (0, 1)),
            jnp.sum(d_trans_in, (0, 1)),
        ]
    )
    summed = lax.psum(
        (grad_in, grad_out, grad_t1, grad_t2, grad_dist, grad_norms, grad_bias, loss_local),
        ("crop", "row", "col"),
    )
    grads = summed[:7]
    squares = jnp.zeros((), jnp.float32)
    for grad in grads:
        squares = squares + jnp.sum(grad * grad)
    grad_norm = jnp.sqrt(squares)
    scale = CLIP_NORM / jnp.maximum(grad_norm, CLIP_NORM)
    params = (w_in, w_out, w_t1, w_t2, w_dist, norm_params, dist_bias)
    firsts = (m_in, m_out, m_t1, m_t2, m_dist, m_norm, m_bias)
    seconds = (v_in, v_out, v_t1, v_t2, v_dist, v_norm, v_bias)
    rates = (LEARN_RATE, LEARN_RATE, LEARN_RATE, LEARN_RATE, LEARN_RATE, GAIN_RATE, GAIN_RATE)
    results = [
        adamw_update(
            params[index], firsts[index], seconds[index], grads[index], scale, rates[index]
        )
        for index in range(7)
    ]
    return (
        results[0][0],
        results[1][0],
        results[2][0],
        results[3][0],
        results[4][0],
        results[5][0],
        results[6][0],
        results[0][1],
        results[1][1],
        results[2][1],
        results[3][1],
        results[4][1],
        results[5][1],
        results[6][1],
        results[0][2],
        results[1][2],
        results[2][2],
        results[3][2],
        results[4][2],
        results[5][2],
        results[6][2],
        summed[7],
        pair_total,
        grad_norm,
    )


F32 = jnp.float32
BF16 = jnp.bfloat16
NT = (((1,), (1,)), ((), ()))
NN = (((1,), (0,)), ((), ()))
TN = (((0,), (0,)), ((), ()))
VMEM_LIMIT = 56 * 1024 * 1024


def dot(left, right, dims=NN):
    return lax.dot_general(left, right, dims, preferred_element_type=F32)


def sigmoid(values):
    return 0.5 * jnp.tanh(0.5 * values) + 0.5


def column_stats(values):
    center = values - jnp.mean(values, 0, keepdims=True)
    rstd = lax.rsqrt(jnp.mean(center * center, 0, keepdims=True) + NORM_EPS)
    return center * rstd, rstd


def column_back(grad, normed, rstd):
    return rstd * (
        grad
        - jnp.mean(grad, 0, keepdims=True)
        - normed * jnp.mean(grad * normed, 0, keepdims=True)
    )


def widen(param, lanes):
    return jnp.concatenate([param] * (lanes // param.shape[1]), 1)


def spread_rows(scratch, block):
    channels, rows, lanes = block.shape
    for part in range(lanes // 128):
        scratch[part] = (
            block[:, :, 128 * part : 128 * part + 128].astype(F32).reshape(channels * rows, 128)
        )


def take_row(scratch, row, channels, rows):
    parts = [
        scratch[part, pl.ds(row, channels, stride=rows), :] for part in range(scratch.shape[0])
    ]
    return parts[0] if len(parts) == 1 else jnp.concatenate(parts, 1)


def put_row(scratch, row, values, rows):
    for part in range(scratch.shape[0]):
        scratch[part, pl.ds(row, values.shape[0], stride=rows), :] = values[
            :, 128 * part : 128 * part + 128
        ]


def gather_rows(scratch, out_ref):
    channels, rows, _ = out_ref.shape
    for part in range(scratch.shape[0]):
        out_ref[:, :, 128 * part : 128 * part + 128] = (
            scratch[part].reshape(channels, rows, 128).astype(out_ref.dtype)
        )


def call(kernel, grid, scalars, ins, outs, scratch, flops, name):
    moved = sum(a.size * a.dtype.itemsize for a, _, _ in ins)
    moved += sum(jnp.dtype(t).itemsize * functools.reduce(lambda x, y: x * y, s) for s, t, _, _ in outs)
    return pl.pallas_call(
        kernel,
        grid_spec=pltpu.PrefetchScalarGridSpec(
            num_scalar_prefetch=len(scalars),
            grid=grid,
            in_specs=[pl.BlockSpec(block, index) for _, block, index in ins],
            out_specs=[pl.BlockSpec(block, index) for _, _, block, index in outs],
            scratch_shapes=scratch,
        ),
        out_shape=[jax.ShapeDtypeStruct(shape, dtype) for shape, dtype, _, _ in outs],
        compiler_params=pltpu.CompilerParams(vmem_limit_bytes=VMEM_LIMIT),
        cost_estimate=pl.CostEstimate(flops=int(flops), bytes_accessed=int(moved), transcendentals=0),
        name=name,
    )(*scalars, *[a for a, _, _ in ins])


ROWS = 16


def project_kernel(row_mask, acts_ref, w_ref, ln_ref, col_ref, a_ref, b_ref, acts_s, a_s, b_s):
    first = pl.program_id(0) * ROWS
    width = a_ref.shape[0]
    spread_rows(acts_s, acts_ref[...])

    def one(row, carry):
        values = take_row(acts_s, row, acts_ref.shape[0], ROWS)
        lanes = values.shape[1]
        normed, _ = column_stats(values)
        low = (normed * widen(ln_ref[0], lanes) + widen(ln_ref[1], lanes)).astype(BF16)
        proj = dot(w_ref[...], low)
        mask = col_ref[...] * row_mask[first + row]
        put_row(a_s, row, proj[:width] * sigmoid(proj[width : 2 * width]) * mask, ROWS)
        put_row(b_s, row, proj[2 * width : 3 * width] * sigmoid(proj[3 * width :]) * mask, ROWS)
        return carry

    lax.fori_loop(0, ROWS, one, 0, unroll=4)
    gather_rows(a_s, a_ref)
    gather_rows(b_s, b_ref)


def fixed(*zeros):
    return lambda i, *_: zeros


def project(acts, w_proj, ln_wide, row_mask, col_mask):
    chans, rows, lanes = acts.shape
    block = (chans, ROWS, lanes)
    mid = lambda i, *_: (0, i, 0)
    out = ((chans, rows, lanes), BF16, block, mid)
    staged = pltpu.VMEM((lanes // 128, chans * ROWS, 128), F32)
    return call(
        project_kernel,
        (rows // ROWS,),
        [row_mask],
        [
            (acts, block, mid),
            (w_proj, w_proj.shape, fixed(0, 0)),
            (ln_wide, ln_wide.shape, fixed(0, 0, 0)),
            (col_mask, col_mask.shape, fixed(0, 0)),
        ],
        [out, out],
        [staged, staged, staged],
        2 * rows * lanes * w_proj.size * 4,
        "project",
    )


CHANS = 8


def triangle_kernel(flag, a0, a1, b0, b1, keep_ref, send_ref):
    kept_first = flag[0] == 0
    for chan in range(CHANS):
        rows = jnp.concatenate([a0[chan], a1[chan]], 0)
        one, two = dot(b0[chan], rows, NT), dot(b1[chan], rows, NT)
        keep_ref[chan] = jnp.where(kept_first, one, two)
        send_ref[chan] = jnp.where(kept_first, two, one).astype(BF16)


def triangle(which, a, b):
    chans, half, lanes = a[0].shape
    lead = lambda i, *_: (i, 0, 0)
    block = (CHANS, half, lanes)
    out = (chans, half, 2 * half)
    return call(
        triangle_kernel,
        (chans // CHANS,),
        [which],
        [(v, block, lead) for v in (*a, *b)],
        [(out, F32, (CHANS, half, 2 * half), lead), (out, BF16, (CHANS, half, 2 * half), lead)],
        [],
        2 * chans * half * 2 * half * 2 * lanes * 4,
        "triangle",
    )


GROUP = 2


def pair_kernel(
    place, x_keep, x_recv, acts_ref, code_ref, scale_ref, ln_ref, w_outT, w_out, w_ogT, w_t1T, w_t1,
    w_t2T, w_t2, w_distT, w_dist, bias_ref,
    dx_ref, g_t1, g_t2, g_out, g_og, g_dist, g_norm, g_bias, loss_ref,
    x_s, acts_s, dx_s,
):
    chans = acts_ref.shape[0]
    lanes = 128 * GROUP

    @pl.when(pl.program_id(0) == 0)
    def _():
        for ref in (g_t1, g_t2, g_out, g_og, g_dist, g_norm, g_bias, loss_ref):
            ref[...] = jnp.zeros_like(ref)

    x_s[0] = (x_keep[...] + x_recv[...].astype(F32)).reshape(chans * ROWS, 128)
    spread_rows(acts_s, acts_ref[...])
    inverse = scale_ref[0:1, :]
    param = [widen(ln_ref[index], lanes) for index in range(6)]
    bins = w_distT.shape[0]
    bin_index = lax.broadcasted_iota(jnp.int32, (bins, lanes), 0)

    def fold(values):
        return sum(values[:, 128 * part : 128 * part + 128] for part in range(GROUP))

    def group(step, carry):
        first = step * GROUP
        cat = lambda pieces: jnp.concatenate(pieces, 1)
        x = cat([take_row(x_s, first + u, chans, ROWS) for u in range(GROUP)])
        acts = cat([take_row(acts_s, first + u, chans, ROWS) for u in range(GROUP)])
        code = cat([code_ref[pl.ds(first + u, 1), :] for u in range(GROUP)])
        normed_two, rstd_two = column_stats(x)
        tri = (normed_two * param[2] + param[3]).astype(BF16)
        out = dot(w_outT[...], tri)
        normed_one, _ = column_stats(acts)
        low = (normed_one * param[0] + param[1]).astype(BF16)
        gate = sigmoid(dot(w_ogT[...], low))
        z1 = acts + gate * out
        normed_three, rstd_three = column_stats(z1)
        trans = (normed_three * param[4] + param[5]).astype(BF16)
        pre = dot(w_t1T[...], trans)
        sig = sigmoid(pre)
        act = pre * sig
        hidden = act.astype(BF16)
        slope = sig * (1.0 + (pre - act))
        final = (z1 + dot(w_t2T[...], hidden)).astype(BF16)
        logits = dot(w_distT[...], final) + widen(bias_ref[...], lanes)
        top = jnp.max(logits, 0, keepdims=True)
        powers = jnp.exp(logits - top)
        total = jnp.sum(powers, 0, keepdims=True)
        present = (code >= 0).astype(F32)
        hot = bin_index == code
        picked = jnp.sum(jnp.where(hot, logits, 0.0), 0, keepdims=True)
        loss_ref[...] += fold(present * (jnp.log(total) + top) - picked)
        weight = present * widen(inverse, lanes)
        d_logits = (
            powers * (weight / total) - jnp.where(hot, widen(inverse, lanes), 0.0)
        ).astype(BF16)
        g_dist[...] += dot(d_logits, final, NT)
        g_bias[...] += fold(d_logits.astype(F32))
        d_final = dot(w_dist[...], d_logits)
        d_trans = d_final.astype(BF16)
        g_t2[...] += dot(hidden, d_trans, NT)
        d_pre = (dot(w_t2[...], d_trans) * slope).astype(BF16)
        g_t1[...] += dot(d_pre, trans, NT)
        d_tn = dot(w_t1[...], d_pre)
        g_norm[2] += fold(d_tn * normed_three)
        g_norm[3] += fold(d_tn)
        d_z1 = d_final + column_back(d_tn * param[4], normed_three, rstd_three)
        d_gated = d_z1 * gate
        d_out = d_gated.astype(BF16)
        d_og = (d_gated * out * (1.0 - gate)).astype(BF16)
        g_out[...] += dot(d_out, tri, NT)
        g_og[...] += dot(d_og, jnp.concatenate([low, normed_one.astype(BF16)], 0), NT)
        g_norm[4] += fold(d_og.astype(F32))
        d_xn = dot(w_out[...], d_out)
        g_norm[0] += fold(d_xn * normed_two)
        g_norm[1] += fold(d_xn)
        d_x = column_back(d_xn * param[2], normed_two, rstd_two)
        for u in range(GROUP):
            put_row(dx_s, first + u, d_x[:, 128 * u : 128 * u + 128], ROWS)
        return carry

    lax.fori_loop(0, ROWS // GROUP, group, 0)
    gather_rows(dx_s, dx_ref)


def pair_block(place, x_keep, x_recv, acts_kj, code, scale, ln_wide, weights, bias):
    chans, rows, lanes = x_keep.shape
    block = (chans, ROWS, lanes)
    mid = lambda i, *_: (0, i, 0)

    def where(i, spot):
        return 8 * ((i // 2) ^ spot[0]) + 2 * spot[1] + i % 2

    full = [(w, w.shape, fixed(*([0] * w.ndim))) for w in (scale, ln_wide, *weights, bias)]
    sums = [(512, 128), (512, 128), (128, 128), (128, 256), (64, 128), (5, 128, 128), (64, 128), (1, 128)]
    return call(
        pair_kernel,
        (rows // ROWS,),
        [place],
        [
            (x_keep, block, mid),
            (x_recv, block, mid),
            (acts_kj, block, lambda i, spot: (0, where(i, spot), 0)),
            (code, (ROWS, lanes), lambda i, spot: (where(i, spot), 0)),
        ]
        + full,
        [((chans, rows, lanes), BF16, block, mid)]
        + [(s, F32, s, fixed(*([0] * len(s)))) for s in sums],
        [pltpu.VMEM((1, chans * ROWS, 128), F32)] * 3,
        rows * lanes * 35e9 / 32768 * 4,
        "pair",
    )


def right_back_kernel(flag, dx_own, dx_other, a0, a1, out0, out1):
    own_first = flag[0] == 0
    for chan in range(CHANS):
        rows = jnp.concatenate([a0[chan], a1[chan]], 0)
        own, other = dx_own[chan], dx_other[chan]
        both = jnp.concatenate(
            [jnp.where(own_first, own, other), jnp.where(own_first, other, own)], 0
        )
        grads = dot(both, rows).astype(BF16)
        half = out0.shape[1]
        out0[chan] = grads[:half]
        out1[chan] = grads[half:]


def right_back(which, dx_own, dx_other, a):
    chans, half, lanes = a[0].shape
    lead = lambda i, *_: (i, 0, 0)
    out = ((chans, half, lanes), BF16, (CHANS, half, lanes), lead)
    return call(
        right_back_kernel,
        (chans // CHANS,),
        [which],
        [(v, (CHANS, half, 2 * half), lead) for v in (dx_own, dx_other)]
        + [(v, (CHANS, half, lanes), lead) for v in a],
        [out, out],
        [],
        2 * chans * 4 * half * half * lanes * 4,
        "right_back",
    )


def left_back_kernel(flag, *refs):
    owns, others, firsts, seconds = refs[:4], refs[4:8], refs[8:12], refs[12:16]
    out0, out1 = refs[16:]
    half = out0.shape[1]
    for chan in range(CHANS):
        total = None
        for pair in range(2):
            own_first = flag[0] == pair
            grads, values = [], []
            for q in (2 * pair, 2 * pair + 1):
                own, other = owns[q][chan], others[q][chan]
                grads += [jnp.where(own_first, own, other), jnp.where(own_first, other, own)]
                values += [firsts[q][chan], seconds[q][chan]]
            term = dot(jnp.concatenate(grads, 0), jnp.concatenate(values, 0), TN)
            total = term if total is None else total + term
        total = total.astype(BF16)
        out0[chan] = total[:half]
        out1[chan] = total[half:]


def left_back(which, owns, others, firsts, seconds):
    chans, half, lanes = firsts[0].shape
    lead = lambda i, *_: (i, 0, 0)
    out = ((chans, half, lanes), BF16, (CHANS, half, lanes), lead)
    return call(
        left_back_kernel,
        (chans // CHANS,),
        [which],
        [(v, (CHANS, half, 2 * half), lead) for v in (*owns, *others)]
        + [(v, (CHANS, half, lanes), lead) for v in (*firsts, *seconds)],
        [out, out],
        [],
        2 * chans * 16 * half * half * lanes * 4,
        "left_back",
    )


def input_back_kernel(row_mask, acts_ref, w_ref, ln_ref, col_ref, *rest):
    grads, (g_ref, sum_ref), (acts_s, grad_s) = rest[:-4], rest[-4:-2], rest[-2:]
    first = pl.program_id(0) * ROWS
    chans = acts_ref.shape[0]
    width = grads[0].shape[0]

    @pl.when(pl.program_id(0) == 0)
    def _():
        g_ref[...] = jnp.zeros_like(g_ref)
        sum_ref[...] = jnp.zeros_like(sum_ref)

    spread_rows(acts_s, acts_ref[...])
    total = grads[0][...].astype(F32)
    for ref in grads[1:]:
        total = total + ref[...].astype(F32)
    spread_rows(grad_s, total)

    def one(row, carry):
        values = take_row(acts_s, row, chans, ROWS)
        lanes = values.shape[1]
        normed, _ = column_stats(values)
        low = (normed * widen(ln_ref[0], lanes) + widen(ln_ref[1], lanes)).astype(BF16)
        proj = dot(w_ref[...], low)
        gate = sigmoid(proj[width:])
        d_value = take_row(grad_s, row, width, ROWS) * (col_ref[...] * row_mask[first + row]) * gate
        d_gate = d_value * proj[:width] * (1.0 - gate)
        d_proj = jnp.concatenate([d_value.astype(BF16), d_gate.astype(BF16)], 0)
        g_ref[...] += dot(d_proj, jnp.concatenate([low, normed.astype(BF16)], 0), NT)
        wide = d_proj.astype(F32)
        sum_ref[...] += sum(wide[:, 128 * u : 128 * u + 128] for u in range(lanes // 128))
        return carry

    lax.fori_loop(0, ROWS, one, 0, unroll=4)


def input_back(acts, w_part, ln_wide, row_mask, col_mask, grads):
    chans, rows, lanes = acts.shape
    block = (chans, ROWS, lanes)
    mid = lambda i, *_: (0, i, 0)
    staged = pltpu.VMEM((lanes // 128, chans * ROWS, 128), F32)
    depth = w_part.shape[0]
    return call(
        input_back_kernel,
        (rows // ROWS,),
        [row_mask],
        [
            (acts, block, mid),
            (w_part, w_part.shape, fixed(0, 0)),
            (ln_wide, ln_wide.shape, fixed(0, 0, 0)),
            (col_mask, col_mask.shape, fixed(0, 0)),
        ]
        + [(v, block, mid) for v in grads],
        [((depth, 2 * chans), F32, (depth, 2 * chans), fixed(0, 0)), ((depth, 128), F32, (depth, 128), fixed(0, 0))],
        [staged, staged],
        2 * rows * lanes * w_part.size * 3 * 4,
        "input_back",
    )


def on_device_planes(
    pair_acts, residue_mask, dist_bins, w_in, w_out, w_t1, w_t2, w_dist, norm_params, dist_bias, *moments
):
    firsts, seconds = moments[:7], moments[7:]
    spot = lax.axis_index("crop")
    level = lax.axis_index("row")
    side = lax.axis_index("col")
    rows, cols, chans = pair_acts.shape[1:]
    width = w_out.shape[0]
    sub = rows // 4

    def over_x(v):
        return lax.ppermute(v, "crop", [(g, g ^ 1) for g in range(4)])

    def over_y(v):
        return lax.ppermute(v, "crop", [(g, g ^ 2) for g in range(4)])

    def over_core(v):
        return lax.ppermute(v, "col", [(0, 1), (1, 0)])

    def to_plane(v, label):
        start = (spot ^ level ^ label) * sub
        piece = lax.dynamic_slice_in_dim(v, start, sub, v.ndim - 2)
        one = [(c * 4 + z, (c ^ label ^ z) * 4 + z) for c in range(4) for z in range(4)]
        two = [(g * 4 + z, g * 4 + (g ^ label ^ z)) for g in range(4) for z in range(4)]
        return lax.ppermute(lax.ppermute(piece, ("crop", "row"), one), ("crop", "row"), two)

    all_masks = lax.all_gather(residue_mask[0], "crop", axis=0).astype(F32)
    pair_total = jnp.sum(jnp.square(jnp.sum(all_masks, -1)))
    mask_vals = lax.dynamic_index_in_dim(all_masks, level, 0, keepdims=False)
    acts_major = jnp.transpose(pair_acts[0], (2, 0, 1))
    pieces = [to_plane(acts_major, label) for label in range(4)]
    acts = [jnp.concatenate(pieces[2 * h : 2 * h + 2], 1) for h in range(2)]
    acts_kj = jnp.swapaxes(jnp.concatenate(acts, 1), 1, 2)
    bins = jnp.concatenate([to_plane(dist_bins[0], label) for label in range(4)], 0)
    row_mask = jnp.concatenate(
        [
            lax.dynamic_slice_in_dim(mask_vals, rows * (spot ^ level ^ label) + sub * spot, sub)
            for label in range(4)
        ]
    )
    col_mask = lax.dynamic_slice_in_dim(mask_vals, cols * side, cols)
    code = jnp.where((col_mask[:, None] * row_mask[None, :]) > 0, bins.T, -1)

    low_in, low_out, low_t1, low_t2, low_dist = [
        weight.astype(BF16) for weight in (w_in, w_out, w_t1, w_t2, w_dist)
    ]
    ln_wide = jnp.broadcast_to(norm_params[:, :, None], (*norm_params.shape, 128))
    bias_wide = jnp.broadcast_to(dist_bias[:, None], (dist_bias.shape[0], 128))
    scale_wide = jnp.full((8, 128), 1.0 / pair_total, F32)
    col_row = col_mask[None, :]
    half_mask = [row_mask[: 2 * sub], row_mask[2 * sub :]]
    in_T = low_in.T

    a, b_own = [], []
    for h in range(2):
        left, right = project(acts[h], in_T[: 4 * width], ln_wide, half_mask[h], col_row)
        a.append(left)
        b_own.append(right)
    b_x = [over_x(v) for v in b_own]
    b_y = [over_y(v) for v in b_own]
    b_d = [over_y(b_x[0]), over_x(b_y[1])]
    blocks = [b_own, b_x, b_y, b_d]

    weights = (
        low_out.T, low_out, in_T[4 * width :], low_t1.T, low_t1, low_t2.T, low_t2, low_dist.T, low_dist,
    )
    dx_own, dx_other, sums, flags = [], [], None, []
    keeps, sends = [], []
    for q in range(4):
        owner = spot ^ q
        flags.append((side ^ (owner // 2) ^ (level // 2)).astype(jnp.int32)[None])
        keep, send = triangle(flags[q], a, blocks[q])
        keeps.append(keep)
        sends.append(over_core(send))
    for q in range(4):
        owner = spot ^ q
        place = jnp.stack([(owner ^ level) & 1, owner]).astype(jnp.int32)
        d_x, *parts = pair_block(
            place, keeps[q], sends[q], acts_kj, code, scale_wide, ln_wide, weights, bias_wide
        )
        dx_own.append(d_x)
        dx_other.append(over_core(d_x))
        sums = parts if sums is None else [u + v for u, v in zip(sums, parts)]
    back = [right_back(flags[q], dx_own[q], dx_other[q], a) for q in range(4)]
    own0 = [back[0][0], over_y(back[2][0])]
    x0 = (back[1][0].astype(F32) + over_y(back[3][0]).astype(F32)).astype(BF16)
    own0.append(over_x(x0))
    own1 = [back[0][1], over_x(back[1][1])]
    y1 = (back[2][1].astype(F32) + over_x(back[3][1]).astype(F32)).astype(BF16)
    own1.append(over_y(y1))
    d_left = left_back(
        flags[0], dx_own, dx_other, [v[0] for v in blocks], [v[1] for v in blocks]
    )
    left_sums = [
        input_back(acts[h], in_T[: 2 * width], ln_wide, half_mask[h], col_row, [d_left[h]])
        for h in range(2)
    ]
    right_sums = [
        input_back(acts[h], in_T[2 * width : 4 * width], ln_wide, half_mask[h], col_row, own)
        for h, own in enumerate((own0, own1))
    ]

    g_t1, g_t2, g_out, g_og, g_dist, g_norm, g_bias, loss = sums
    outer = jnp.concatenate(
        [
            left_sums[0][0] + left_sums[1][0],
            right_sums[0][0] + right_sums[1][0],
            g_og,
        ],
        0,
    )
    norm_sums = jnp.sum(g_norm, -1)
    totals = jnp.concatenate(
        [
            jnp.sum(left_sums[0][1] + left_sums[1][1], -1),
            jnp.sum(right_sums[0][1] + right_sums[1][1], -1),
            norm_sums[4],
        ]
    )
    wide_in = in_T.astype(F32)
    grad_norms = jnp.concatenate(
        [
            jnp.sum(wide_in * outer[:, chans:], 0)[None],
            jnp.sum(wide_in * totals[:, None], 0)[None],
            norm_sums[:4],
        ],
        0,
    )
    summed = lax.psum(
        (
            outer[:, :chans],
            g_out,
            g_t1,
            g_t2,
            g_dist,
            grad_norms,
            jnp.sum(g_bias, -1),
            jnp.sum(loss),
        ),
        ("crop", "row", "col"),
    )
    grads = (
        summed[0].T,
        summed[1].T,
        summed[2].T,
        summed[3],
        summed[4].T,
        summed[5],
        summed[6],
    )
    squares = jnp.zeros((), F32)
    for grad in grads:
        squares = squares + jnp.sum(grad * grad)
    grad_norm = jnp.sqrt(squares)
    scale = CLIP_NORM / jnp.maximum(grad_norm, CLIP_NORM)
    params = (w_in, w_out, w_t1, w_t2, w_dist, norm_params, dist_bias)
    rates = (LEARN_RATE,) * 5 + (GAIN_RATE,) * 2
    results = [
        adamw_update(*terms, scale, rate)
        for *terms, rate in zip(params, firsts, seconds, grads, rates)
    ]
    return (
        *[r[0] for r in results],
        *[r[1] for r in results],
        *[r[2] for r in results],
        summed[7],
        pair_total,
        grad_norm,
    )


def solution(mesh):
    planes = mesh.shape["crop"] == 4 and mesh.shape["row"] == 4 and mesh.shape["col"] == 2
    body = on_device_planes if planes else on_device_general
    in_specs = (
        P("crop", "row", "col", None),
        P("crop", None),
        P("crop", "row", "col"),
    ) + (P(),) * 21
    return jax.shard_map(
        body, mesh=mesh, in_specs=in_specs, out_specs=(P(),) * 24, check_vma=False
    )
```

```python
import functools

import jax
import jax.numpy as jnp
from jax import lax
from jax.experimental import pallas as pl
from jax.experimental.pallas import tpu as pltpu
from jax.sharding import PartitionSpec as P

STEP = 10


NORM_EPS = 1e-05
CLIP_NORM = 0.02
LEARN_RATE = 0.03
GAIN_RATE = 0.3
BETA_ONE = 0.9
BETA_TWO = 0.999
ADAM_EPS = 1e-08
WEIGHT_DECAY = 0.01


def standardize(values):
    center = values - jnp.mean(values, -1, keepdims=True)
    rstd = lax.rsqrt(jnp.mean(center * center, -1, keepdims=True) + NORM_EPS)
    return (center * rstd, rstd)


def standard_back(grad, normed, rstd):
    return rstd * (
        grad
        - jnp.mean(grad, -1, keepdims=True)
        - normed * jnp.mean(grad * normed, -1, keepdims=True)
    )


def linear(values, weight):
    return jnp.einsum("ijc,cd->ijd", values, weight, preferred_element_type=jnp.float32)


def weight_grad(values, grad):
    return jnp.einsum("ijc,ijd->cd", values, grad, preferred_element_type=jnp.float32)


def transposed(grad, weight):
    return jnp.einsum("ijd,cd->ijc", grad, weight, preferred_element_type=jnp.float32)


def adamw_update(weight, first, second, grad, scale, rate):
    clipped = grad * scale
    first_new = BETA_ONE * first + (1.0 - BETA_ONE) * clipped
    second_new = BETA_TWO * second + (1.0 - BETA_TWO) * clipped * clipped
    first_hat = first_new / (1.0 - BETA_ONE**STEP)
    second_hat = second_new / (1.0 - BETA_TWO**STEP)
    stepped = weight - rate * (
        first_hat / (jnp.sqrt(second_hat) + ADAM_EPS) + WEIGHT_DECAY * weight
    )
    return (stepped, first_new, second_new)


def on_device_general(
    pair_acts,
    residue_mask,
    dist_bins,
    w_in,
    w_out,
    w_t1,
    w_t2,
    w_dist,
    norm_params,
    dist_bias,
    m_in,
    m_out,
    m_t1,
    m_t2,
    m_dist,
    m_norm,
    m_bias,
    v_in,
    v_out,
    v_t1,
    v_t2,
    v_dist,
    v_norm,
    v_bias,
):
    tile_rows = pair_acts.shape[1]
    tile_cols = pair_acts.shape[2]
    width = w_out.shape[0]
    row_first = lax.axis_index("row") * tile_rows
    col_first = lax.axis_index("col") * tile_cols
    mask_vals = residue_mask[0].astype(jnp.float32)
    row_mask = lax.dynamic_slice_in_dim(mask_vals, row_first, tile_rows)
    col_mask = lax.dynamic_slice_in_dim(mask_vals, col_first, tile_cols)
    pair_mask = row_mask[:, None] * col_mask[None, :]
    mask_cube = pair_mask[..., None]
    pair_total = lax.psum(jnp.sum(pair_mask), ("crop", "row", "col"))
    low_in, low_out, low_t1, low_t2, low_dist = [
        weight.astype(jnp.bfloat16) for weight in (w_in, w_out, w_t1, w_t2, w_dist)
    ]
    acts = pair_acts[0].astype(jnp.float32)
    normed_one, rstd_one = standardize(acts)
    pair_norm = (normed_one * norm_params[0] + norm_params[1]).astype(jnp.bfloat16)
    projected = linear(pair_norm, low_in)
    left_proj = projected[..., :width]
    left_sig = jax.nn.sigmoid(projected[..., width : 2 * width])
    right_proj = projected[..., 2 * width : 3 * width]
    right_sig = jax.nn.sigmoid(projected[..., 3 * width : 4 * width])
    gate_sig = jax.nn.sigmoid(projected[..., 4 * width :])
    left_vals = (mask_cube * left_sig * left_proj).astype(jnp.bfloat16)
    right_vals = (mask_cube * right_sig * right_proj).astype(jnp.bfloat16)
    strips = lax.all_gather(right_vals, "row", axis=0, tiled=True)
    piece = strips
    triangle = jnp.transpose(
        lax.psum_scatter(
            jnp.einsum("jkc,ikc->jic", piece, left_vals, preferred_element_type=jnp.float32),
            "col",
            scatter_dimension=0,
            tiled=True,
        ),
        (1, 0, 2),
    )
    normed_two, rstd_two = standardize(triangle)
    tri_norm = (normed_two * norm_params[2] + norm_params[3]).astype(jnp.bfloat16)
    out_proj = linear(tri_norm, low_out)
    updated = acts + gate_sig * out_proj
    normed_three, rstd_three = standardize(updated)
    trans_in = (normed_three * norm_params[4] + norm_params[5]).astype(jnp.bfloat16)
    pre_act = linear(trans_in, low_t1)
    hidden = jax.nn.silu(pre_act).astype(jnp.bfloat16)
    final = updated + linear(hidden, low_t2)
    final_low = final.astype(jnp.bfloat16)
    logits = linear(final_low, low_dist) + dist_bias
    log_total = jax.nn.logsumexp(logits, -1)
    onehot = (dist_bins[0][..., None] == jnp.arange(w_dist.shape[1])).astype(jnp.float32)
    loss_local = jnp.sum(pair_mask * (log_total - jnp.sum(logits * onehot, -1)))
    d_logits = (mask_cube * (jnp.exp(logits - log_total[..., None]) - onehot) / pair_total).astype(
        jnp.bfloat16
    )
    grad_dist = weight_grad(final_low, d_logits)
    grad_bias = jnp.sum(d_logits.astype(jnp.float32), (0, 1))
    d_final = transposed(d_logits, low_dist)
    d_trans = d_final.astype(jnp.bfloat16)
    grad_t2 = weight_grad(hidden, d_trans)
    d_hidden = transposed(d_trans, low_t2)
    sig_pre = jax.nn.sigmoid(pre_act)
    d_pre = (d_hidden * sig_pre * (1.0 + pre_act * (1.0 - sig_pre))).astype(jnp.bfloat16)
    grad_t1 = weight_grad(trans_in, d_pre)
    d_trans_in = transposed(d_pre, low_t1)
    d_updated = d_final + standard_back(d_trans_in * norm_params[4], normed_three, rstd_three)
    d_out = (d_updated * gate_sig).astype(jnp.bfloat16)
    d_out_gate = d_updated * out_proj * gate_sig * (1.0 - gate_sig)
    grad_out = weight_grad(tri_norm, d_out)
    d_tri_norm = transposed(d_out, low_out)
    d_triangle = standard_back(d_tri_norm * norm_params[2], normed_two, rstd_two).astype(
        jnp.bfloat16
    )
    d_rows = lax.all_gather(d_triangle, "col", axis=1, tiled=True)
    d_left = jnp.einsum("ijc,jkc->ikc", d_rows, strips, preferred_element_type=jnp.float32)
    piece = d_rows
    d_right = lax.psum_scatter(
        jnp.einsum("ijc,ikc->jkc", piece, left_vals, preferred_element_type=jnp.float32).astype(
            jnp.bfloat16
        ),
        "row",
        scatter_dimension=0,
        tiled=True,
    ).astype(jnp.float32)
    d_proj = jnp.concatenate(
        [
            d_left * mask_cube * left_sig,
            d_left * mask_cube * left_proj * left_sig * (1.0 - left_sig),
            d_right * mask_cube * right_sig,
            d_right * mask_cube * right_proj * right_sig * (1.0 - right_sig),
            d_out_gate,
        ],
        -1,
    ).astype(jnp.bfloat16)
    grad_in = weight_grad(pair_norm, d_proj)
    d_pair_norm = transposed(d_proj, low_in)
    grad_norms = jnp.stack(
        [
            jnp.sum(d_pair_norm * normed_one, (0, 1)),
            jnp.sum(d_pair_norm, (0, 1)),
            jnp.sum(d_tri_norm * normed_two, (0, 1)),
            jnp.sum(d_tri_norm, (0, 1)),
            jnp.sum(d_trans_in * normed_three, (0, 1)),
            jnp.sum(d_trans_in, (0, 1)),
        ]
    )
    summed = lax.psum(
        (grad_in, grad_out, grad_t1, grad_t2, grad_dist, grad_norms, grad_bias, loss_local),
        ("crop", "row", "col"),
    )
    grads = summed[:7]
    squares = jnp.zeros((), jnp.float32)
    for grad in grads:
        squares = squares + jnp.sum(grad * grad)
    grad_norm = jnp.sqrt(squares)
    scale = CLIP_NORM / jnp.maximum(grad_norm, CLIP_NORM)
    params = (w_in, w_out, w_t1, w_t2, w_dist, norm_params, dist_bias)
    firsts = (m_in, m_out, m_t1, m_t2, m_dist, m_norm, m_bias)
    seconds = (v_in, v_out, v_t1, v_t2, v_dist, v_norm, v_bias)
    rates = (LEARN_RATE, LEARN_RATE, LEARN_RATE, LEARN_RATE, LEARN_RATE, GAIN_RATE, GAIN_RATE)
    results = [
        adamw_update(
            params[index], firsts[index], seconds[index], grads[index], scale, rates[index]
        )
        for index in range(7)
    ]
    return (
        results[0][0],
        results[1][0],
        results[2][0],
        results[3][0],
        results[4][0],
        results[5][0],
        results[6][0],
        results[0][1],
        results[1][1],
        results[2][1],
        results[3][1],
        results[4][1],
        results[5][1],
        results[6][1],
        results[0][2],
        results[1][2],
        results[2][2],
        results[3][2],
        results[4][2],
        results[5][2],
        results[6][2],
        summed[7],
        pair_total,
        grad_norm,
    )


F32 = jnp.float32
BF16 = jnp.bfloat16
NT = (((1,), (1,)), ((), ()))
NN = (((1,), (0,)), ((), ()))
TN = (((0,), (0,)), ((), ()))
MICRO = 1e3
VMEM_LIMIT = 56 * 1024 * 1024


def dot(left, right, dims=NN):
    return lax.dot_general(left, right, dims, preferred_element_type=F32)


def sigmoid(values):
    return 0.5 * jnp.tanh(0.5 * values) + 0.5


def column_stats(values):
    center = values - jnp.mean(values, 0, keepdims=True)
    rstd = lax.rsqrt(jnp.mean(center * center, 0, keepdims=True) + NORM_EPS)
    return center * rstd, rstd


def column_back(grad, normed, rstd):
    return rstd * (
        grad
        - jnp.mean(grad, 0, keepdims=True)
        - normed * jnp.mean(grad * normed, 0, keepdims=True)
    )


def widen(param, lanes):
    return jnp.concatenate([param] * (lanes // param.shape[1]), 1)


def spread_rows(scratch, block):
    scratch[...] = jnp.swapaxes(block, 0, 1).astype(scratch.dtype)


def take_rows(scratch, start, count):
    return jnp.concatenate([scratch[start + u] for u in range(count)], 1).astype(F32)


def put_rows(scratch, start, count, values):
    lanes = values.shape[1] // count
    for u in range(count):
        scratch[start + u] = values[:, u * lanes : (u + 1) * lanes].astype(scratch.dtype)


def gather_rows(scratch, out_ref):
    out_ref[...] = jnp.swapaxes(scratch[...], 0, 1)


def call(kernel, grid, scalars, ins, outs, scratch, flops, name, aliases=None):
    return pl.pallas_call(
        kernel,
        grid_spec=pltpu.PrefetchScalarGridSpec(
            num_scalar_prefetch=len(scalars),
            grid=grid,
            in_specs=[pl.BlockSpec(block, index) for _, block, index in ins],
            out_specs=[pl.BlockSpec(block, index) for _, _, block, index in outs],
            scratch_shapes=scratch,
        ),
        out_shape=[jax.ShapeDtypeStruct(shape, dtype) for shape, dtype, _, _ in outs],
        compiler_params=pltpu.CompilerParams(vmem_limit_bytes=VMEM_LIMIT),
        cost_estimate=pl.CostEstimate(flops=int(flops), bytes_accessed=1, transcendentals=0),
        name=name,
        input_output_aliases=aliases or {},
    )(*scalars, *[a for a, _, _ in ins])


def code_rows(code_s, start, count):
    return jnp.concatenate([code_s[pl.ds(start + u, 1), :] for u in range(count)], 1)


def present_rows(code_s, start, count):
    return jnp.where(code_rows(code_s, start, count) < 0.0, 0.0, 1.0)


ROWS = 16
PROJECT_GROUP = 8
INPUT_GROUP = 8


def project_kernel(acts_ref, code_ref, w_ref, ln_ref, a_ref, b_ref, acts_s, a_s, b_s, code_s):
    width = a_ref.shape[0]
    code_s[...] = code_ref[0].astype(F32)
    spread_rows(acts_s, acts_ref[...])

    def some(step, carry):
        start = step * PROJECT_GROUP
        values = take_rows(acts_s, start, PROJECT_GROUP)
        lanes = values.shape[1]
        normed, _ = column_stats(values)
        low = (normed * widen(ln_ref[0], lanes) + widen(ln_ref[1], lanes)).astype(BF16)
        proj = dot(w_ref[...], low)
        mask = present_rows(code_s, start, PROJECT_GROUP)
        left = proj[:width] * sigmoid(proj[width : 2 * width]) * mask
        right = proj[2 * width : 3 * width] * sigmoid(proj[3 * width :]) * mask
        put_rows(a_s, start, PROJECT_GROUP, left)
        put_rows(b_s, start, PROJECT_GROUP, right)
        return carry

    lax.fori_loop(0, ROWS // PROJECT_GROUP, some, 0)
    gather_rows(a_s, a_ref)
    gather_rows(b_s, b_ref)


def fixed(*zeros):
    return lambda i, *_: zeros


def project(acts, w_proj, ln_wide):
    chans, rows, lanes = acts.shape[0] - 1, acts.shape[1], acts.shape[2]
    block = (chans, ROWS, lanes)
    mid = lambda i, *_: (0, i, 0)
    out = ((chans, rows, lanes), BF16, block, mid)
    staged = pltpu.VMEM((ROWS, chans, lanes), BF16)
    return call(
        project_kernel,
        (rows // ROWS,),
        [],
        [
            (acts, block, mid),
            (acts, (1, ROWS, lanes), lambda i, *_: (chans, i, 0)),
            (w_proj, w_proj.shape, fixed(0, 0)),
            (ln_wide, ln_wide.shape, fixed(0, 0, 0)),
        ],
        [out, out],
        [staged, staged, staged, pltpu.VMEM((ROWS, lanes), F32)],
        15 * MICRO,
        "project",
    )


CHANS = 16


def ordered(flag, own, other):
    part = own.shape[0] // 2
    waves = []
    for wave in range(2):
        mine, rest = own[wave * part : (wave + 1) * part], other[wave * part : (wave + 1) * part]
        waves += [jnp.where(flag, mine, rest), jnp.where(flag, rest, mine)]
    return jnp.concatenate(waves, 0)


def triangle_kernel(flag, a0, a1, b0, b1, keep_ref, send_ref):
    kept_first = flag[0] == 0
    part = b0.shape[1] // 2
    for chan in range(CHANS):
        rows = jnp.concatenate([a0[chan], a1[chan]], 0)
        one, two = [
            dot(jnp.concatenate([b[chan, part * u : part * u + part] for b in (b0, b1)], 0), rows, NT)
            for u in range(2)
        ]
        keep_ref[chan] = jnp.where(kept_first, one, two)
        send_ref[chan] = jnp.where(kept_first, two, one).astype(BF16)


def triangle(which, a, b):
    chans, half, lanes = a[0].shape
    lead = lambda i, *_: (i, 0, 0)
    block = (CHANS, half, lanes)
    out = (chans, half, 2 * half)
    return call(
        triangle_kernel,
        (chans // CHANS,),
        [which],
        [(v, block, lead) for v in (*a, *b)],
        [(out, F32, (CHANS, half, 2 * half), lead), (out, BF16, (CHANS, half, 2 * half), lead)],
        [],
        14 * MICRO,
        "triangle",
    )


GROUP = 16


T1_ROW, T2_ROW, OUT_ROW, OG_ROW, DIST_ROW, NORM_ROW, BIAS_ROW, LOSS_ROW, SUM_ROWS = (
    0, 512, 1024, 1152, 1280, 1344, 1350, 1351, 1352,
)


def row_sums(values):
    return jnp.sum(jnp.transpose(values), 0, keepdims=True)


def pair_kernel(
    first_call, last_call,
    place, x_keep, x_recv, acts_ref, code_ref, ln_ref, w_outT, w_out, w_ogT, w_t1T, w_t1,
    w_t2T, w_t2, w_distT, w_dist, bias_ref, *rest,
):
    prior = () if first_call else rest[:2]
    dx_ref, sums, wide, x_s, acts_s, dx_s, code_s = rest[len(prior) :]
    chans = acts_ref.shape[0]
    lanes = 128 * GROUP
    bins = w_distT.shape[0]
    hidden_width = w_t1T.shape[0]

    @pl.when(pl.program_id(0) == 0)
    def _():
        if first_call:
            sums[...] = jnp.zeros_like(sums)
            wide[...] = jnp.zeros_like(wide)
        else:
            sums[...] = prior[0][...]
            wide[...] = prior[1][...]

    spread_rows(x_s, x_keep[...] + x_recv[...].astype(F32))
    spread_rows(acts_s, acts_ref[...])
    code_s[...] = code_ref[0].astype(F32)
    param = [widen(ln_ref[index], lanes) for index in range(6)]
    bin_index = lax.broadcasted_iota(jnp.int32, (bins, lanes), 0).astype(F32)

    def fold(values):
        return sum(values[:, 128 * part : 128 * part + 128] for part in range(GROUP))

    def add(row, values):
        sums[row : row + values.shape[0]] += values

    def group(step, carry):
        first = step * GROUP
        x = take_rows(x_s, first, GROUP)
        acts = take_rows(acts_s, first, GROUP)
        code = code_rows(code_s, first, GROUP)
        normed_two, rstd_two = column_stats(x)
        tri = (normed_two * param[2] + param[3]).astype(BF16)
        out = dot(w_outT[...], tri)
        normed_one, _ = column_stats(acts)
        low = (normed_one * param[0] + param[1]).astype(BF16)
        gate = sigmoid(dot(w_ogT[...], low))
        z1 = acts + gate * out
        normed_three, rstd_three = column_stats(z1)
        trans = (normed_three * param[4] + param[5]).astype(BF16)
        pre = dot(w_t1T[...], trans)
        sig = sigmoid(pre)
        act = pre * sig
        hidden = act.astype(BF16)
        slope = sig * (1.0 + (pre - act))
        final = (z1 + dot(w_t2T[...], hidden)).astype(BF16)
        logits = dot(w_distT[...], final) + widen(bias_ref[...], lanes)
        top = jnp.max(logits, 0, keepdims=True)
        powers = jnp.exp(logits - top)
        total = jnp.sum(powers, 0, keepdims=True)
        present = jnp.where(code < 0.0, 0.0, 1.0)
        hot = bin_index == code
        picked = jnp.sum(jnp.where(hot, logits, 0.0), 0, keepdims=True)
        sums[LOSS_ROW : LOSS_ROW + 1] += fold(present * (jnp.log(total) + top) - picked)
        d_logits = (powers * (present / total) - jnp.where(hot, 1.0, 0.0)).astype(BF16)
        add(DIST_ROW, dot(d_logits, final, NT))
        wide[5, :bins] += fold(d_logits.astype(F32))
        d_final = dot(w_dist[...], d_logits)
        d_trans = d_final.astype(BF16)
        add(T2_ROW, dot(hidden, d_trans, NT))
        d_pre = (dot(w_t2[...], d_trans) * slope).astype(BF16)
        add(T1_ROW, dot(d_pre, trans, NT))
        d_tn = dot(w_t1[...], d_pre)
        wide[2] += fold(d_tn * normed_three)
        wide[3] += fold(d_tn)
        d_z1 = d_final + column_back(d_tn * param[4], normed_three, rstd_three)
        d_gated = d_z1 * gate
        d_out = d_gated.astype(BF16)
        d_og = (d_gated * out * (1.0 - gate)).astype(BF16)
        add(OUT_ROW, dot(d_out, tri, NT))
        g_og = dot(d_og, jnp.concatenate([low, normed_one.astype(BF16)], 0), NT)
        add(OG_ROW, g_og[:, :chans])
        wide[6] += g_og[:, chans:]
        wide[4] += fold(d_og.astype(F32))
        d_xn = dot(w_out[...], d_out)
        wide[0] += fold(d_xn * normed_two)
        wide[1] += fold(d_xn)
        d_x = column_back(d_xn * param[2], normed_two, rstd_two)
        put_rows(dx_s, first, GROUP, d_x)
        return carry

    lax.fori_loop(0, ROWS // GROUP, group, 0)
    gather_rows(dx_s, dx_ref)

    if last_call:

        @pl.when(pl.program_id(0) == pl.num_programs(0) - 1)
        def _():
            gate_w = w_ogT[...].astype(F32)
            for index in range(4):
                add(NORM_ROW + index, row_sums(wide[index]))
            add(NORM_ROW + 4, jnp.sum(gate_w * wide[6], 0, keepdims=True))
            add(NORM_ROW + 5, jnp.sum(gate_w * jnp.sum(wide[4], 1, keepdims=True), 0, keepdims=True))
            add(BIAS_ROW, row_sums(wide[5]))


def pair_block(place, x_keep, x_recv, acts_kj, ln_wide, weights, bias, prior, last_call):
    chans, rows, lanes = x_keep.shape
    block = (chans, ROWS, lanes)
    mid = lambda i, *_: (0, i, 0)

    def where(i, spot):
        return 8 * ((i % 2) ^ spot[0]) + 2 * spot[1] + i // 2

    full = [(w, w.shape, fixed(*([0] * w.ndim))) for w in (ln_wide, *weights, bias, *prior)]
    shapes = [(SUM_ROWS, 128), (7, 128, 128)]
    return call(
        functools.partial(pair_kernel, not prior, last_call),
        (rows // ROWS,),
        [place],
        [
            (x_keep, block, mid),
            (x_recv, block, mid),
            (acts_kj, block, lambda i, spot: (0, where(i, spot), 0)),
            (acts_kj, (1, ROWS, lanes), lambda i, spot: (chans, where(i, spot), 0)),
        ]
        + full,
        [((chans, rows, lanes), BF16, block, mid)]
        + [(s, F32, s, fixed(*([0] * len(s)))) for s in shapes],
        [pltpu.VMEM((ROWS, chans, lanes), t) for t in (F32, BF16, BF16)] + [pltpu.VMEM((ROWS, lanes), F32)],
        35 * MICRO,
        "pair",
    )


def right_back_kernel(flag, dx_own, dx_other, a0, a1, out0, out1):
    own_first = flag[0] == 0
    for chan in range(CHANS):
        rows = jnp.concatenate([a0[chan], a1[chan]], 0)
        both = ordered(own_first, dx_own[chan], dx_other[chan])
        grads = dot(both, rows).astype(BF16)
        half = out0.shape[1]
        out0[chan] = grads[:half]
        out1[chan] = grads[half:]


def right_back(which, dx_own, dx_other, a):
    chans, half, lanes = a[0].shape
    lead = lambda i, *_: (i, 0, 0)
    out = ((chans, half, lanes), BF16, (CHANS, half, lanes), lead)
    return call(
        right_back_kernel,
        (chans // CHANS,),
        [which],
        [(v, (CHANS, half, 2 * half), lead) for v in (dx_own, dx_other)]
        + [(v, (CHANS, half, lanes), lead) for v in a],
        [out, out],
        [],
        12 * MICRO,
        "right_back",
    )


def left_back_kernel(flag, *refs):
    owns, others, firsts, seconds = refs[:4], refs[4:8], refs[8:12], refs[12:16]
    out0, out1 = refs[16:]
    half = out0.shape[1]
    for chan in range(CHANS):
        total = None
        for pair in range(2):
            own_first = flag[0] == pair
            grads, values = [], []
            for q in (2 * pair, 2 * pair + 1):
                grads.append(ordered(own_first, owns[q][chan], others[q][chan]))
                values += [firsts[q][chan], seconds[q][chan]]
            term = dot(jnp.concatenate(grads, 0), jnp.concatenate(values, 0), TN)
            total = term if total is None else total + term
        total = total.astype(BF16)
        out0[chan] = total[:half]
        out1[chan] = total[half:]


def left_back(which, owns, others, firsts, seconds):
    chans, half, lanes = firsts[0].shape
    lead = lambda i, *_: (i, 0, 0)
    out = ((chans, half, lanes), BF16, (CHANS, half, lanes), lead)
    return call(
        left_back_kernel,
        (chans // CHANS,),
        [which],
        [(v, (CHANS, half, 2 * half), lead) for v in (*owns, *others)]
        + [(v, (CHANS, half, lanes), lead) for v in (*firsts, *seconds)],
        [out, out],
        [],
        25 * MICRO,
        "left_back",
    )


SIDE_ROWS = 272


def input_back_kernel(count, first_call, last_call, acts_ref, code_ref, w_ref, ln_ref, *rest):
    grads, rest = rest[:count], rest[count:]
    prior = () if first_call else rest[:3]
    out_ref, g_ref, sum_ref, acts_s, grad_s, code_s = rest[len(prior) :]
    width = grads[0].shape[0]
    chans = acts_ref.shape[0]

    @pl.when(pl.program_id(0) == 0)
    def _():
        if first_call:
            out_ref[...] = jnp.zeros_like(out_ref)
            g_ref[...] = jnp.zeros_like(g_ref)
            sum_ref[...] = jnp.zeros_like(sum_ref)
        else:
            out_ref[...] = prior[0][...]
            g_ref[...] = prior[1][...]
            sum_ref[...] = prior[2][...]

    code_s[...] = code_ref[0].astype(F32)
    spread_rows(acts_s, acts_ref[...])
    total = grads[0][...].astype(F32)
    for ref in grads[1:]:
        total = total + ref[...].astype(F32)
    spread_rows(grad_s, total)

    def some(step, carry):
        start = step * INPUT_GROUP
        values = take_rows(acts_s, start, INPUT_GROUP)
        lanes = values.shape[1]
        normed, _ = column_stats(values)
        low = (normed * widen(ln_ref[0], lanes) + widen(ln_ref[1], lanes)).astype(BF16)
        proj = dot(w_ref[...], low)
        gate = sigmoid(proj[width:])
        mask = present_rows(code_s, start, INPUT_GROUP)
        d_value = take_rows(grad_s, start, INPUT_GROUP) * mask * gate
        d_gate = d_value * proj[:width] * (1.0 - gate)
        d_proj = jnp.concatenate([d_value.astype(BF16), d_gate.astype(BF16)], 0)
        g_all = dot(d_proj, jnp.concatenate([low, normed.astype(BF16)], 0), NT)
        out_ref[: 2 * width] += g_all[:, :chans]
        g_ref[...] += g_all[:, chans:]
        wide = d_proj.astype(F32)
        sum_ref[...] += sum(wide[:, 128 * u : 128 * u + 128] for u in range(lanes // 128))
        return carry

    lax.fori_loop(0, ROWS // INPUT_GROUP, some, 0)

    if last_call:

        @pl.when(pl.program_id(0) == pl.num_programs(0) - 1)
        def _():
            part = w_ref[...].astype(F32)
            gain = jnp.sum(part * g_ref[...], 0, keepdims=True)
            shift = jnp.sum(part * jnp.sum(sum_ref[...], 1, keepdims=True), 0, keepdims=True)
            out_ref[2 * width : 2 * width + 1] = gain
            out_ref[2 * width + 1 : 2 * width + 2] = shift


def input_back(acts, w_part, ln_wide, grads, prior, last_call):
    chans, rows, lanes = acts.shape[0] - 1, acts.shape[1], acts.shape[2]
    block = (chans, ROWS, lanes)
    mid = lambda i, *_: (0, i, 0)
    depth = w_part.shape[0]
    shapes = [(SIDE_ROWS, chans), (depth, chans), (depth, 128)]
    return call(
        functools.partial(input_back_kernel, len(grads), not prior, last_call),
        (rows // ROWS,),
        [],
        [
            (acts, block, mid),
            (acts, (1, ROWS, lanes), lambda i, *_: (chans, i, 0)),
            (w_part, w_part.shape, fixed(0, 0)),
            (ln_wide, ln_wide.shape, fixed(0, 0, 0)),
        ]
        + [(v, block, mid) for v in grads]
        + [(v, v.shape, fixed(0, 0)) for v in prior],
        [(s, F32, s, fixed(0, 0)) for s in shapes],
        [
            pltpu.VMEM((ROWS, chans, lanes), BF16),
            pltpu.VMEM((ROWS, chans, lanes), F32),
            pltpu.VMEM((ROWS, lanes), F32),
        ],
        16 * MICRO,
        "input_back",
    )


def reduce_kernel(part_ref, out_ref, half_s, crop_s, row_s, full_s, send, recv):
    side, spot, level = lax.axis_index("col"), lax.axis_index("crop"), lax.axis_index("row")
    sibling = {"col": 1 - side}
    others = [{"crop": lax.rem(spot + n, 4)} for n in range(1, 4)]
    others += [{"row": lax.rem(level + n, 4)} for n in range(1, 4)]
    barrier = pltpu.get_barrier_semaphore()
    for device in [sibling] + others:
        pl.semaphore_signal(barrier, inc=1, device_id=device, device_id_type=pl.DeviceIdType.MESH)
    pl.semaphore_wait(barrier, 7)

    def copy(source, target, index, device):
        return pltpu.make_async_remote_copy(
            src_ref=source, dst_ref=target, send_sem=send.at[index], recv_sem=recv.at[index],
            device_id=device, device_id_type=pl.DeviceIdType.MESH,
        )

    rows = half_s.shape[0]
    away = pl.multiple_of((1 - side) * rows, 8)
    here = pl.multiple_of(side * rows, 8)
    one = copy(part_ref.at[pl.ds(away, rows)], half_s, 0, sibling)
    one.start()
    one.wait()
    crop_s[spot] = part_ref[pl.ds(here, rows)] + half_s[...]
    sends = [copy(crop_s.at[spot], crop_s.at[spot], 1 + n, others[n]) for n in range(3)]
    for one in sends:
        one.start()
    for one in sends:
        one.wait()
    row_s[level] = crop_s[0] + crop_s[1] + crop_s[2] + crop_s[3]
    sends = [copy(row_s.at[level], row_s.at[level], 4 + n, others[3 + n]) for n in range(3)]
    for one in sends:
        one.start()
    for one in sends:
        one.wait()
    full_s[side] = row_s[0] + row_s[1] + row_s[2] + row_s[3]
    one = copy(full_s.at[side], full_s.at[side], 7, sibling)
    one.start()
    one.wait()
    out_ref[:rows] = full_s[0]
    out_ref[rows:] = full_s[1]


def reduce_all(part):
    rows, lanes = part.shape[0] // 2, part.shape[1]
    return pl.pallas_call(
        reduce_kernel,
        out_shape=jax.ShapeDtypeStruct(part.shape, F32),
        scratch_shapes=[
            pltpu.VMEM((rows, lanes), F32),
            pltpu.VMEM((4, rows, lanes), F32),
            pltpu.VMEM((4, rows, lanes), F32),
            pltpu.VMEM((2, rows, lanes), F32),
            pltpu.SemaphoreType.DMA((8,)),
            pltpu.SemaphoreType.DMA((8,)),
        ],
        compiler_params=pltpu.CompilerParams(collective_id=1, has_side_effects=True),
        name="reduce_all",
    )(part)


def flip(a, b):
    return 2 * lax.rem(a // 2 + b // 2, 2) + lax.rem(a + b, 2)


def swap_bits(a):
    return 2 * lax.rem(a, 2) + a // 2


def spread_kernel(acts_ref, wave0_ref, mid1_ref, mid0, plane_send, plane_recv, level_send, level_recv, local):
    side, spot, level = lax.axis_index("col"), lax.axis_index("crop"), lax.axis_index("row")
    chans = acts_ref.shape[0]
    cuts = [(0, chans // 2), (chans // 2, chans - chans // 2)]
    barrier = pltpu.get_barrier_semaphore()
    for n in range(1, 4):
        for device in ({"crop": lax.rem(spot + n, 4)}, {"row": lax.rem(level + n, 4)}):
            pl.semaphore_signal(barrier, inc=1, device_id=device, device_id_type=pl.DeviceIdType.MESH)
    pl.semaphore_wait(barrier, 6)

    def plane_copy(wave, cut, distance):
        first, count = cuts[cut] if wave == 0 else (0, chans)
        target = flip(spot, distance)
        rows = pl.ds(pl.multiple_of(32 * target + 16 * wave, 16), 16)
        source = acts_ref.at[pl.ds(first, count), rows]
        landing = (mid0 if wave == 0 else mid1_ref).at[distance, pl.ds(first, count)]
        index = 4 * cut + distance if wave == 0 else 8 + distance
        if distance == 0:
            return pltpu.make_async_copy(source, landing, plane_recv.at[index])
        return pltpu.make_async_remote_copy(
            src_ref=source, dst_ref=landing, send_sem=plane_send.at[index], recv_sem=plane_recv.at[index],
            device_id={"crop": target}, device_id_type=pl.DeviceIdType.MESH,
        )

    def level_copy(cut, label, distance):
        first, count = cuts[cut]
        source = mid0.at[distance, pl.ds(first, count)]
        landing = wave0_ref.at[pl.ds(first, count), pl.ds(16 * label, 16)]
        target = swap_bits(flip(spot, distance))
        index = 4 * cut + label
        remote = pltpu.make_async_remote_copy(
            src_ref=source, dst_ref=landing, send_sem=level_send.at[index], recv_sem=level_recv.at[index],
            device_id={"row": target}, device_id_type=pl.DeviceIdType.MESH,
        )
        return target, remote, pltpu.make_async_copy(source, landing, local.at[cut])

    def each_level(action):
        for cut in range(2):
            for label in range(4):
                for distance in range(4):

                    @pl.when(flip(level, label) == distance)
                    def _(cut=cut, label=label, distance=distance):
                        action(cut, label, distance)

    plane = [plane_copy(0, cut, distance) for cut in range(2) for distance in range(4)]
    plane += [plane_copy(1, 0, distance) for distance in range(4)]
    for one in plane:
        one.start()

    def begin(cut, label, distance):
        one = plane[4 * cut + distance]
        one.wait() if distance == 0 else one.wait_recv()
        target, remote, stay = level_copy(cut, label, distance)

        @pl.when(target == level)
        def _():
            stay.start()

        @pl.when(target != level)
        def _():
            remote.start()

    def finish(cut, label, distance):
        target, remote, stay = level_copy(cut, label, distance)

        @pl.when(target == level)
        def _():
            stay.wait()

        @pl.when(target != level)
        def _():
            remote.wait()

    each_level(begin)
    for index, one in enumerate(plane):
        if index % 4 == 0:
            if index == 8:
                one.wait()
        else:
            one.wait_send()
            if index > 8:
                one.wait_recv()
    each_level(finish)


def spread(acts_major):
    chans, rows, lanes = acts_major.shape
    anywhere = pl.BlockSpec(memory_space=pl.ANY)
    return pl.pallas_call(
        spread_kernel,
        in_specs=[anywhere],
        out_specs=[anywhere, anywhere],
        out_shape=[
            jax.ShapeDtypeStruct((chans, rows // 2, lanes), BF16),
            jax.ShapeDtypeStruct((4, chans, rows // 8, lanes), BF16),
        ],
        scratch_shapes=[
            pltpu.VMEM((4, chans, rows // 8, lanes), BF16),
            pltpu.SemaphoreType.DMA((12,)),
            pltpu.SemaphoreType.DMA((12,)),
            pltpu.SemaphoreType.DMA((8,)),
            pltpu.SemaphoreType.DMA((8,)),
            pltpu.SemaphoreType.DMA((2,)),
        ],
        compiler_params=pltpu.CompilerParams(
            collective_id=2, has_side_effects=True, vmem_limit_bytes=VMEM_LIMIT
        ),
        name="spread",
    )(acts_major)


def update_kernel(early_ref, left_ref, right_ref, *refs):
    ins, outs = refs[:21], refs[21:]
    loss_ref, total_ref, norm_ref = outs[21:]
    total = early_ref[LOSS_ROW - 1, 127]
    inverse = 1.0 / total
    half = left_ref.shape[0] - 16
    grads = [
        jnp.concatenate(
            [
                jnp.transpose(left_ref[:half]),
                jnp.transpose(right_ref[:half]),
                jnp.transpose(early_ref[OG_ROW : OG_ROW + 128]),
            ],
            1,
        ),
        jnp.transpose(early_ref[OUT_ROW : OUT_ROW + 128]),
        jnp.transpose(early_ref[T1_ROW : T1_ROW + 512]),
        early_ref[T2_ROW : T2_ROW + 512],
        jnp.transpose(early_ref[DIST_ROW : DIST_ROW + 64]),
        jnp.concatenate(
            [
                left_ref[half : half + 2] + right_ref[half : half + 2] + early_ref[NORM_ROW + 4 : NORM_ROW + 6],
                early_ref[NORM_ROW : NORM_ROW + 4],
            ],
            0,
        ),
        early_ref[BIAS_ROW : BIAS_ROW + 1, :64],
    ]
    grads = [grad * inverse for grad in grads]
    squares = sum(jnp.sum(grad * grad, keepdims=True).reshape(1, 1) for grad in grads)
    grad_norm = jnp.sqrt(squares)
    scale = CLIP_NORM / jnp.maximum(grad_norm, CLIP_NORM)
    rates = (LEARN_RATE,) * 5 + (GAIN_RATE,) * 2
    for index in range(7):
        new = adamw_update(
            ins[index][...], ins[7 + index][...], ins[14 + index][...], grads[index], scale, rates[index]
        )
        for part in range(3):
            outs[7 * part + index][...] = new[part]
    norm_ref[...] = grad_norm
    loss_ref[...] = jnp.sum(early_ref[LOSS_ROW : LOSS_ROW + 1], keepdims=True).reshape(1, 1)
    total_ref[...] = jnp.full((1, 1), total, F32)


def update(early, left, right, params, firsts, seconds):
    flat = [v.reshape(1, -1) if v.ndim == 1 else v for v in (*params, *firsts, *seconds)]
    shapes = [v.shape for v in flat] + [(1, 1)] * 3
    outs = pl.pallas_call(
        update_kernel,
        out_shape=[jax.ShapeDtypeStruct(s, F32) for s in shapes],
        compiler_params=pltpu.CompilerParams(vmem_limit_bytes=VMEM_LIMIT),
        name="update",
    )(early, left, right, *flat)
    outs = [v.reshape(-1) if index in (6, 13, 20) else v for index, v in enumerate(outs)]
    return (*outs[:21], *[v[0, 0] for v in outs[21:]])


def after(value, *earlier):
    return lax.optimization_barrier((value, *earlier))[0]


def on_device_planes(
    pair_acts, residue_mask, dist_bins, w_in, w_out, w_t1, w_t2, w_dist, norm_params, dist_bias, *moments
):
    firsts, seconds = moments[:7], moments[7:]
    spot = lax.axis_index("crop")
    level = lax.axis_index("row")
    side = lax.axis_index("col")
    rows, cols, chans = pair_acts.shape[1:]
    width = w_out.shape[0]
    sub = rows // 4
    plane_of = (0, 2, 1, 3)
    crop = (level % 2) * 2 + level // 2

    def over_x(v):
        return lax.ppermute(v, "crop", [(g, g ^ 1) for g in range(4)])

    def over_y(v):
        return lax.ppermute(v, "crop", [(g, g ^ 2) for g in range(4)])

    def over_core(v):
        return lax.ppermute(v, "col", [(0, 1), (1, 0)])

    own_mask = residue_mask[0]
    row_own = lax.dynamic_slice_in_dim(own_mask, rows * level, rows)
    col_own = lax.dynamic_slice_in_dim(own_mask, cols * side, cols)
    code_own = jnp.where((row_own[:, None] * col_own[None, :]) > 0, dist_bins[0], -1).astype(BF16)
    acts_major = jnp.transpose(pair_acts[0], (2, 0, 1))

    acts_major = jnp.concatenate([acts_major, code_own[None]], 0)
    wave0, mid1 = spread(acts_major)

    def along_z(label):
        piece = lax.dynamic_index_in_dim(mid1, level ^ label, 0, keepdims=False)
        pairs = [(g * 4 + z, g * 4 + plane_of[g ^ label ^ z]) for g in range(4) for z in range(4)]
        stays = sum(((spot * 4 + level) == i).astype(jnp.int32) for i, j in pairs if i == j)
        moved = lax.ppermute(piece, ("crop", "row"), [(i, j) for i, j in pairs if i != j])
        return jnp.where(stays > 0, piece, moved)

    count = jnp.sum(own_mask).astype(F32)
    share = count * count / (lax.axis_size("row") * lax.axis_size("col"))
    low_in, low_out, low_t1, low_t2, low_dist = [
        weight.astype(BF16) for weight in (w_in, w_out, w_t1, w_t2, w_dist)
    ]
    ln_wide = jnp.broadcast_to(norm_params[:, :, None], (*norm_params.shape, 128))
    bias_wide = jnp.broadcast_to(dist_bias[:, None], (dist_bias.shape[0], 128))
    in_T = low_in.T

    pieces = [along_z(label) for label in range(4)]
    acts, a, b_own = [], [], []
    for h in range(2):
        acts.append(wave0 if h == 0 else jnp.concatenate([after(v, a[0]) for v in pieces], 1))
        left, right = project(acts[h], in_T[: 4 * width], ln_wide)
        a.append(left)
        b_own.append(right)
    b_x = [over_x(v) for v in b_own]
    b_y = [over_y(v) for v in b_own]
    b_d = [over_y(b_x[0]), over_x(b_y[1])]
    blocks = [b_own, b_x, b_y, b_d]

    weights = (
        low_out.T, low_out, in_T[4 * width :], low_t1.T, low_t1, low_t2.T, low_t2, low_dist.T, low_dist,
    )
    flags = [(side ^ ((spot ^ q) // 2) ^ (crop // 2)).astype(jnp.int32)[None] for q in range(4)]
    keeps, recvs, dx_own, dx_other, back = {}, {}, {}, {}, {}
    sums = []

    def forward(q, *earlier):
        keeps[q], send = triangle(flags[q], [after(v, *earlier) for v in a], blocks[q])
        recvs[q] = over_core(send)
        return send

    def middle(q, *earlier):
        owner = spot ^ q
        place = jnp.stack([(owner ^ crop) & 1, owner]).astype(jnp.int32)
        dx_own[q], *sums[:] = pair_block(
            after(place, *earlier), keeps[q], recvs[q], acts_kj, ln_wide, weights, bias_wide, list(sums), q == 3
        )
        dx_other[q] = over_core(dx_own[q])
        return dx_own[q]

    def backward(q, *earlier):
        back[q] = right_back(after(flags[q], *earlier), dx_own[q], dx_other[q], a)
        return back[q][0]

    done = forward(0, b_own[1], b_x[0], b_y[0])
    acts_kj = jnp.swapaxes(jnp.concatenate([after(v, done) for v in acts], 1), 1, 2)
    done = middle(0, acts_kj)
    done = forward(1, done)
    done = forward(2, done)
    done = middle(1, done)
    done = middle(2, done)
    done = backward(1, done)
    done = backward(2, done)
    done = forward(3, done)
    y0, x1 = over_y(back[2][0]), over_x(back[1][1])
    done = middle(3, done)
    done = backward(3, done, y0, x1)
    d0, d1 = over_y(back[3][0]), over_x(back[3][1])
    done = backward(0, done)
    d_left = left_back(
        after(flags[0], done),
        [dx_own[q] for q in range(4)],
        [dx_other[q] for q in range(4)],
        [v[0] for v in blocks],
        [v[1] for v in blocks],
    )
    x0 = (back[1][0].astype(F32) + d0.astype(F32)).astype(BF16)
    y1 = (back[2][1].astype(F32) + d1.astype(F32)).astype(BF16)
    own = [[back[0][0], y0, over_x(x0)], [back[0][1], x1, over_y(y1)]]
    left_w, right_w = in_T[: 2 * width], in_T[2 * width : 4 * width]
    left, right = [], []
    for h in range(2):
        left = input_back(acts[h], left_w, ln_wide, [d_left[h]], left, h == 1)
    everywhere = ("crop", "row", "col")
    early = sums[0].at[LOSS_ROW - 1, 127].set(share)
    early = lax.psum(early, everywhere)
    own[0][0] = after(own[0][0], left[0])
    for h in range(2):
        right = input_back(acts[h], right_w, ln_wide, own[h], right, h == 1)
    both = reduce_all(jnp.concatenate([left[0], after(right[0], early)], 0))
    params = (w_in, w_out, w_t1, w_t2, w_dist, norm_params, dist_bias)
    return update(early, both[:SIDE_ROWS], both[SIDE_ROWS:], params, firsts, seconds)


def solution(mesh):
    planes = mesh.shape["crop"] == 4 and mesh.shape["row"] == 4 and mesh.shape["col"] == 2
    body = on_device_planes if planes else on_device_general
    in_specs = (
        P("crop", "row", "col", None),
        P("crop", None),
        P("crop", "row", "col"),
    ) + (P(),) * 21
    return jax.shard_map(
        body, mesh=mesh, in_specs=in_specs, out_specs=(P(),) * 24, check_vma=False
    )
```

```python
import functools

import jax
import jax.numpy as jnp
from jax import lax
from jax.experimental import pallas as pl
from jax.experimental.pallas import tpu as pltpu
from jax.sharding import PartitionSpec as P

STEP = 10


NORM_EPS = 1e-05
CLIP_NORM = 0.02
LEARN_RATE = 0.03
GAIN_RATE = 0.3
BETA_ONE = 0.9
BETA_TWO = 0.999
ADAM_EPS = 1e-08
WEIGHT_DECAY = 0.01


def standardize(values):
    center = values - jnp.mean(values, -1, keepdims=True)
    rstd = lax.rsqrt(jnp.mean(center * center, -1, keepdims=True) + NORM_EPS)
    return (center * rstd, rstd)


def standard_back(grad, normed, rstd):
    return rstd * (
        grad
        - jnp.mean(grad, -1, keepdims=True)
        - normed * jnp.mean(grad * normed, -1, keepdims=True)
    )


def linear(values, weight):
    return jnp.einsum("ijc,cd->ijd", values, weight, preferred_element_type=jnp.float32)


def weight_grad(values, grad):
    return jnp.einsum("ijc,ijd->cd", values, grad, preferred_element_type=jnp.float32)


def transposed(grad, weight):
    return jnp.einsum("ijd,cd->ijc", grad, weight, preferred_element_type=jnp.float32)


def adamw_update(weight, first, second, grad, scale, rate):
    clipped = grad * scale
    first_new = BETA_ONE * first + (1.0 - BETA_ONE) * clipped
    second_new = BETA_TWO * second + (1.0 - BETA_TWO) * clipped * clipped
    first_hat = first_new / (1.0 - BETA_ONE**STEP)
    second_hat = second_new / (1.0 - BETA_TWO**STEP)
    stepped = weight - rate * (
        first_hat / (jnp.sqrt(second_hat) + ADAM_EPS) + WEIGHT_DECAY * weight
    )
    return (stepped, first_new, second_new)


def on_device_general(
    pair_acts,
    residue_mask,
    dist_bins,
    w_in,
    w_out,
    w_t1,
    w_t2,
    w_dist,
    norm_params,
    dist_bias,
    m_in,
    m_out,
    m_t1,
    m_t2,
    m_dist,
    m_norm,
    m_bias,
    v_in,
    v_out,
    v_t1,
    v_t2,
    v_dist,
    v_norm,
    v_bias,
):
    tile_rows = pair_acts.shape[1]
    tile_cols = pair_acts.shape[2]
    width = w_out.shape[0]
    row_first = lax.axis_index("row") * tile_rows
    col_first = lax.axis_index("col") * tile_cols
    mask_vals = residue_mask[0].astype(jnp.float32)
    row_mask = lax.dynamic_slice_in_dim(mask_vals, row_first, tile_rows)
    col_mask = lax.dynamic_slice_in_dim(mask_vals, col_first, tile_cols)
    pair_mask = row_mask[:, None] * col_mask[None, :]
    mask_cube = pair_mask[..., None]
    pair_total = lax.psum(jnp.sum(pair_mask), ("crop", "row", "col"))
    low_in, low_out, low_t1, low_t2, low_dist = [
        weight.astype(jnp.bfloat16) for weight in (w_in, w_out, w_t1, w_t2, w_dist)
    ]
    acts = pair_acts[0].astype(jnp.float32)
    normed_one, rstd_one = standardize(acts)
    pair_norm = (normed_one * norm_params[0] + norm_params[1]).astype(jnp.bfloat16)
    projected = linear(pair_norm, low_in)
    left_proj = projected[..., :width]
    left_sig = jax.nn.sigmoid(projected[..., width : 2 * width])
    right_proj = projected[..., 2 * width : 3 * width]
    right_sig = jax.nn.sigmoid(projected[..., 3 * width : 4 * width])
    gate_sig = jax.nn.sigmoid(projected[..., 4 * width :])
    left_vals = (mask_cube * left_sig * left_proj).astype(jnp.bfloat16)
    right_vals = (mask_cube * right_sig * right_proj).astype(jnp.bfloat16)
    strips = lax.all_gather(right_vals, "row", axis=0, tiled=True)
    piece = strips
    triangle = jnp.transpose(
        lax.psum_scatter(
            jnp.einsum("jkc,ikc->jic", piece, left_vals, preferred_element_type=jnp.float32),
            "col",
            scatter_dimension=0,
            tiled=True,
        ),
        (1, 0, 2),
    )
    normed_two, rstd_two = standardize(triangle)
    tri_norm = (normed_two * norm_params[2] + norm_params[3]).astype(jnp.bfloat16)
    out_proj = linear(tri_norm, low_out)
    updated = acts + gate_sig * out_proj
    normed_three, rstd_three = standardize(updated)
    trans_in = (normed_three * norm_params[4] + norm_params[5]).astype(jnp.bfloat16)
    pre_act = linear(trans_in, low_t1)
    hidden = jax.nn.silu(pre_act).astype(jnp.bfloat16)
    final = updated + linear(hidden, low_t2)
    final_low = final.astype(jnp.bfloat16)
    logits = linear(final_low, low_dist) + dist_bias
    log_total = jax.nn.logsumexp(logits, -1)
    onehot = (dist_bins[0][..., None] == jnp.arange(w_dist.shape[1])).astype(jnp.float32)
    loss_local = jnp.sum(pair_mask * (log_total - jnp.sum(logits * onehot, -1)))
    d_logits = (mask_cube * (jnp.exp(logits - log_total[..., None]) - onehot) / pair_total).astype(
        jnp.bfloat16
    )
    grad_dist = weight_grad(final_low, d_logits)
    grad_bias = jnp.sum(d_logits.astype(jnp.float32), (0, 1))
    d_final = transposed(d_logits, low_dist)
    d_trans = d_final.astype(jnp.bfloat16)
    grad_t2 = weight_grad(hidden, d_trans)
    d_hidden = transposed(d_trans, low_t2)
    sig_pre = jax.nn.sigmoid(pre_act)
    d_pre = (d_hidden * sig_pre * (1.0 + pre_act * (1.0 - sig_pre))).astype(jnp.bfloat16)
    grad_t1 = weight_grad(trans_in, d_pre)
    d_trans_in = transposed(d_pre, low_t1)
    d_updated = d_final + standard_back(d_trans_in * norm_params[4], normed_three, rstd_three)
    d_out = (d_updated * gate_sig).astype(jnp.bfloat16)
    d_out_gate = d_updated * out_proj * gate_sig * (1.0 - gate_sig)
    grad_out = weight_grad(tri_norm, d_out)
    d_tri_norm = transposed(d_out, low_out)
    d_triangle = standard_back(d_tri_norm * norm_params[2], normed_two, rstd_two).astype(
        jnp.bfloat16
    )
    d_rows = lax.all_gather(d_triangle, "col", axis=1, tiled=True)
    d_left = jnp.einsum("ijc,jkc->ikc", d_rows, strips, preferred_element_type=jnp.float32)
    piece = d_rows
    d_right = lax.psum_scatter(
        jnp.einsum("ijc,ikc->jkc", piece, left_vals, preferred_element_type=jnp.float32).astype(
            jnp.bfloat16
        ),
        "row",
        scatter_dimension=0,
        tiled=True,
    ).astype(jnp.float32)
    d_proj = jnp.concatenate(
        [
            d_left * mask_cube * left_sig,
            d_left * mask_cube * left_proj * left_sig * (1.0 - left_sig),
            d_right * mask_cube * right_sig,
            d_right * mask_cube * right_proj * right_sig * (1.0 - right_sig),
            d_out_gate,
        ],
        -1,
    ).astype(jnp.bfloat16)
    grad_in = weight_grad(pair_norm, d_proj)
    d_pair_norm = transposed(d_proj, low_in)
    grad_norms = jnp.stack(
        [
            jnp.sum(d_pair_norm * normed_one, (0, 1)),
            jnp.sum(d_pair_norm, (0, 1)),
            jnp.sum(d_tri_norm * normed_two, (0, 1)),
            jnp.sum(d_tri_norm, (0, 1)),
            jnp.sum(d_trans_in * normed_three, (0, 1)),
            jnp.sum(d_trans_in, (0, 1)),
        ]
    )
    summed = lax.psum(
        (grad_in, grad_out, grad_t1, grad_t2, grad_dist, grad_norms, grad_bias, loss_local),
        ("crop", "row", "col"),
    )
    grads = summed[:7]
    squares = jnp.zeros((), jnp.float32)
    for grad in grads:
        squares = squares + jnp.sum(grad * grad)
    grad_norm = jnp.sqrt(squares)
    scale = CLIP_NORM / jnp.maximum(grad_norm, CLIP_NORM)
    params = (w_in, w_out, w_t1, w_t2, w_dist, norm_params, dist_bias)
    firsts = (m_in, m_out, m_t1, m_t2, m_dist, m_norm, m_bias)
    seconds = (v_in, v_out, v_t1, v_t2, v_dist, v_norm, v_bias)
    rates = (LEARN_RATE, LEARN_RATE, LEARN_RATE, LEARN_RATE, LEARN_RATE, GAIN_RATE, GAIN_RATE)
    results = [
        adamw_update(
            params[index], firsts[index], seconds[index], grads[index], scale, rates[index]
        )
        for index in range(7)
    ]
    return (
        results[0][0],
        results[1][0],
        results[2][0],
        results[3][0],
        results[4][0],
        results[5][0],
        results[6][0],
        results[0][1],
        results[1][1],
        results[2][1],
        results[3][1],
        results[4][1],
        results[5][1],
        results[6][1],
        results[0][2],
        results[1][2],
        results[2][2],
        results[3][2],
        results[4][2],
        results[5][2],
        results[6][2],
        summed[7],
        pair_total,
        grad_norm,
    )


F32 = jnp.float32
BF16 = jnp.bfloat16
NT = (((1,), (1,)), ((), ()))
NN = (((1,), (0,)), ((), ()))
TN = (((0,), (0,)), ((), ()))
MICRO = 1e3
VMEM_LIMIT = 56 * 1024 * 1024


def dot(left, right, dims=NN):
    return lax.dot_general(left, right, dims, preferred_element_type=F32)


def sigmoid(values):
    return 0.5 * jnp.tanh(0.5 * values) + 0.5


def column_stats(values):
    center = values - jnp.mean(values, 0, keepdims=True)
    rstd = lax.rsqrt(jnp.mean(center * center, 0, keepdims=True) + NORM_EPS)
    return center * rstd, rstd


def column_back(grad, normed, rstd):
    return rstd * (
        grad
        - jnp.mean(grad, 0, keepdims=True)
        - normed * jnp.mean(grad * normed, 0, keepdims=True)
    )


def widen(param, lanes):
    return jnp.concatenate([param] * (lanes // param.shape[1]), 1)


def spread_rows(scratch, block):
    scratch[...] = jnp.swapaxes(block, 0, 1).astype(scratch.dtype)


def take_rows(scratch, start, count):
    return jnp.concatenate([scratch[start + u] for u in range(count)], 1).astype(F32)


def put_rows(scratch, start, count, values):
    lanes = values.shape[1] // count
    for u in range(count):
        scratch[start + u] = values[:, u * lanes : (u + 1) * lanes].astype(scratch.dtype)


def gather_rows(scratch, out_ref):
    out_ref[...] = jnp.swapaxes(scratch[...], 0, 1)


def call(kernel, grid, scalars, ins, outs, scratch, flops, name, aliases=None):
    return pl.pallas_call(
        kernel,
        grid_spec=pltpu.PrefetchScalarGridSpec(
            num_scalar_prefetch=len(scalars),
            grid=grid,
            in_specs=[pl.BlockSpec(block, index) for _, block, index in ins],
            out_specs=[pl.BlockSpec(block, index) for _, _, block, index in outs],
            scratch_shapes=scratch,
        ),
        out_shape=[jax.ShapeDtypeStruct(shape, dtype) for shape, dtype, _, _ in outs],
        compiler_params=pltpu.CompilerParams(vmem_limit_bytes=VMEM_LIMIT),
        cost_estimate=pl.CostEstimate(flops=int(flops), bytes_accessed=1, transcendentals=0),
        name=name,
        input_output_aliases=aliases or {},
    )(*scalars, *[a for a, _, _ in ins])


def code_rows(code_s, start, count):
    return jnp.concatenate([code_s[pl.ds(start + u, 1), :] for u in range(count)], 1)


def present_rows(code_s, start, count):
    return jnp.where(code_rows(code_s, start, count) < 0.0, 0.0, 1.0)


ROWS = 16
PROJECT_GROUP = 8
INPUT_GROUP = 8


def project_kernel(acts_ref, code_ref, w_ref, ln_ref, a_ref, b_ref, acts_s, a_s, b_s, code_s):
    width = a_ref.shape[0]
    code_s[...] = code_ref[0].astype(F32)
    spread_rows(acts_s, acts_ref[...])

    def some(step, carry):
        start = step * PROJECT_GROUP
        values = take_rows(acts_s, start, PROJECT_GROUP)
        lanes = values.shape[1]
        normed, _ = column_stats(values)
        low = (normed * widen(ln_ref[0], lanes) + widen(ln_ref[1], lanes)).astype(BF16)
        proj = dot(w_ref[...], low)
        mask = present_rows(code_s, start, PROJECT_GROUP)
        left = proj[:width] * sigmoid(proj[width : 2 * width]) * mask
        right = proj[2 * width : 3 * width] * sigmoid(proj[3 * width :]) * mask
        put_rows(a_s, start, PROJECT_GROUP, left)
        put_rows(b_s, start, PROJECT_GROUP, right)
        return carry

    lax.fori_loop(0, ROWS // PROJECT_GROUP, some, 0)
    gather_rows(a_s, a_ref)
    gather_rows(b_s, b_ref)


def fixed(*zeros):
    return lambda i, *_: zeros


def project(acts, w_proj, ln_wide):
    chans, rows, lanes = acts.shape[0] - 1, acts.shape[1], acts.shape[2]
    block = (chans, ROWS, lanes)
    mid = lambda i, *_: (0, i, 0)
    out = ((chans, rows, lanes), BF16, block, mid)
    staged = pltpu.VMEM((ROWS, chans, lanes), BF16)
    return call(
        project_kernel,
        (rows // ROWS,),
        [],
        [
            (acts, block, mid),
            (acts, (1, ROWS, lanes), lambda i, *_: (chans, i, 0)),
            (w_proj, w_proj.shape, fixed(0, 0)),
            (ln_wide, ln_wide.shape, fixed(0, 0, 0)),
        ],
        [out, out],
        [staged, staged, staged, pltpu.VMEM((ROWS, lanes), F32)],
        15 * MICRO,
        "project",
    )


CHANS = 16


def ordered(flag, own, other):
    part = own.shape[0] // 2
    waves = []
    for wave in range(2):
        mine, rest = own[wave * part : (wave + 1) * part], other[wave * part : (wave + 1) * part]
        waves += [jnp.where(flag, mine, rest), jnp.where(flag, rest, mine)]
    return jnp.concatenate(waves, 0)


def triangle_kernel(flag, a0, a1, b0, b1, keep_ref, send_ref):
    kept_first = flag[0] == 0
    part = b0.shape[1] // 2
    for chan in range(CHANS):
        rows = jnp.concatenate([a0[chan], a1[chan]], 0)
        one, two = [
            dot(jnp.concatenate([b[chan, part * u : part * u + part] for b in (b0, b1)], 0), rows, NT)
            for u in range(2)
        ]
        keep_ref[chan] = jnp.where(kept_first, one, two)
        send_ref[chan] = jnp.where(kept_first, two, one).astype(BF16)


def triangle(which, a, b):
    chans, half, lanes = a[0].shape
    lead = lambda i, *_: (i, 0, 0)
    block = (CHANS, half, lanes)
    out = (chans, half, 2 * half)
    return call(
        triangle_kernel,
        (chans // CHANS,),
        [which],
        [(v, block, lead) for v in (*a, *b)],
        [(out, F32, (CHANS, half, 2 * half), lead), (out, BF16, (CHANS, half, 2 * half), lead)],
        [],
        14 * MICRO,
        "triangle",
    )


GROUP = 16


T1_ROW, T2_ROW, OUT_ROW, OG_ROW, DIST_ROW, NORM_ROW, BIAS_ROW, LOSS_ROW, SUM_ROWS = (
    0, 512, 1024, 1152, 1280, 1344, 1350, 1351, 1352,
)


def row_sums(values):
    return jnp.sum(jnp.transpose(values), 0, keepdims=True)


def pair_kernel(
    first_call, last_call,
    place, x_keep, x_recv, acts_ref, code_ref, ln_ref, w_outT, w_out, w_ogT, w_t1T, w_t1,
    w_t2T, w_t2, w_distT, w_dist, bias_ref, *rest,
):
    prior = () if first_call else rest[:2]
    dx_ref, sums, wide, x_s, acts_s, dx_s, code_s = rest[len(prior) :]
    chans = acts_ref.shape[0]
    lanes = 128 * GROUP
    bins = w_distT.shape[0]
    hidden_width = w_t1T.shape[0]

    @pl.when(pl.program_id(0) == 0)
    def _():
        if first_call:
            sums[...] = jnp.zeros_like(sums)
            wide[...] = jnp.zeros_like(wide)
        else:
            sums[...] = prior[0][...]
            wide[...] = prior[1][...]

    spread_rows(x_s, x_keep[...] + x_recv[...].astype(F32))
    spread_rows(acts_s, acts_ref[...])
    code_s[...] = code_ref[0].astype(F32)
    param = [widen(ln_ref[index], lanes) for index in range(6)]
    bin_index = lax.broadcasted_iota(jnp.int32, (bins, lanes), 0).astype(F32)

    def fold(values):
        return sum(values[:, 128 * part : 128 * part + 128] for part in range(GROUP))

    def add(row, values):
        sums[row : row + values.shape[0]] += values

    def group(step, carry):
        first = step * GROUP
        x = take_rows(x_s, first, GROUP)
        acts = take_rows(acts_s, first, GROUP)
        code = code_rows(code_s, first, GROUP)
        normed_two, rstd_two = column_stats(x)
        tri = (normed_two * param[2] + param[3]).astype(BF16)
        out = dot(w_outT[...], tri)
        normed_one, _ = column_stats(acts)
        low = (normed_one * param[0] + param[1]).astype(BF16)
        gate = sigmoid(dot(w_ogT[...], low))
        z1 = acts + gate * out
        normed_three, rstd_three = column_stats(z1)
        trans = (normed_three * param[4] + param[5]).astype(BF16)
        pre = dot(w_t1T[...], trans)
        sig = sigmoid(pre)
        act = pre * sig
        hidden = act.astype(BF16)
        slope = sig * (1.0 + (pre - act))
        final = (z1 + dot(w_t2T[...], hidden)).astype(BF16)
        logits = dot(w_distT[...], final) + widen(bias_ref[...], lanes)
        top = jnp.max(logits, 0, keepdims=True)
        powers = jnp.exp(logits - top)
        total = jnp.sum(powers, 0, keepdims=True)
        present = jnp.where(code < 0.0, 0.0, 1.0)
        hot = bin_index == code
        picked = jnp.sum(jnp.where(hot, logits, 0.0), 0, keepdims=True)
        sums[LOSS_ROW : LOSS_ROW + 1] += fold(present * (jnp.log(total) + top) - picked)
        d_logits = (powers * (present / total) - jnp.where(hot, 1.0, 0.0)).astype(BF16)
        add(DIST_ROW, dot(d_logits, final, NT))
        wide[5, :bins] += fold(d_logits.astype(F32))
        d_final = dot(w_dist[...], d_logits)
        d_trans = d_final.astype(BF16)
        add(T2_ROW, dot(hidden, d_trans, NT))
        d_pre = (dot(w_t2[...], d_trans) * slope).astype(BF16)
        add(T1_ROW, dot(d_pre, trans, NT))
        d_tn = dot(w_t1[...], d_pre)
        wide[2] += fold(d_tn * normed_three)
        wide[3] += fold(d_tn)
        d_z1 = d_final + column_back(d_tn * param[4], normed_three, rstd_three)
        d_gated = d_z1 * gate
        d_out = d_gated.astype(BF16)
        d_og = (d_gated * out * (1.0 - gate)).astype(BF16)
        add(OUT_ROW, dot(d_out, tri, NT))
        g_og = dot(d_og, jnp.concatenate([low, normed_one.astype(BF16)], 0), NT)
        add(OG_ROW, g_og[:, :chans])
        wide[6] += g_og[:, chans:]
        wide[4] += fold(d_og.astype(F32))
        d_xn = dot(w_out[...], d_out)
        wide[0] += fold(d_xn * normed_two)
        wide[1] += fold(d_xn)
        d_x = column_back(d_xn * param[2], normed_two, rstd_two)
        put_rows(dx_s, first, GROUP, d_x)
        return carry

    lax.fori_loop(0, ROWS // GROUP, group, 0)
    gather_rows(dx_s, dx_ref)

    if last_call:

        @pl.when(pl.program_id(0) == pl.num_programs(0) - 1)
        def _():
            gate_w = w_ogT[...].astype(F32)
            for index in range(4):
                add(NORM_ROW + index, row_sums(wide[index]))
            add(NORM_ROW + 4, jnp.sum(gate_w * wide[6], 0, keepdims=True))
            add(NORM_ROW + 5, jnp.sum(gate_w * jnp.sum(wide[4], 1, keepdims=True), 0, keepdims=True))
            add(BIAS_ROW, row_sums(wide[5]))


def pair_block(place, x_keep, x_recv, acts_kj, ln_wide, weights, bias, prior, last_call):
    chans, rows, lanes = x_keep.shape
    block = (chans, ROWS, lanes)
    mid = lambda i, *_: (0, i, 0)

    def where(i, spot):
        return 8 * ((i % 2) ^ spot[0]) + 2 * spot[1] + i // 2

    full = [(w, w.shape, fixed(*([0] * w.ndim))) for w in (ln_wide, *weights, bias, *prior)]
    shapes = [(SUM_ROWS, 128), (7, 128, 128)]
    return call(
        functools.partial(pair_kernel, not prior, last_call),
        (rows // ROWS,),
        [place],
        [
            (x_keep, block, mid),
            (x_recv, block, mid),
            (acts_kj, block, lambda i, spot: (0, where(i, spot), 0)),
            (acts_kj, (1, ROWS, lanes), lambda i, spot: (chans, where(i, spot), 0)),
        ]
        + full,
        [((chans, rows, lanes), BF16, block, mid)]
        + [(s, F32, s, fixed(*([0] * len(s)))) for s in shapes],
        [pltpu.VMEM((ROWS, chans, lanes), t) for t in (F32, BF16, BF16)] + [pltpu.VMEM((ROWS, lanes), F32)],
        35 * MICRO,
        "pair",
    )


def right_back_kernel(flag, *refs):
    owns, others, firsts, seconds = refs[:4], refs[4:8], refs[8:12], refs[12:16]
    out0, out1 = refs[16:]
    half = out0.shape[1]
    own_first = flag[0] == 0
    for chan in range(CHANS):
        grads = jnp.concatenate(
            [ordered(own_first, owns[q][chan], others[q][chan]) for q in range(4)], 1
        )
        values = jnp.concatenate([v[q][chan] for q in range(4) for v in (firsts, seconds)], 0)
        total = dot(grads, values).astype(BF16)
        out0[chan] = total[:half]
        out1[chan] = total[half:]


def right_back(which, owns, others, firsts, seconds):
    chans, half, lanes = firsts[0].shape
    lead = lambda i, *_: (i, 0, 0)
    out = ((chans, half, lanes), BF16, (CHANS, half, lanes), lead)
    return call(
        right_back_kernel,
        (chans // CHANS,),
        [which],
        [(v, (CHANS, half, 2 * half), lead) for v in (*owns, *others)]
        + [(v, (CHANS, half, lanes), lead) for v in (*firsts, *seconds)],
        [out, out],
        [],
        25 * MICRO,
        "right_back",
    )


def turn_kernel(first, second, out_ref):
    for chan in range(first.shape[0]):
        out_ref[chan] = jnp.transpose(jnp.concatenate([first[chan], second[chan]], 0))


def turn(first, second):
    chans, half, lanes = first.shape
    lead = lambda i, *_: (i, 0, 0)
    count = next(n for n in (43, 16, 8, 4, 2, 1) if chans % n == 0)
    block = (count, half, lanes)
    return call(
        turn_kernel,
        (chans // count,),
        [],
        [(first, block, lead), (second, block, lead)],
        [((chans, lanes, 2 * half), BF16, (count, lanes, 2 * half), lead)],
        [],
        12 * MICRO,
        "turn",
    )[0]


def left_back_kernel(flag, *refs):
    owns, others, firsts, seconds = refs[:4], refs[4:8], refs[8:12], refs[12:16]
    out0, out1 = refs[16:]
    half = out0.shape[1]
    for chan in range(CHANS):
        total = None
        for pair in range(2):
            own_first = flag[0] == pair
            grads, values = [], []
            for q in (2 * pair, 2 * pair + 1):
                grads.append(ordered(own_first, owns[q][chan], others[q][chan]))
                values += [firsts[q][chan], seconds[q][chan]]
            term = dot(jnp.concatenate(grads, 0), jnp.concatenate(values, 0), TN)
            total = term if total is None else total + term
        total = total.astype(BF16)
        out0[chan] = total[:half]
        out1[chan] = total[half:]


def left_back(which, owns, others, firsts, seconds):
    chans, half, lanes = firsts[0].shape
    lead = lambda i, *_: (i, 0, 0)
    out = ((chans, half, lanes), BF16, (CHANS, half, lanes), lead)
    return call(
        left_back_kernel,
        (chans // CHANS,),
        [which],
        [(v, (CHANS, half, 2 * half), lead) for v in (*owns, *others)]
        + [(v, (CHANS, half, lanes), lead) for v in (*firsts, *seconds)],
        [out, out],
        [],
        25 * MICRO,
        "left_back",
    )


SIDE_ROWS = 272


def input_back_kernel(count, first_call, last_call, acts_ref, code_ref, w_ref, ln_ref, *rest):
    grads, rest = rest[:count], rest[count:]
    prior = () if first_call else rest[:3]
    out_ref, g_ref, sum_ref, acts_s, grad_s, code_s = rest[len(prior) :]
    width = grads[0].shape[0]
    chans = acts_ref.shape[0]

    @pl.when(pl.program_id(0) == 0)
    def _():
        if first_call:
            out_ref[...] = jnp.zeros_like(out_ref)
            g_ref[...] = jnp.zeros_like(g_ref)
            sum_ref[...] = jnp.zeros_like(sum_ref)
        else:
            out_ref[...] = prior[0][...]
            g_ref[...] = prior[1][...]
            sum_ref[...] = prior[2][...]

    code_s[...] = code_ref[0].astype(F32)
    spread_rows(acts_s, acts_ref[...])
    total = grads[0][...].astype(F32)
    for ref in grads[1:]:
        total = total + ref[...].astype(F32)
    spread_rows(grad_s, total)

    def some(step, carry):
        start = step * INPUT_GROUP
        values = take_rows(acts_s, start, INPUT_GROUP)
        lanes = values.shape[1]
        normed, _ = column_stats(values)
        low = (normed * widen(ln_ref[0], lanes) + widen(ln_ref[1], lanes)).astype(BF16)
        proj = dot(w_ref[...], low)
        gate = sigmoid(proj[width:])
        mask = present_rows(code_s, start, INPUT_GROUP)
        d_value = take_rows(grad_s, start, INPUT_GROUP) * mask * gate
        d_gate = d_value * proj[:width] * (1.0 - gate)
        d_proj = jnp.concatenate([d_value.astype(BF16), d_gate.astype(BF16)], 0)
        g_all = dot(d_proj, jnp.concatenate([low, normed.astype(BF16)], 0), NT)
        out_ref[: 2 * width] += g_all[:, :chans]
        g_ref[...] += g_all[:, chans:]
        wide = d_proj.astype(F32)
        sum_ref[...] += sum(wide[:, 128 * u : 128 * u + 128] for u in range(lanes // 128))
        return carry

    lax.fori_loop(0, ROWS // INPUT_GROUP, some, 0)

    if last_call:

        @pl.when(pl.program_id(0) == pl.num_programs(0) - 1)
        def _():
            part = w_ref[...].astype(F32)
            gain = jnp.sum(part * g_ref[...], 0, keepdims=True)
            shift = jnp.sum(part * jnp.sum(sum_ref[...], 1, keepdims=True), 0, keepdims=True)
            out_ref[2 * width : 2 * width + 1] = gain
            out_ref[2 * width + 1 : 2 * width + 2] = shift


def input_back(acts, w_part, ln_wide, grads, prior, last_call):
    chans, rows, lanes = acts.shape[0] - 1, acts.shape[1], acts.shape[2]
    block = (chans, ROWS, lanes)
    mid = lambda i, *_: (0, i, 0)
    depth = w_part.shape[0]
    shapes = [(SIDE_ROWS, chans), (depth, chans), (depth, 128)]
    return call(
        functools.partial(input_back_kernel, len(grads), not prior, last_call),
        (rows // ROWS,),
        [],
        [
            (acts, block, mid),
            (acts, (1, ROWS, lanes), lambda i, *_: (chans, i, 0)),
            (w_part, w_part.shape, fixed(0, 0)),
            (ln_wide, ln_wide.shape, fixed(0, 0, 0)),
        ]
        + [(v, block, mid) for v in grads]
        + [(v, v.shape, fixed(0, 0)) for v in prior],
        [(s, F32, s, fixed(0, 0)) for s in shapes],
        [
            pltpu.VMEM((ROWS, chans, lanes), BF16),
            pltpu.VMEM((ROWS, chans, lanes), F32),
            pltpu.VMEM((ROWS, lanes), F32),
        ],
        16 * MICRO,
        "input_back",
    )


def reduce_kernel(pair_ref, left_ref, right_ref, out_ref, full_s, core_s, crop_s, row_s, send, recv):
    side, spot, level = lax.axis_index("col"), lax.axis_index("crop"), lax.axis_index("row")
    mesh_id = pl.DeviceIdType.MESH
    sibling = {"col": 1 - side}
    crops = [{"crop": lax.rem(spot + n, 4)} for n in range(1, 4)]
    levels = [{"row": lax.rem(level + n, 4)} for n in range(1, 4)]
    barrier = pltpu.get_barrier_semaphore()
    for device in [sibling] + crops + levels:
        pl.semaphore_signal(barrier, inc=1, device_id=device, device_id_type=mesh_id)
    pl.semaphore_wait(barrier, 7)

    def copy(source, target, index, device):
        return pltpu.make_async_remote_copy(
            src_ref=source, dst_ref=target, send_sem=send.at[index], recv_sem=recv.at[index],
            device_id=device, device_id_type=mesh_id,
        )

    def run(copies):
        for one in copies:
            one.start()
        for one in copies:
            one.wait()

    half = full_s.shape[0] // 2
    quarter, share = half // 4, half // 16
    row = 0
    for ref in (pair_ref, left_ref, right_ref):
        full_s[row : row + ref.shape[0]] = ref[...]
        row += ref.shape[0]
    full_s[row:] = jnp.zeros((full_s.shape[0] - row, full_s.shape[1]), F32)
    base = pl.multiple_of(side * half, 8)
    run([copy(full_s.at[pl.ds(pl.multiple_of((1 - side) * half, 8), half)], core_s, 0, sibling)])
    full_s[pl.ds(base, half)] += core_s[...]
    def part(number):
        return pl.ds(pl.multiple_of(base + number * quarter, 8), quarter)

    run([copy(full_s.at[part(lax.rem(spot + n, 4))], crop_s.at[spot], n, crops[n - 1]) for n in range(1, 4)])
    mine = part(spot)
    crop_s[spot] = full_s[mine]
    full_s[mine] = crop_s[0] + crop_s[1] + crop_s[2] + crop_s[3]
    def slot(number):
        return pl.ds(pl.multiple_of(base + spot * quarter + number * share, 8), share)

    run([copy(full_s.at[slot(lax.rem(level + n, 4))], row_s.at[level], 3 + n, levels[n - 1]) for n in range(1, 4)])
    own = slot(level)
    row_s[level] = full_s[own]
    out_ref[own] = row_s[0] + row_s[1] + row_s[2] + row_s[3]
    run([copy(out_ref.at[own], out_ref.at[own], 6 + n, levels[n - 1]) for n in range(1, 4)])
    run([copy(out_ref.at[mine], out_ref.at[mine], 9 + n, crops[n - 1]) for n in range(1, 4)])
    run([copy(out_ref.at[pl.ds(base, half)], out_ref.at[pl.ds(base, half)], 13, sibling)])


ALL_ROWS = 2048


def reduce_all(*parts):
    lanes = parts[0].shape[1]
    return pl.pallas_call(
        reduce_kernel,
        out_shape=jax.ShapeDtypeStruct((ALL_ROWS, lanes), F32),
        scratch_shapes=[
            pltpu.VMEM((ALL_ROWS, lanes), F32),
            pltpu.VMEM((ALL_ROWS // 2, lanes), F32),
            pltpu.VMEM((4, ALL_ROWS // 8, lanes), F32),
            pltpu.VMEM((4, ALL_ROWS // 32, lanes), F32),
            pltpu.SemaphoreType.DMA((14,)),
            pltpu.SemaphoreType.DMA((14,)),
        ],
        compiler_params=pltpu.CompilerParams(
            collective_id=1, has_side_effects=True, vmem_limit_bytes=VMEM_LIMIT
        ),
        name="reduce_all",
    )(*parts)


def flip(a, b):
    return 2 * lax.rem(a // 2 + b // 2, 2) + lax.rem(a + b, 2)


def swap_bits(a):
    return 2 * lax.rem(a, 2) + a // 2


def spread_kernel(
    acts_ref, wave0_ref, wave1_ref, x_ref, y_ref, mid,
    plane_send, plane_recv, level_send, level_recv, share_send, share_recv, local,
):
    spot, level = lax.axis_index("crop"), lax.axis_index("row")
    chans = acts_ref.shape[0]
    cuts = [(0, chans // 2), (chans // 2, chans - chans // 2)]
    waves = (wave0_ref, wave1_ref)
    mesh_id = pl.DeviceIdType.MESH
    barrier = pltpu.get_barrier_semaphore()
    for n in range(1, 4):
        for device in ({"crop": lax.rem(spot + n, 4)}, {"row": lax.rem(level + n, 4)}):
            pl.semaphore_signal(barrier, inc=1, device_id=device, device_id_type=mesh_id)
    pl.semaphore_wait(barrier, 6)

    def plane_copy(wave, cut, distance):
        first, count = cuts[cut]
        target = flip(spot, distance)
        source = acts_ref.at[
            pl.ds(first, count), pl.ds(pl.multiple_of(32 * target + 16 * wave, 16), 16)
        ]
        landing = mid.at[wave, distance, pl.ds(first, count)]
        index = 8 * wave + 4 * cut + distance
        if distance == 0:
            return pltpu.make_async_copy(source, landing, plane_recv.at[index])
        return pltpu.make_async_remote_copy(
            src_ref=source, dst_ref=landing, send_sem=plane_send.at[index], recv_sem=plane_recv.at[index],
            device_id={"crop": target}, device_id_type=mesh_id,
        )

    def landed(wave, cut, label):
        first, count = cuts[cut]
        return waves[wave].at[pl.ds(first, count), pl.ds(16 * label, 16)]

    def level_copy(wave, cut, label, distance):
        first, count = cuts[cut]
        source = mid.at[wave, distance, pl.ds(first, count)]
        target = swap_bits(flip(spot, distance))
        index = 8 * wave + 4 * cut + label
        remote = pltpu.make_async_remote_copy(
            src_ref=source, dst_ref=landed(wave, cut, label),
            send_sem=level_send.at[index], recv_sem=level_recv.at[index],
            device_id={"row": target}, device_id_type=mesh_id,
        )
        return target, remote, pltpu.make_async_copy(source, landed(wave, cut, label), local.at[2 * wave + cut])

    def each_level(action, wave, cut):
        for label in range(4):
            for distance in range(4):

                @pl.when(flip(level, label) == distance)
                def _(label=label, distance=distance):
                    action(wave, cut, label, distance)

    def shares(cut, label):
        first, count = cuts[cut]
        index = 8 * cut + 2 * label
        return [
            pltpu.make_async_remote_copy(
                src_ref=landed(0, cut, label),
                dst_ref=ref.at[pl.ds(first, count), pl.ds(16 * label, 16)],
                send_sem=share_send.at[index + n], recv_sem=share_recv.at[index + n],
                device_id={"crop": flip(spot, 1 + n)}, device_id_type=mesh_id,
            )
            for n, ref in enumerate((x_ref, y_ref))
        ]

    plane = [
        [[plane_copy(wave, cut, distance) for distance in range(4)] for cut in range(2)] for wave in range(2)
    ]
    for wave in range(2):
        for cut in range(2):
            for one in plane[wave][cut]:
                one.start()

    def begin(wave, cut, label, distance):
        one = plane[wave][cut][distance]
        one.wait() if distance == 0 else one.wait_recv()
        target, remote, stay = level_copy(wave, cut, label, distance)

        @pl.when(target == level)
        def _():
            stay.start()

        @pl.when(target != level)
        def _():
            remote.start()

    def arrive(wave, cut, label, distance):
        target, remote, stay = level_copy(wave, cut, label, distance)

        @pl.when(target == level)
        def _():
            stay.wait()

        @pl.when(target != level)
        def _():
            remote.wait_recv()
            remote.wait_send()

    def pass_on(cut):
        each_level(arrive, 0, cut)
        for label in range(4):
            for one in shares(cut, label):
                one.start()

    each_level(begin, 0, 0)
    each_level(begin, 0, 1)
    each_level(begin, 1, 0)
    pass_on(0)
    each_level(begin, 1, 1)
    pass_on(1)
    for wave in range(2):
        for cut in range(2):
            for one in plane[wave][cut][1:]:
                one.wait_send()
    each_level(arrive, 1, 0)
    each_level(arrive, 1, 1)
    for cut in range(2):
        for label in range(4):
            for one in shares(cut, label):
                one.wait()


def spread(acts_major):
    chans, rows, lanes = acts_major.shape
    anywhere = pl.BlockSpec(memory_space=pl.ANY)
    return pl.pallas_call(
        spread_kernel,
        in_specs=[anywhere],
        out_specs=[anywhere] * 4,
        out_shape=[jax.ShapeDtypeStruct((chans, rows // 2, lanes), BF16)] * 4,
        scratch_shapes=[pltpu.VMEM((2, 4, chans, rows // 8, lanes), BF16)]
        + [pltpu.SemaphoreType.DMA((16,)) for _ in range(6)]
        + [pltpu.SemaphoreType.DMA((4,))],
        compiler_params=pltpu.CompilerParams(
            collective_id=2, has_side_effects=True, vmem_limit_bytes=VMEM_LIMIT
        ),
        name="spread",
    )(acts_major)


def update_kernel(early_ref, *refs):
    ins, outs = refs[:21], refs[21:]
    left_ref = early_ref.at[pl.ds(SUM_ROWS, SIDE_ROWS)]
    right_ref = early_ref.at[pl.ds(SUM_ROWS + SIDE_ROWS, SIDE_ROWS)]
    loss_ref, total_ref, norm_ref = outs[21:]
    total = early_ref[LOSS_ROW - 1, 127]
    inverse = 1.0 / total
    half = SIDE_ROWS - 16
    grads = [
        jnp.concatenate(
            [
                jnp.transpose(left_ref[:half]),
                jnp.transpose(right_ref[:half]),
                jnp.transpose(early_ref[OG_ROW : OG_ROW + 128]),
            ],
            1,
        ),
        jnp.transpose(early_ref[OUT_ROW : OUT_ROW + 128]),
        jnp.transpose(early_ref[T1_ROW : T1_ROW + 512]),
        early_ref[T2_ROW : T2_ROW + 512],
        jnp.transpose(early_ref[DIST_ROW : DIST_ROW + 64]),
        jnp.concatenate(
            [
                left_ref[half : half + 2] + right_ref[half : half + 2] + early_ref[NORM_ROW + 4 : NORM_ROW + 6],
                early_ref[NORM_ROW : NORM_ROW + 4],
            ],
            0,
        ),
        early_ref[BIAS_ROW : BIAS_ROW + 1, :64],
    ]
    grads = [grad * inverse for grad in grads]
    squares = sum(jnp.sum(grad * grad, keepdims=True).reshape(1, 1) for grad in grads)
    grad_norm = jnp.sqrt(squares)
    scale = CLIP_NORM / jnp.maximum(grad_norm, CLIP_NORM)
    rates = (LEARN_RATE,) * 5 + (GAIN_RATE,) * 2
    for index in range(7):
        new = adamw_update(
            ins[index][...], ins[7 + index][...], ins[14 + index][...], grads[index], scale, rates[index]
        )
        for part in range(3):
            outs[7 * part + index][...] = new[part]
    norm_ref[...] = grad_norm
    loss_ref[...] = jnp.sum(early_ref[LOSS_ROW : LOSS_ROW + 1], keepdims=True).reshape(1, 1)
    total_ref[...] = jnp.full((1, 1), total, F32)


def update(early, params, firsts, seconds):
    flat = [v.reshape(1, -1) if v.ndim == 1 else v for v in (*params, *firsts, *seconds)]
    shapes = [v.shape for v in flat] + [(1, 1)] * 3
    outs = pl.pallas_call(
        update_kernel,
        out_shape=[jax.ShapeDtypeStruct(s, F32) for s in shapes],
        compiler_params=pltpu.CompilerParams(vmem_limit_bytes=VMEM_LIMIT),
        name="update",
    )(early, *flat)
    outs = [v.reshape(-1) if index in (6, 13, 20) else v for index, v in enumerate(outs)]
    return (*outs[:21], *[v[0, 0] for v in outs[21:]])


def after(value, *earlier):
    return lax.optimization_barrier((value, *earlier))[0]


def on_device_planes(
    pair_acts, residue_mask, dist_bins, w_in, w_out, w_t1, w_t2, w_dist, norm_params, dist_bias, *moments
):
    firsts, seconds = moments[:7], moments[7:]
    spot = lax.axis_index("crop")
    level = lax.axis_index("row")
    side = lax.axis_index("col")
    rows, cols, chans = pair_acts.shape[1:]
    width = w_out.shape[0]
    sub = rows // 4
    plane_of = (0, 2, 1, 3)
    crop = (level % 2) * 2 + level // 2

    def over_x(v):
        return lax.ppermute(v, "crop", [(g, g ^ 1) for g in range(4)])

    def over_y(v):
        return lax.ppermute(v, "crop", [(g, g ^ 2) for g in range(4)])

    def over_both(v):
        return lax.ppermute(v, "crop", [(g, g ^ 3) for g in range(4)])

    def over_core(v):
        return lax.ppermute(v, "col", [(0, 1), (1, 0)])

    own_mask = residue_mask[0]
    row_own = lax.dynamic_slice_in_dim(own_mask, rows * level, rows)
    col_own = lax.dynamic_slice_in_dim(own_mask, cols * side, cols)
    code_own = jnp.where((row_own[:, None] * col_own[None, :]) > 0, dist_bins[0], -1).astype(BF16)
    acts_major = jnp.transpose(pair_acts[0], (2, 0, 1))

    acts_major = jnp.concatenate([acts_major, code_own[None]], 0)
    wave0, wave1, wave0_x, wave0_y = spread(acts_major)

    count = jnp.sum(own_mask).astype(F32)
    share_count = lax.axis_size("row") * lax.axis_size("col")
    low_in, low_out, low_t1, low_t2, low_dist = [
        weight.astype(BF16) for weight in (w_in, w_out, w_t1, w_t2, w_dist)
    ]
    ln_wide = jnp.broadcast_to(norm_params[:, :, None], (*norm_params.shape, 128))
    bias_wide = jnp.broadcast_to(dist_bias[:, None], (dist_bias.shape[0], 128))
    in_T = low_in.T

    proj_w = in_T[: 4 * width]
    acts, left, right = {}, {}, {}

    def share(q, source, shift, half):
        acts[q, half] = shift(acts[source, half])

    def values(q, half, *earlier):
        left[q, half], right[q, half] = project(after(acts[q, half], *earlier), proj_w, ln_wide)
        return right[q, half]

    acts[0, 0], acts[0, 1], acts[1, 0], acts[2, 0] = wave0, wave1, wave0_x, wave0_y
    share(1, 0, over_x, 1)
    share(2, 0, over_y, 1)
    done = values(0, 0)
    done = values(0, 1, done)

    weights = (
        low_out.T, low_out, in_T[4 * width :], low_t1.T, low_t1, low_t2.T, low_t2, low_dist.T, low_dist,
    )
    flags = [(side ^ ((spot ^ q) // 2) ^ (crop // 2)).astype(jnp.int32)[None] for q in range(4)]
    keeps, recvs, dx_own, dx_other, seen, seen_other = {}, {}, {}, {}, {}, {}
    sums = []

    def forward(q, *earlier):
        mine = [after(left[0, h], *earlier) for h in range(2)]
        keeps[q], send = triangle(flags[q], mine, [right[q, h] for h in range(2)])
        recvs[q] = over_core(send)
        return send

    def middle(q, *earlier):
        owner = spot ^ q
        place = jnp.stack([(owner ^ crop) & 1, owner]).astype(jnp.int32)
        dx_own[q], *sums[:] = pair_block(
            after(place, *earlier), keeps[q], recvs[q], acts_kj, ln_wide, weights, bias_wide, list(sums), q == 3
        )
        dx_other[q] = over_core(dx_own[q])
        seen[q] = (lambda v: v, over_x, over_y, over_both)[q](dx_own[q])
        seen_other[q] = over_core(seen[q]) if q in (1, 2) else dx_other[q]
        return dx_own[q]

    done = forward(0, done)
    acts_kj = turn(after(acts[0, 0], done), acts[0, 1])
    done = values(1, 0, acts_kj)
    done = values(2, 0, done)
    done = middle(0, done)
    acts[1, 1], acts[2, 1] = after(acts[1, 1], done), after(acts[2, 1], done)
    acts[3, 0] = over_y(after(acts[1, 0], done))
    acts[3, 1] = over_x(acts[2, 1])
    done = values(1, 1, done)
    done = forward(1, done)
    done = values(2, 1, done)
    done = forward(2, done)
    done = middle(1, done)
    done = middle(2, done)
    done = values(3, 0, done)
    done = values(3, 1, done, seen[1])
    done = forward(3, done)
    done = middle(3, done, seen[2], seen_other[1])
    d_left = left_back(
        after(flags[0], done, seen_other[2]),
        [dx_own[q] for q in range(4)],
        [dx_other[q] for q in range(4)],
        [right[q, 0] for q in range(4)],
        [right[q, 1] for q in range(4)],
    )
    pair_sums = sums[0].at[LOSS_ROW - 1, 127].set(count * count / share_count)
    left_sum, right_sum = [], []
    left_w, right_w = in_T[: 2 * width], in_T[2 * width : 4 * width]
    for h in range(2):
        left_sum = input_back(acts[0, h], left_w, ln_wide, [d_left[h]], left_sum, h == 1)
        if h == 0:
            seen_other[3] = over_core(after(seen[3], left_sum[0]))
    d_right = right_back(
        after(flags[0], left_sum[0]),
        [seen[q] for q in range(4)],
        [seen_other[q] for q in range(4)],
        [left[q, 0] for q in range(4)],
        [left[q, 1] for q in range(4)],
    )
    for h in range(2):
        right_sum = input_back(acts[0, h], right_w, ln_wide, [d_right[h]], right_sum, h == 1)
    params = (w_in, w_out, w_t1, w_t2, w_dist, norm_params, dist_bias)
    return update(reduce_all(pair_sums, left_sum[0], right_sum[0]), params, firsts, seconds)


def solution(mesh):
    planes = mesh.shape["crop"] == 4 and mesh.shape["row"] == 4 and mesh.shape["col"] == 2
    body = on_device_planes if planes else on_device_general
    in_specs = (
        P("crop", "row", "col", None),
        P("crop", None),
        P("crop", "row", "col"),
    ) + (P(),) * 21
    return jax.shard_map(
        body, mesh=mesh, in_specs=in_specs, out_specs=(P(),) * 24, check_vma=False
    )
```

```python
import functools

import jax
import jax.numpy as jnp
from jax import lax
from jax.experimental import pallas as pl
from jax.experimental.pallas import tpu as pltpu
from jax.sharding import PartitionSpec as P

STEP = 10


NORM_EPS = 1e-05
CLIP_NORM = 0.02
LEARN_RATE = 0.03
GAIN_RATE = 0.3
BETA_ONE = 0.9
BETA_TWO = 0.999
ADAM_EPS = 1e-08
WEIGHT_DECAY = 0.01


def standardize(values):
    center = values - jnp.mean(values, -1, keepdims=True)
    rstd = lax.rsqrt(jnp.mean(center * center, -1, keepdims=True) + NORM_EPS)
    return (center * rstd, rstd)


def standard_back(grad, normed, rstd):
    return rstd * (
        grad
        - jnp.mean(grad, -1, keepdims=True)
        - normed * jnp.mean(grad * normed, -1, keepdims=True)
    )


def linear(values, weight):
    return jnp.einsum("ijc,cd->ijd", values, weight, preferred_element_type=jnp.float32)


def weight_grad(values, grad):
    return jnp.einsum("ijc,ijd->cd", values, grad, preferred_element_type=jnp.float32)


def transposed(grad, weight):
    return jnp.einsum("ijd,cd->ijc", grad, weight, preferred_element_type=jnp.float32)


def adamw_update(weight, first, second, grad, scale, rate):
    clipped = grad * scale
    first_new = BETA_ONE * first + (1.0 - BETA_ONE) * clipped
    second_new = BETA_TWO * second + (1.0 - BETA_TWO) * clipped * clipped
    first_hat = first_new / (1.0 - BETA_ONE**STEP)
    second_hat = second_new / (1.0 - BETA_TWO**STEP)
    stepped = weight - rate * (
        first_hat / (jnp.sqrt(second_hat) + ADAM_EPS) + WEIGHT_DECAY * weight
    )
    return (stepped, first_new, second_new)


def on_device_general(
    pair_acts,
    residue_mask,
    dist_bins,
    w_in,
    w_out,
    w_t1,
    w_t2,
    w_dist,
    norm_params,
    dist_bias,
    m_in,
    m_out,
    m_t1,
    m_t2,
    m_dist,
    m_norm,
    m_bias,
    v_in,
    v_out,
    v_t1,
    v_t2,
    v_dist,
    v_norm,
    v_bias,
):
    tile_rows = pair_acts.shape[1]
    tile_cols = pair_acts.shape[2]
    width = w_out.shape[0]
    row_first = lax.axis_index("row") * tile_rows
    col_first = lax.axis_index("col") * tile_cols
    mask_vals = residue_mask[0].astype(jnp.float32)
    row_mask = lax.dynamic_slice_in_dim(mask_vals, row_first, tile_rows)
    col_mask = lax.dynamic_slice_in_dim(mask_vals, col_first, tile_cols)
    pair_mask = row_mask[:, None] * col_mask[None, :]
    mask_cube = pair_mask[..., None]
    pair_total = lax.psum(jnp.sum(pair_mask), ("crop", "row", "col"))
    low_in, low_out, low_t1, low_t2, low_dist = [
        weight.astype(jnp.bfloat16) for weight in (w_in, w_out, w_t1, w_t2, w_dist)
    ]
    acts = pair_acts[0].astype(jnp.float32)
    normed_one, rstd_one = standardize(acts)
    pair_norm = (normed_one * norm_params[0] + norm_params[1]).astype(jnp.bfloat16)
    projected = linear(pair_norm, low_in)
    left_proj = projected[..., :width]
    left_sig = jax.nn.sigmoid(projected[..., width : 2 * width])
    right_proj = projected[..., 2 * width : 3 * width]
    right_sig = jax.nn.sigmoid(projected[..., 3 * width : 4 * width])
    gate_sig = jax.nn.sigmoid(projected[..., 4 * width :])
    left_vals = (mask_cube * left_sig * left_proj).astype(jnp.bfloat16)
    right_vals = (mask_cube * right_sig * right_proj).astype(jnp.bfloat16)
    strips = lax.all_gather(right_vals, "row", axis=0, tiled=True)
    piece = strips
    triangle = jnp.transpose(
        lax.psum_scatter(
            jnp.einsum("jkc,ikc->jic", piece, left_vals, preferred_element_type=jnp.float32),
            "col",
            scatter_dimension=0,
            tiled=True,
        ),
        (1, 0, 2),
    )
    normed_two, rstd_two = standardize(triangle)
    tri_norm = (normed_two * norm_params[2] + norm_params[3]).astype(jnp.bfloat16)
    out_proj = linear(tri_norm, low_out)
    updated = acts + gate_sig * out_proj
    normed_three, rstd_three = standardize(updated)
    trans_in = (normed_three * norm_params[4] + norm_params[5]).astype(jnp.bfloat16)
    pre_act = linear(trans_in, low_t1)
    hidden = jax.nn.silu(pre_act).astype(jnp.bfloat16)
    final = updated + linear(hidden, low_t2)
    final_low = final.astype(jnp.bfloat16)
    logits = linear(final_low, low_dist) + dist_bias
    log_total = jax.nn.logsumexp(logits, -1)
    onehot = (dist_bins[0][..., None] == jnp.arange(w_dist.shape[1])).astype(jnp.float32)
    loss_local = jnp.sum(pair_mask * (log_total - jnp.sum(logits * onehot, -1)))
    d_logits = (mask_cube * (jnp.exp(logits - log_total[..., None]) - onehot) / pair_total).astype(
        jnp.bfloat16
    )
    grad_dist = weight_grad(final_low, d_logits)
    grad_bias = jnp.sum(d_logits.astype(jnp.float32), (0, 1))
    d_final = transposed(d_logits, low_dist)
    d_trans = d_final.astype(jnp.bfloat16)
    grad_t2 = weight_grad(hidden, d_trans)
    d_hidden = transposed(d_trans, low_t2)
    sig_pre = jax.nn.sigmoid(pre_act)
    d_pre = (d_hidden * sig_pre * (1.0 + pre_act * (1.0 - sig_pre))).astype(jnp.bfloat16)
    grad_t1 = weight_grad(trans_in, d_pre)
    d_trans_in = transposed(d_pre, low_t1)
    d_updated = d_final + standard_back(d_trans_in * norm_params[4], normed_three, rstd_three)
    d_out = (d_updated * gate_sig).astype(jnp.bfloat16)
    d_out_gate = d_updated * out_proj * gate_sig * (1.0 - gate_sig)
    grad_out = weight_grad(tri_norm, d_out)
    d_tri_norm = transposed(d_out, low_out)
    d_triangle = standard_back(d_tri_norm * norm_params[2], normed_two, rstd_two).astype(
        jnp.bfloat16
    )
    d_rows = lax.all_gather(d_triangle, "col", axis=1, tiled=True)
    d_left = jnp.einsum("ijc,jkc->ikc", d_rows, strips, preferred_element_type=jnp.float32)
    piece = d_rows
    d_right = lax.psum_scatter(
        jnp.einsum("ijc,ikc->jkc", piece, left_vals, preferred_element_type=jnp.float32).astype(
            jnp.bfloat16
        ),
        "row",
        scatter_dimension=0,
        tiled=True,
    ).astype(jnp.float32)
    d_proj = jnp.concatenate(
        [
            d_left * mask_cube * left_sig,
            d_left * mask_cube * left_proj * left_sig * (1.0 - left_sig),
            d_right * mask_cube * right_sig,
            d_right * mask_cube * right_proj * right_sig * (1.0 - right_sig),
            d_out_gate,
        ],
        -1,
    ).astype(jnp.bfloat16)
    grad_in = weight_grad(pair_norm, d_proj)
    d_pair_norm = transposed(d_proj, low_in)
    grad_norms = jnp.stack(
        [
            jnp.sum(d_pair_norm * normed_one, (0, 1)),
            jnp.sum(d_pair_norm, (0, 1)),
            jnp.sum(d_tri_norm * normed_two, (0, 1)),
            jnp.sum(d_tri_norm, (0, 1)),
            jnp.sum(d_trans_in * normed_three, (0, 1)),
            jnp.sum(d_trans_in, (0, 1)),
        ]
    )
    summed = lax.psum(
        (grad_in, grad_out, grad_t1, grad_t2, grad_dist, grad_norms, grad_bias, loss_local),
        ("crop", "row", "col"),
    )
    grads = summed[:7]
    squares = jnp.zeros((), jnp.float32)
    for grad in grads:
        squares = squares + jnp.sum(grad * grad)
    grad_norm = jnp.sqrt(squares)
    scale = CLIP_NORM / jnp.maximum(grad_norm, CLIP_NORM)
    params = (w_in, w_out, w_t1, w_t2, w_dist, norm_params, dist_bias)
    firsts = (m_in, m_out, m_t1, m_t2, m_dist, m_norm, m_bias)
    seconds = (v_in, v_out, v_t1, v_t2, v_dist, v_norm, v_bias)
    rates = (LEARN_RATE, LEARN_RATE, LEARN_RATE, LEARN_RATE, LEARN_RATE, GAIN_RATE, GAIN_RATE)
    results = [
        adamw_update(
            params[index], firsts[index], seconds[index], grads[index], scale, rates[index]
        )
        for index in range(7)
    ]
    return (
        results[0][0],
        results[1][0],
        results[2][0],
        results[3][0],
        results[4][0],
        results[5][0],
        results[6][0],
        results[0][1],
        results[1][1],
        results[2][1],
        results[3][1],
        results[4][1],
        results[5][1],
        results[6][1],
        results[0][2],
        results[1][2],
        results[2][2],
        results[3][2],
        results[4][2],
        results[5][2],
        results[6][2],
        summed[7],
        pair_total,
        grad_norm,
    )


F32 = jnp.float32
BF16 = jnp.bfloat16
NT = (((1,), (1,)), ((), ()))
NN = (((1,), (0,)), ((), ()))
TN = (((0,), (0,)), ((), ()))
MICRO = 1e3
VMEM_LIMIT = 56 * 1024 * 1024


def dot(left, right, dims=NN):
    return lax.dot_general(left, right, dims, preferred_element_type=F32)


def sigmoid(values):
    return 0.5 * jnp.tanh(0.5 * values) + 0.5


def column_stats(values):
    center = values - jnp.mean(values, 0, keepdims=True)
    rstd = lax.rsqrt(jnp.mean(center * center, 0, keepdims=True) + NORM_EPS)
    return center * rstd, rstd


def column_back(grad, normed, rstd):
    return rstd * (
        grad
        - jnp.mean(grad, 0, keepdims=True)
        - normed * jnp.mean(grad * normed, 0, keepdims=True)
    )


def widen(param, lanes):
    return jnp.concatenate([param] * (lanes // param.shape[1]), 1)


def spread_rows(scratch, block):
    scratch[...] = jnp.swapaxes(block, 0, 1).astype(scratch.dtype)


def take_rows(scratch, start, count):
    return jnp.concatenate([scratch[start + u] for u in range(count)], 1).astype(F32)


def put_rows(scratch, start, count, values):
    lanes = values.shape[1] // count
    for u in range(count):
        scratch[start + u] = values[:, u * lanes : (u + 1) * lanes].astype(scratch.dtype)


def gather_rows(scratch, out_ref):
    out_ref[...] = jnp.swapaxes(scratch[...], 0, 1)


def call(kernel, grid, scalars, ins, outs, scratch, flops, name, aliases=None):
    return pl.pallas_call(
        kernel,
        grid_spec=pltpu.PrefetchScalarGridSpec(
            num_scalar_prefetch=len(scalars),
            grid=grid,
            in_specs=[pl.BlockSpec(block, index) for _, block, index in ins],
            out_specs=[pl.BlockSpec(block, index) for _, _, block, index in outs],
            scratch_shapes=scratch,
        ),
        out_shape=[jax.ShapeDtypeStruct(shape, dtype) for shape, dtype, _, _ in outs],
        compiler_params=pltpu.CompilerParams(vmem_limit_bytes=VMEM_LIMIT),
        cost_estimate=pl.CostEstimate(flops=int(flops), bytes_accessed=1, transcendentals=0),
        name=name,
        input_output_aliases=aliases or {},
    )(*scalars, *[a for a, _, _ in ins])


def code_rows(code_s, start, count):
    return jnp.concatenate([code_s[pl.ds(start + u, 1), :] for u in range(count)], 1)


def present_rows(code_s, start, count):
    return jnp.where(code_rows(code_s, start, count) < 0.0, 0.0, 1.0)


ROWS = 16
PROJECT_GROUP = 8
INPUT_GROUP = 8


def prepare_kernel(
    acts_ref, code_ref, w_in, w_out, w_t1, w_t2, w_dist, norms, bias,
    out_ref, projT, ogT, outT, out_w, t1T, t1, t2T, t2, distT, dist, ln_ref, bias_ref, rows_s,
):
    chans = acts_ref.shape[2]
    for row in range(ROWS):
        rows_s[row] = jnp.transpose(acts_ref[row])
    out_ref[:chans] = jnp.swapaxes(rows_s[...], 0, 1)
    out_ref[chans] = code_ref[...]

    @pl.when(pl.program_id(0) == 0)
    def _():
        count = projT.shape[0]
        projT[...] = jnp.transpose(w_in[:, :count]).astype(BF16)
        ogT[...] = jnp.transpose(w_in[:, count:]).astype(BF16)
        for weight, plain, turned in (
            (w_out, out_w, outT), (w_t1, t1, t1T), (w_t2, t2, t2T), (w_dist, distT, dist)
        ):
            plain[...] = weight[...].astype(BF16)
            turned[...] = jnp.transpose(weight[...]).astype(BF16)
        for index in range(6):
            ln_ref[index] = jnp.transpose(jnp.broadcast_to(norms[index : index + 1, :], (128, chans)))
        bias_ref[...] = jnp.transpose(jnp.broadcast_to(bias[...], (128, bias.shape[1])))


def prepare(acts, code, w_in, w_out, w_t1, w_t2, w_dist, norms, bias):
    rows, lanes, chans = acts.shape
    width = w_out.shape[0]
    params = (w_in, w_out, w_t1, w_t2, w_dist.T, norms, bias.reshape(1, -1))
    shapes = [(4 * width, chans), (chans, chans)]
    for weight in (w_out, w_t1, w_t2, w_dist):
        turned = (weight.shape[1], weight.shape[0])
        shapes += [turned, weight.shape]
    shapes = [(shape, BF16) for shape in shapes]
    shapes += [((6, chans, 128), F32), ((bias.shape[0], 128), F32)]
    return call(
        prepare_kernel,
        (rows // ROWS,),
        [],
        [
            (acts, (ROWS, lanes, chans), lambda i, *_: (i, 0, 0)),
            (code, (ROWS, lanes), lambda i, *_: (i, 0)),
        ]
        + [(v, v.shape, fixed(*([0] * v.ndim))) for v in params],
        [((chans + 1, rows, lanes), BF16, (chans + 1, ROWS, lanes), lambda i, *_: (0, i, 0))]
        + [(shape, dtype, shape, fixed(*([0] * len(shape)))) for shape, dtype in shapes],
        [pltpu.VMEM((ROWS, chans, lanes), BF16)],
        1,
        "prepare",
    )


def project_kernel(acts_ref, code_ref, w_ref, ln_ref, a_ref, b_ref, acts_s, a_s, b_s, code_s):
    width = a_ref.shape[0]
    code_s[...] = code_ref[0].astype(F32)
    spread_rows(acts_s, acts_ref[...])

    def some(step, carry):
        start = step * PROJECT_GROUP
        values = take_rows(acts_s, start, PROJECT_GROUP)
        lanes = values.shape[1]
        normed, _ = column_stats(values)
        low = (normed * widen(ln_ref[0], lanes) + widen(ln_ref[1], lanes)).astype(BF16)
        proj = dot(w_ref[...], low)
        mask = present_rows(code_s, start, PROJECT_GROUP)
        left = proj[:width] * sigmoid(proj[width : 2 * width]) * mask
        right = proj[2 * width : 3 * width] * sigmoid(proj[3 * width :]) * mask
        put_rows(a_s, start, PROJECT_GROUP, left)
        put_rows(b_s, start, PROJECT_GROUP, right)
        return carry

    lax.fori_loop(0, ROWS // PROJECT_GROUP, some, 0)
    gather_rows(a_s, a_ref)
    gather_rows(b_s, b_ref)


def fixed(*zeros):
    return lambda i, *_: zeros


def project(acts, w_proj, ln_wide):
    chans, rows, lanes = acts.shape[0] - 1, acts.shape[1], acts.shape[2]
    block = (chans, ROWS, lanes)
    mid = lambda i, *_: (0, i, 0)
    out = ((chans, rows, lanes), BF16, block, mid)
    staged = pltpu.VMEM((ROWS, chans, lanes), BF16)
    return call(
        project_kernel,
        (rows // ROWS,),
        [],
        [
            (acts, block, mid),
            (acts, (1, ROWS, lanes), lambda i, *_: (chans, i, 0)),
            (w_proj, w_proj.shape, fixed(0, 0)),
            (ln_wide, ln_wide.shape, fixed(0, 0, 0)),
        ],
        [out, out],
        [staged, staged, staged, pltpu.VMEM((ROWS, lanes), F32)],
        15 * MICRO,
        "project",
    )


CHANS = 16
TRIANGLE_CHANS = 32


def ordered(flag, own, other):
    part = own.shape[0] // 2
    waves = []
    for wave in range(2):
        mine, rest = own[wave * part : (wave + 1) * part], other[wave * part : (wave + 1) * part]
        waves += [jnp.where(flag, mine, rest), jnp.where(flag, rest, mine)]
    return jnp.concatenate(waves, 0)


def kept_first(ids, q):
    return ids[2] ^ ((ids[0] ^ q) // 2) ^ (ids[1] // 2) == 0


def triangle_kernel(q, ids, a0, a1, b0, b1, keep_ref, send_ref):
    first = kept_first(ids, q)
    part = b0.shape[1] // 2
    for chan in range(TRIANGLE_CHANS):
        rows = jnp.concatenate([a0[chan], a1[chan]], 0)
        x = dot(jnp.concatenate([b0[chan], b1[chan]], 0), rows, NT)
        one = jnp.concatenate([x[:part], x[2 * part : 3 * part]], 0)
        two = jnp.concatenate([x[part : 2 * part], x[3 * part :]], 0)
        keep_ref[chan] = jnp.where(first, one, two)
        send_ref[chan] = jnp.where(first, two, one).astype(BF16)


def triangle(q, ids, a, b):
    chans, half, lanes = a[0].shape
    lead = lambda i, *_: (i, 0, 0)
    block = (TRIANGLE_CHANS, half, lanes)
    out = (chans, half, 2 * half)
    return call(
        functools.partial(triangle_kernel, q),
        (chans // TRIANGLE_CHANS,),
        [ids],
        [(v, block, lead) for v in (*a, *b)],
        [(out, F32, (TRIANGLE_CHANS, half, 2 * half), lead), (out, BF16, (TRIANGLE_CHANS, half, 2 * half), lead)],
        [],
        14 * MICRO,
        "triangle",
    )


GROUP = 16


T1_ROW, T2_ROW, OUT_ROW, OG_ROW, DIST_ROW, NORM_ROW, BIAS_ROW, LOSS_ROW, SUM_ROWS = (
    0, 512, 1024, 1152, 1280, 1344, 1350, 1351, 1352,
)


def row_sums(values):
    return jnp.sum(jnp.transpose(values), 0, keepdims=True)


def pair_kernel(
    first_call, last_call,
    ids, x_keep, x_recv, acts_ref, code_ref, ln_ref, w_outT, w_out, w_ogT, w_t1T, w_t1,
    w_t2T, w_t2, w_distT, w_dist, bias_ref, *rest,
):
    prior = () if first_call else rest[:2]
    dx_ref, sums, wide, x_s, acts_s, dx_s, code_s = rest[len(prior) :]
    chans = acts_ref.shape[0]
    lanes = 128 * GROUP
    bins = w_distT.shape[0]
    hidden_width = w_t1T.shape[0]

    @pl.when(pl.program_id(0) == 0)
    def _():
        if first_call:
            sums[...] = jnp.zeros_like(sums)
            wide[...] = jnp.zeros_like(wide)
        else:
            sums[...] = prior[0][...]
            wide[...] = prior[1][...]

    spread_rows(x_s, x_keep[...] + x_recv[...].astype(F32))
    spread_rows(acts_s, acts_ref[...])
    code_s[...] = code_ref[0].astype(F32)
    param = [widen(ln_ref[index], lanes) for index in range(6)]
    bin_index = lax.broadcasted_iota(jnp.int32, (bins, lanes), 0).astype(F32)

    def fold(values):
        return sum(values[:, 128 * part : 128 * part + 128] for part in range(GROUP))

    def add(row, values):
        sums[row : row + values.shape[0]] += values

    def group(step, carry):
        first = step * GROUP
        x = take_rows(x_s, first, GROUP)
        acts = take_rows(acts_s, first, GROUP)
        code = code_rows(code_s, first, GROUP)
        normed_two, rstd_two = column_stats(x)
        tri = (normed_two * param[2] + param[3]).astype(BF16)
        out = dot(w_outT[...], tri)
        normed_one, _ = column_stats(acts)
        low = (normed_one * param[0] + param[1]).astype(BF16)
        gate = sigmoid(dot(w_ogT[...], low))
        z1 = acts + gate * out
        normed_three, rstd_three = column_stats(z1)
        trans = (normed_three * param[4] + param[5]).astype(BF16)
        pre = dot(w_t1T[...], trans)
        sig = sigmoid(pre)
        act = pre * sig
        hidden = act.astype(BF16)
        slope = sig * (1.0 + (pre - act))
        final = (z1 + dot(w_t2T[...], hidden)).astype(BF16)
        logits = dot(w_distT[...], final) + widen(bias_ref[...], lanes)
        top = jnp.max(logits, 0, keepdims=True)
        powers = jnp.exp(logits - top)
        total = jnp.sum(powers, 0, keepdims=True)
        present = jnp.where(code < 0.0, 0.0, 1.0)
        hot = bin_index == code
        picked = jnp.sum(jnp.where(hot, logits, 0.0), 0, keepdims=True)
        sums[LOSS_ROW : LOSS_ROW + 1] += fold(present * (jnp.log(total) + top) - picked)
        d_logits = (powers * (present / total) - jnp.where(hot, 1.0, 0.0)).astype(BF16)
        add(DIST_ROW, dot(d_logits, final, NT))
        wide[5, :bins] += fold(d_logits.astype(F32))
        d_final = dot(w_dist[...], d_logits)
        d_trans = d_final.astype(BF16)
        add(T2_ROW, dot(hidden, d_trans, NT))
        d_pre = (dot(w_t2[...], d_trans) * slope).astype(BF16)
        add(T1_ROW, dot(d_pre, trans, NT))
        d_tn = dot(w_t1[...], d_pre)
        wide[2] += fold(d_tn * normed_three)
        wide[3] += fold(d_tn)
        d_z1 = d_final + column_back(d_tn * param[4], normed_three, rstd_three)
        d_gated = d_z1 * gate
        d_out = d_gated.astype(BF16)
        d_og = (d_gated * out * (1.0 - gate)).astype(BF16)
        add(OUT_ROW, dot(d_out, tri, NT))
        wide[6] += dot(d_og, normed_one.astype(BF16), NT)
        wide[4] += fold(d_og.astype(F32))
        d_xn = dot(w_out[...], d_out)
        wide[0] += fold(d_xn * normed_two)
        wide[1] += fold(d_xn)
        d_x = column_back(d_xn * param[2], normed_two, rstd_two)
        put_rows(dx_s, first, GROUP, d_x)
        return carry

    lax.fori_loop(0, ROWS // GROUP, group, 0)
    gather_rows(dx_s, dx_ref)

    if last_call:

        @pl.when(pl.program_id(0) == pl.num_programs(0) - 1)
        def _():
            gate_w = w_ogT[...].astype(F32)
            for index in range(4):
                add(NORM_ROW + index, row_sums(wide[index]))
            total = jnp.sum(wide[4], 1, keepdims=True)
            add(OG_ROW, affine_grad(wide[6], total, ln_ref))
            add(NORM_ROW + 4, jnp.sum(gate_w * wide[6], 0, keepdims=True))
            add(NORM_ROW + 5, jnp.sum(gate_w * total, 0, keepdims=True))
            add(BIAS_ROW, row_sums(wide[5]))


def pair_block(q, ids, x_keep, x_recv, acts_kj, ln_wide, weights, bias, prior, last_call):
    chans, rows, lanes = x_keep.shape
    block = (chans, ROWS, lanes)
    mid = lambda i, *_: (0, i, 0)

    def where(i, ids):
        owner = ids[0] ^ q
        return 8 * ((i % 2) ^ (owner % 2) ^ (ids[1] % 2)) + 2 * owner + i // 2

    full = [(w, w.shape, fixed(*([0] * w.ndim))) for w in (ln_wide, *weights, bias, *prior)]
    shapes = [(SUM_ROWS, 128), (7, 128, 128)]
    return call(
        functools.partial(pair_kernel, not prior, last_call),
        (rows // ROWS,),
        [ids],
        [
            (x_keep, block, mid),
            (x_recv, block, mid),
            (acts_kj, block, lambda i, ids: (0, where(i, ids), 0)),
            (acts_kj, (1, ROWS, lanes), lambda i, ids: (chans, where(i, ids), 0)),
        ]
        + full,
        [((chans, rows, lanes), BF16, block, mid)]
        + [(s, F32, s, fixed(*([0] * len(s)))) for s in shapes],
        [pltpu.VMEM((ROWS, chans, lanes), t) for t in (F32, BF16, BF16)] + [pltpu.VMEM((ROWS, lanes), F32)],
        35 * MICRO,
        "pair",
    )


def right_back_kernel(ids, *refs):
    owns, others, firsts, seconds = refs[:4], refs[4:8], refs[8:12], refs[12:16]
    out0, out1 = refs[16:]
    half = out0.shape[1]
    own_first = kept_first(ids, 0)
    for chan in range(CHANS):
        grads = jnp.concatenate(
            [ordered(own_first, owns[q][chan], others[q][chan]) for q in range(4)], 1
        )
        values = jnp.concatenate([v[q][chan] for q in range(4) for v in (firsts, seconds)], 0)
        total = dot(grads, values).astype(BF16)
        out0[chan] = total[:half]
        out1[chan] = total[half:]


def right_back(ids, owns, others, firsts, seconds):
    chans, half, lanes = firsts[0].shape
    lead = lambda i, *_: (i, 0, 0)
    out = ((chans, half, lanes), BF16, (CHANS, half, lanes), lead)
    return call(
        right_back_kernel,
        (chans // CHANS,),
        [ids],
        [(v, (CHANS, half, 2 * half), lead) for v in (*owns, *others)]
        + [(v, (CHANS, half, lanes), lead) for v in (*firsts, *seconds)],
        [out, out],
        [],
        25 * MICRO,
        "right_back",
    )


def turn_kernel(first, second, out_ref):
    for chan in range(first.shape[0]):
        out_ref[chan] = jnp.transpose(jnp.concatenate([first[chan], second[chan]], 0))


def turn(first, second):
    chans, half, lanes = first.shape
    lead = lambda i, *_: (i, 0, 0)
    count = next(n for n in (43, 16, 8, 4, 2, 1) if chans % n == 0)
    block = (count, half, lanes)
    return call(
        turn_kernel,
        (chans // count,),
        [],
        [(first, block, lead), (second, block, lead)],
        [((chans, lanes, 2 * half), BF16, (count, lanes, 2 * half), lead)],
        [],
        12 * MICRO,
        "turn",
    )[0]


def left_back_kernel(ids, *refs):
    owns, others, firsts, seconds = refs[:4], refs[4:8], refs[8:12], refs[12:16]
    out0, out1 = refs[16:]
    half = out0.shape[1]
    for chan in range(CHANS):
        total = None
        for pair in range(2):
            own_first = kept_first(ids, 2 * pair)
            grads, values = [], []
            for q in (2 * pair, 2 * pair + 1):
                grads.append(ordered(own_first, owns[q][chan], others[q][chan]))
                values += [firsts[q][chan], seconds[q][chan]]
            term = dot(jnp.concatenate(grads, 0), jnp.concatenate(values, 0), TN)
            total = term if total is None else total + term
        total = total.astype(BF16)
        out0[chan] = total[:half]
        out1[chan] = total[half:]


def left_back(ids, owns, others, firsts, seconds):
    chans, half, lanes = firsts[0].shape
    lead = lambda i, *_: (i, 0, 0)
    out = ((chans, half, lanes), BF16, (CHANS, half, lanes), lead)
    return call(
        left_back_kernel,
        (chans // CHANS,),
        [ids],
        [(v, (CHANS, half, 2 * half), lead) for v in (*owns, *others)]
        + [(v, (CHANS, half, lanes), lead) for v in (*firsts, *seconds)],
        [out, out],
        [],
        25 * MICRO,
        "left_back",
    )


SIDE_ROWS = 272


def affine_grad(normed_grad, total, ln_ref):
    gain, shift = jnp.transpose(ln_ref[0])[:1], jnp.transpose(ln_ref[1])[:1]
    return normed_grad * gain + total * shift


def input_back_kernel(count, first_call, last_call, acts_ref, code_ref, w_ref, ln_ref, *rest):
    grads, rest = rest[:count], rest[count:]
    prior = () if first_call else rest[:3]
    out_ref, g_ref, sum_ref, acts_s, grad_s, code_s = rest[len(prior) :]
    width = grads[0].shape[0]
    chans = acts_ref.shape[0]

    @pl.when(pl.program_id(0) == 0)
    def _():
        if first_call:
            out_ref[...] = jnp.zeros_like(out_ref)
            g_ref[...] = jnp.zeros_like(g_ref)
            sum_ref[...] = jnp.zeros_like(sum_ref)
        else:
            out_ref[...] = prior[0][...]
            g_ref[...] = prior[1][...]
            sum_ref[...] = prior[2][...]

    code_s[...] = code_ref[0].astype(F32)
    spread_rows(acts_s, acts_ref[...])
    total = grads[0][...].astype(F32)
    for ref in grads[1:]:
        total = total + ref[...].astype(F32)
    spread_rows(grad_s, total)

    def some(step, carry):
        start = step * INPUT_GROUP
        values = take_rows(acts_s, start, INPUT_GROUP)
        lanes = values.shape[1]
        normed, _ = column_stats(values)
        low = (normed * widen(ln_ref[0], lanes) + widen(ln_ref[1], lanes)).astype(BF16)
        proj = dot(w_ref[...], low)
        gate = sigmoid(proj[width:])
        mask = present_rows(code_s, start, INPUT_GROUP)
        d_value = take_rows(grad_s, start, INPUT_GROUP) * mask * gate
        d_gate = d_value * proj[:width] * (1.0 - gate)
        d_proj = jnp.concatenate([d_value.astype(BF16), d_gate.astype(BF16)], 0)
        g_ref[...] += dot(d_proj, normed.astype(BF16), NT)
        wide = d_proj.astype(F32)
        sum_ref[...] += sum(wide[:, 128 * u : 128 * u + 128] for u in range(lanes // 128))
        return carry

    lax.fori_loop(0, ROWS // INPUT_GROUP, some, 0)

    if last_call:

        @pl.when(pl.program_id(0) == pl.num_programs(0) - 1)
        def _():
            part = w_ref[...].astype(F32)
            total = jnp.sum(sum_ref[...], 1, keepdims=True)
            gain = jnp.sum(part * g_ref[...], 0, keepdims=True)
            shift = jnp.sum(part * total, 0, keepdims=True)
            out_ref[: 2 * width] = affine_grad(g_ref[...], total, ln_ref)
            out_ref[2 * width : 2 * width + 1] = gain
            out_ref[2 * width + 1 : 2 * width + 2] = shift


def input_back(acts, part, w_proj, ln_wide, grads, prior, last_call):
    chans, rows, lanes = acts.shape[0] - 1, acts.shape[1], acts.shape[2]
    block = (chans, ROWS, lanes)
    mid = lambda i, *_: (0, i, 0)
    depth = w_proj.shape[0] // 2
    shapes = [(SIDE_ROWS, chans), (depth, chans), (depth, 128)]
    return call(
        functools.partial(input_back_kernel, len(grads), not prior, last_call),
        (rows // ROWS,),
        [],
        [
            (acts, block, mid),
            (acts, (1, ROWS, lanes), lambda i, *_: (chans, i, 0)),
            (w_proj, (depth, chans), fixed(part, 0)),
            (ln_wide, ln_wide.shape, fixed(0, 0, 0)),
        ]
        + [(v, block, mid) for v in grads]
        + [(v, v.shape, fixed(0, 0)) for v in prior],
        [(s, F32, s, fixed(0, 0)) for s in shapes],
        [
            pltpu.VMEM((ROWS, chans, lanes), BF16),
            pltpu.VMEM((ROWS, chans, lanes), F32),
            pltpu.VMEM((ROWS, lanes), F32),
        ],
        16 * MICRO,
        "input_back",
    )


def reduce_kernel(pair_ref, left_ref, right_ref, out_ref, full_s, core_s, crop_s, row_s, send, recv):
    side, spot, level = lax.axis_index("col"), lax.axis_index("crop"), lax.axis_index("row")
    mesh_id = pl.DeviceIdType.MESH
    sibling = {"col": 1 - side}
    crops = [{"crop": lax.rem(spot + n, 4)} for n in range(1, 4)]
    levels = [{"row": lax.rem(level + n, 4)} for n in range(1, 4)]
    barrier = pltpu.get_barrier_semaphore()
    for device in [sibling] + crops + levels:
        pl.semaphore_signal(barrier, inc=1, device_id=device, device_id_type=mesh_id)
    pl.semaphore_wait(barrier, 7)

    def copy(source, target, index, device):
        return pltpu.make_async_remote_copy(
            src_ref=source, dst_ref=target, send_sem=send.at[index], recv_sem=recv.at[index],
            device_id=device, device_id_type=mesh_id,
        )

    def run(copies):
        for one in copies:
            one.start()
        for one in copies:
            one.wait()

    half = full_s.shape[0] // 2
    quarter, share = half // 4, half // 16
    row = 0
    for ref in (pair_ref, left_ref, right_ref):
        full_s[row : row + ref.shape[0]] = ref[...]
        row += ref.shape[0]
    full_s[row:] = jnp.zeros((full_s.shape[0] - row, full_s.shape[1]), F32)
    base = pl.multiple_of(side * half, 8)
    run([copy(full_s.at[pl.ds(pl.multiple_of((1 - side) * half, 8), half)], core_s, 0, sibling)])
    full_s[pl.ds(base, half)] += core_s[...]
    def part(number):
        return pl.ds(pl.multiple_of(base + number * quarter, 8), quarter)

    run([copy(full_s.at[part(lax.rem(spot + n, 4))], crop_s.at[spot], n, crops[n - 1]) for n in range(1, 4)])
    mine = part(spot)
    crop_s[spot] = full_s[mine]
    full_s[mine] = crop_s[0] + crop_s[1] + crop_s[2] + crop_s[3]
    def slot(number):
        return pl.ds(pl.multiple_of(base + spot * quarter + number * share, 8), share)

    run([copy(full_s.at[slot(lax.rem(level + n, 4))], row_s.at[level], 3 + n, levels[n - 1]) for n in range(1, 4)])
    own = slot(level)
    row_s[level] = full_s[own]
    out_ref[own] = row_s[0] + row_s[1] + row_s[2] + row_s[3]
    run([copy(out_ref.at[own], out_ref.at[own], 6 + n, levels[n - 1]) for n in range(1, 4)])
    run([copy(out_ref.at[mine], out_ref.at[mine], 9 + n, crops[n - 1]) for n in range(1, 4)])
    run([copy(out_ref.at[pl.ds(base, half)], out_ref.at[pl.ds(base, half)], 13, sibling)])


ALL_ROWS = 2048


def reduce_all(*parts):
    lanes = parts[0].shape[1]
    return pl.pallas_call(
        reduce_kernel,
        out_shape=jax.ShapeDtypeStruct((ALL_ROWS, lanes), F32),
        scratch_shapes=[
            pltpu.VMEM((ALL_ROWS, lanes), F32),
            pltpu.VMEM((ALL_ROWS // 2, lanes), F32),
            pltpu.VMEM((4, ALL_ROWS // 8, lanes), F32),
            pltpu.VMEM((4, ALL_ROWS // 32, lanes), F32),
            pltpu.SemaphoreType.DMA((14,)),
            pltpu.SemaphoreType.DMA((14,)),
        ],
        compiler_params=pltpu.CompilerParams(
            collective_id=1, has_side_effects=True, vmem_limit_bytes=VMEM_LIMIT
        ),
        name="reduce_all",
    )(*parts)


def flip(a, b):
    return 2 * lax.rem(a // 2 + b // 2, 2) + lax.rem(a + b, 2)


def swap_bits(a):
    return 2 * lax.rem(a, 2) + a // 2


def spread_kernel(
    acts_ref, w_ref, ln_ref, wave0_ref, wave1_ref, x_ref, y_ref, a_ref, b_ref, mid,
    plane_send, plane_recv, share_send, share_recv, level_send, level_recv, local,
    wave_v, a_v, b_v, acts_s, a_s, b_s, code_s,
):
    spot, level = lax.axis_index("crop"), lax.axis_index("row")
    chans = acts_ref.shape[0]
    early, middle = chans // 4, 5 * chans // 8
    cuts = [[(0, early), (early, middle - early), (middle, chans - middle)], [(0, chans)]]
    waves = (wave0_ref, wave1_ref)
    mesh_id = pl.DeviceIdType.MESH
    barrier = pltpu.get_barrier_semaphore()
    for n in range(1, 4):
        for device in ({"crop": lax.rem(spot + n, 4)}, {"row": lax.rem(level + n, 4)}):
            pl.semaphore_signal(barrier, inc=1, device_id=device, device_id_type=mesh_id)
    pl.semaphore_wait(barrier, 6)

    def plane_copy(wave, cut, distance):
        first, count = cuts[wave][cut]
        target = flip(spot, distance)
        source = acts_ref.at[
            pl.ds(first, count), pl.ds(pl.multiple_of(32 * target + 16 * wave, 16), 16)
        ]
        landing = mid.at[wave, distance, pl.ds(first, count)]
        index = 12 * wave + 4 * cut + distance
        if distance == 0:
            return pltpu.make_async_copy(source, landing, plane_recv.at[index])
        return pltpu.make_async_remote_copy(
            src_ref=source, dst_ref=landing, send_sem=plane_send.at[index], recv_sem=plane_recv.at[index],
            device_id={"crop": target}, device_id_type=mesh_id,
        )

    def landed(wave, cut, label):
        first, count = cuts[wave][cut]
        return waves[wave].at[pl.ds(first, count), pl.ds(16 * label, 16)]

    def level_copy(wave, cut, label, distance):
        first, count = cuts[wave][cut]
        source = mid.at[wave, distance, pl.ds(first, count)]
        target = swap_bits(flip(spot, distance))
        index = 12 * wave + 4 * cut + label
        remote = pltpu.make_async_remote_copy(
            src_ref=source, dst_ref=landed(wave, cut, label),
            send_sem=level_send.at[index], recv_sem=level_recv.at[index],
            device_id={"row": target}, device_id_type=mesh_id,
        )
        return target, remote, pltpu.make_async_copy(source, landed(wave, cut, label), local.at[3 * wave + cut])

    def each_level(action, wave, cut):
        for label in range(4):
            for distance in range(4):

                @pl.when(flip(level, label) == distance)
                def _(label=label, distance=distance):
                    action(wave, cut, label, distance)

    def shares(cut, label):
        first, count = cuts[0][cut]
        index = 8 * cut + 2 * label
        return [
            pltpu.make_async_remote_copy(
                src_ref=landed(0, cut, label),
                dst_ref=ref.at[pl.ds(first, count), pl.ds(16 * label, 16)],
                send_sem=share_send.at[index + n], recv_sem=share_recv.at[index + n],
                device_id={"crop": flip(spot, 1 + n)}, device_id_type=mesh_id,
            )
            for n, ref in enumerate((x_ref, y_ref))
        ]

    plane = [
        [[plane_copy(wave, cut, distance) for distance in range(4)] for cut in range(len(cuts[wave]))]
        for wave in range(2)
    ]
    for copies in plane[0] + plane[1]:
        for one in copies:
            one.start()

    def begin(wave, cut, label, distance):
        one = plane[wave][cut][distance]
        one.wait() if distance == 0 else one.wait_recv()
        target, remote, stay = level_copy(wave, cut, label, distance)

        @pl.when(target == level)
        def _():
            stay.start()

        @pl.when(target != level)
        def _():
            remote.start()

    def arrive(wave, cut, label, distance):
        target, remote, stay = level_copy(wave, cut, label, distance)

        @pl.when(target == level)
        def _():
            stay.wait()

        @pl.when(target != level)
        def _():
            remote.wait_recv()
            remote.wait_send()

    def pass_on(cut):
        each_level(arrive, 0, cut)
        for label in range(4):
            for one in shares(cut, label):
                one.start()

    for cut in range(3):
        each_level(begin, 0, cut)
    each_level(begin, 1, 0)
    for cut in range(3):
        pass_on(cut)
    fetch = pltpu.make_async_copy(wave0_ref, wave_v, local.at[4])
    fetch.start()
    fetch.wait()
    width = a_v.shape[0]

    def project_rows(step, carry):
        rows = pl.ds(pl.multiple_of(step * ROWS, ROWS), ROWS)
        project_kernel(
            wave_v.at[pl.ds(0, width), rows], wave_v.at[pl.ds(width, 1), rows], w_ref, ln_ref,
            a_v.at[:, rows], b_v.at[:, rows], acts_s, a_s, b_s, code_s,
        )
        return carry

    lax.fori_loop(0, wave_v.shape[1] // ROWS, project_rows, 0)
    results = [
        pltpu.make_async_copy(a_v, a_ref, local.at[5]), pltpu.make_async_copy(b_v, b_ref, local.at[6])
    ]
    for one in results:
        one.start()
    for copies in plane[0] + plane[1]:
        for one in copies[1:]:
            one.wait_send()
    for cut in range(3):
        for label in range(4):
            for one in shares(cut, label):
                one.wait()
    for one in results:
        one.wait()
    each_level(arrive, 1, 0)


def spread(acts_major, w_proj, ln_wide):
    chans, rows, lanes = acts_major.shape
    half, width = rows // 2, chans - 1
    anywhere = pl.BlockSpec(memory_space=pl.ANY)
    whole = pl.BlockSpec(memory_space=pltpu.VMEM)
    staged = pltpu.VMEM((ROWS, width, lanes), BF16)
    return pl.pallas_call(
        spread_kernel,
        in_specs=[anywhere, whole, whole],
        out_specs=[anywhere] * 6,
        out_shape=[jax.ShapeDtypeStruct((chans, half, lanes), BF16)] * 4
        + [jax.ShapeDtypeStruct((width, half, lanes), BF16)] * 2,
        scratch_shapes=[pltpu.VMEM((2, 4, chans, rows // 8, lanes), BF16)]
        + [pltpu.SemaphoreType.DMA((16,)) for _ in range(2)]
        + [pltpu.SemaphoreType.DMA((24,)) for _ in range(2)]
        + [pltpu.SemaphoreType.DMA((16,)) for _ in range(2)]
        + [pltpu.SemaphoreType.DMA((7,))]
        + [pltpu.VMEM((chans, half, lanes), BF16)]
        + [pltpu.VMEM((width, half, lanes), BF16)] * 2
        + [staged] * 3
        + [pltpu.VMEM((ROWS, lanes), F32)],
        compiler_params=pltpu.CompilerParams(
            collective_id=2, has_side_effects=True, vmem_limit_bytes=VMEM_LIMIT
        ),
        name="spread",
    )(acts_major, w_proj, ln_wide)


def update_kernel(early_ref, *refs):
    ins, outs = refs[:21], refs[21:]
    left_ref = early_ref.at[pl.ds(SUM_ROWS, SIDE_ROWS)]
    right_ref = early_ref.at[pl.ds(SUM_ROWS + SIDE_ROWS, SIDE_ROWS)]
    loss_ref, total_ref, norm_ref = outs[21:]
    total = early_ref[LOSS_ROW - 1, 127]
    inverse = 1.0 / total
    half = SIDE_ROWS - 16
    grads = [
        jnp.concatenate(
            [
                jnp.transpose(left_ref[:half]),
                jnp.transpose(right_ref[:half]),
                jnp.transpose(early_ref[OG_ROW : OG_ROW + 128]),
            ],
            1,
        ),
        jnp.transpose(early_ref[OUT_ROW : OUT_ROW + 128]),
        jnp.transpose(early_ref[T1_ROW : T1_ROW + 512]),
        early_ref[T2_ROW : T2_ROW + 512],
        early_ref[DIST_ROW : DIST_ROW + 64],
        jnp.concatenate(
            [
                left_ref[half : half + 2] + right_ref[half : half + 2] + early_ref[NORM_ROW + 4 : NORM_ROW + 6],
                early_ref[NORM_ROW : NORM_ROW + 4],
            ],
            0,
        ),
        early_ref[BIAS_ROW : BIAS_ROW + 1, :64],
    ]
    grads = [grad * inverse for grad in grads]
    squares = sum(jnp.sum(grad * grad, keepdims=True).reshape(1, 1) for grad in grads)
    grad_norm = jnp.sqrt(squares)
    scale = CLIP_NORM / jnp.maximum(grad_norm, CLIP_NORM)
    rates = (LEARN_RATE,) * 5 + (GAIN_RATE,) * 2
    for index in range(7):
        new = adamw_update(
            *[ins[7 * part + index][...].reshape(grads[index].shape) for part in range(3)],
            grads[index], scale, rates[index],
        )
        for part in range(3):
            outs[7 * part + index][...] = new[part].reshape(outs[7 * part + index].shape)
    norm_ref[...] = grad_norm
    loss_ref[...] = jnp.sum(early_ref[LOSS_ROW : LOSS_ROW + 1], keepdims=True).reshape(1, 1)
    total_ref[...] = jnp.full((1, 1), total, F32)


def update(early, params, firsts, seconds):
    flat = [v.T if index % 7 == 4 else v for index, v in enumerate((*params, *firsts, *seconds))]
    shapes = [v.shape for v in flat] + [(1, 1)] * 3
    outs = pl.pallas_call(
        update_kernel,
        out_shape=[jax.ShapeDtypeStruct(s, F32) for s in shapes],
        compiler_params=pltpu.CompilerParams(vmem_limit_bytes=VMEM_LIMIT),
        name="update",
    )(early, *flat)
    outs = [v.T if index in (4, 11, 18) else v for index, v in enumerate(outs)]
    return (*outs[:21], *[v[0, 0] for v in outs[21:]])


def after(value, *earlier):
    return lax.optimization_barrier((value, *earlier))[0]


def on_device_planes(
    pair_acts, residue_mask, dist_bins, w_in, w_out, w_t1, w_t2, w_dist, norm_params, dist_bias, *moments
):
    firsts, seconds = moments[:7], moments[7:]
    spot = lax.axis_index("crop")
    level = lax.axis_index("row")
    side = lax.axis_index("col")
    rows, cols, chans = pair_acts.shape[1:]
    width = w_out.shape[0]
    sub = rows // 4
    plane_of = (0, 2, 1, 3)
    crop = (level % 2) * 2 + level // 2

    def over_x(v):
        return lax.ppermute(v, "crop", [(g, g ^ 1) for g in range(4)])

    def over_y(v):
        return lax.ppermute(v, "crop", [(g, g ^ 2) for g in range(4)])

    def over_both(v):
        return lax.ppermute(v, "crop", [(g, g ^ 3) for g in range(4)])

    def over_core(v):
        return lax.ppermute(v, "col", [(0, 1), (1, 0)])

    own_mask = residue_mask[0]
    row_own = lax.dynamic_slice_in_dim(own_mask, rows * level, rows)
    col_own = lax.dynamic_slice_in_dim(own_mask, cols * side, cols)
    code_own = jnp.where((row_own[:, None] * col_own[None, :]) > 0, dist_bins[0], -1).astype(BF16)
    acts_major, proj_w, *weights, ln_wide, bias_wide = prepare(
        pair_acts[0], code_own, w_in, w_out, w_t1, w_t2, w_dist, norm_params, dist_bias
    )
    og_T, out_T, out_w, t1_T, t1_w, t2_T, t2_w, dist_T, dist_w = weights
    weights = (out_T, out_w, og_T, t1_T, t1_w, t2_T, t2_w, dist_T, dist_w)

    wave0, wave1, wave0_x, wave0_y, left_own, right_own = spread(acts_major, proj_w, ln_wide)

    count = jnp.sum(own_mask).astype(F32)
    share_count = lax.axis_size("row") * lax.axis_size("col")
    acts, left, right = {}, {}, {}

    def share(q, source, shift, half):
        acts[q, half] = shift(acts[source, half])

    def values(q, half, *earlier):
        left[q, half], right[q, half] = project(after(acts[q, half], *earlier), proj_w, ln_wide)
        return right[q, half]

    acts[0, 0], acts[0, 1], acts[1, 0], acts[2, 0] = wave0, wave1, wave0_x, wave0_y
    share(1, 0, over_x, 1)
    share(2, 0, over_y, 1)
    left[0, 0], right[0, 0] = left_own, right_own
    done = values(0, 1)

    ids = jnp.stack([spot, crop, side]).astype(jnp.int32)
    keeps, recvs, dx_own, dx_other, seen, seen_other = {}, {}, {}, {}, {}, {}
    sums = []

    def forward(q, *earlier):
        keeps[q], send = triangle(
            q, after(ids, *earlier), [left[0, h] for h in range(2)], [right[q, h] for h in range(2)]
        )
        recvs[q] = over_core(send)
        return send

    def middle(q, *earlier):
        dx_own[q], *sums[:] = pair_block(
            q, after(ids, *earlier), keeps[q], recvs[q], acts_kj, ln_wide, weights, bias_wide, list(sums), q == 3
        )
        dx_other[q] = over_core(dx_own[q])
        seen[q] = (lambda v: v, over_x, over_y, over_both)[q](dx_own[q])
        seen_other[q] = over_core(seen[q]) if q in (1, 2) else dx_other[q]
        return dx_own[q]

    done = forward(0, done)
    acts_kj = turn(after(acts[0, 0], done), acts[0, 1])
    done = values(1, 0, acts_kj)
    done = values(2, 0, done)
    done = middle(0, done)
    acts[1, 1], acts[2, 1] = after(acts[1, 1], done), after(acts[2, 1], done)
    acts[3, 0] = over_y(after(acts[1, 0], done))
    acts[3, 1] = over_x(acts[2, 1])
    done = values(1, 1, done)
    done = forward(1, done)
    done = values(2, 1, done)
    done = forward(2, done)
    done = middle(1, done)
    done = middle(2, done)
    done = values(3, 0, done)
    done = values(3, 1, done)
    done = forward(3, done)
    done = middle(3, done, seen[1], seen[2])
    d_left = left_back(
        after(ids, done, seen_other[1]),
        [dx_own[q] for q in range(4)],
        [dx_other[q] for q in range(4)],
        [right[q, 0] for q in range(4)],
        [right[q, 1] for q in range(4)],
    )
    pair_sums = sums[0].at[LOSS_ROW - 1, 127].set(count * count / share_count)
    left_sum, right_sum = [], []
    for h in range(2):
        left_sum = input_back(acts[0, h], 0, proj_w, ln_wide, [d_left[h]], left_sum, h == 1)
        if h == 0:
            seen_other[3] = over_core(after(seen[3], left_sum[0]))
    d_right = right_back(
        after(ids, left_sum[0], seen_other[2]),
        [seen[q] for q in range(4)],
        [seen_other[q] for q in range(4)],
        [left[q, 0] for q in range(4)],
        [left[q, 1] for q in range(4)],
    )
    for h in range(2):
        right_sum = input_back(acts[0, h], 1, proj_w, ln_wide, [d_right[h]], right_sum, h == 1)
    params = (w_in, w_out, w_t1, w_t2, w_dist, norm_params, dist_bias)
    return update(reduce_all(pair_sums, left_sum[0], right_sum[0]), params, firsts, seconds)


def solution(mesh):
    planes = mesh.shape["crop"] == 4 and mesh.shape["row"] == 4 and mesh.shape["col"] == 2
    body = on_device_planes if planes else on_device_general
    in_specs = (
        P("crop", "row", "col", None),
        P("crop", None),
        P("crop", "row", "col"),
    ) + (P(),) * 21
    return jax.shard_map(
        body, mesh=mesh, in_specs=in_specs, out_specs=(P(),) * 24, check_vma=False
    )
```

```python
import functools

import jax
import jax.numpy as jnp
from jax import lax
from jax.experimental import pallas as pl
from jax.experimental.pallas import tpu as pltpu
from jax.sharding import PartitionSpec as P

STEP = 10


NORM_EPS = 1e-05
CLIP_NORM = 0.02
LEARN_RATE = 0.03
GAIN_RATE = 0.3
BETA_ONE = 0.9
BETA_TWO = 0.999
ADAM_EPS = 1e-08
WEIGHT_DECAY = 0.01


def standardize(values):
    center = values - jnp.mean(values, -1, keepdims=True)
    rstd = lax.rsqrt(jnp.mean(center * center, -1, keepdims=True) + NORM_EPS)
    return (center * rstd, rstd)


def standard_back(grad, normed, rstd):
    return rstd * (
        grad
        - jnp.mean(grad, -1, keepdims=True)
        - normed * jnp.mean(grad * normed, -1, keepdims=True)
    )


def linear(values, weight):
    return jnp.einsum("ijc,cd->ijd", values, weight, preferred_element_type=jnp.float32)


def weight_grad(values, grad):
    return jnp.einsum("ijc,ijd->cd", values, grad, preferred_element_type=jnp.float32)


def transposed(grad, weight):
    return jnp.einsum("ijd,cd->ijc", grad, weight, preferred_element_type=jnp.float32)


def adamw_update(weight, first, second, grad, scale, rate):
    clipped = grad * scale
    first_new = BETA_ONE * first + (1.0 - BETA_ONE) * clipped
    second_new = BETA_TWO * second + (1.0 - BETA_TWO) * clipped * clipped
    first_hat = first_new / (1.0 - BETA_ONE**STEP)
    second_hat = second_new / (1.0 - BETA_TWO**STEP)
    stepped = weight - rate * (
        first_hat / (jnp.sqrt(second_hat) + ADAM_EPS) + WEIGHT_DECAY * weight
    )
    return (stepped, first_new, second_new)


def on_device_general(
    pair_acts,
    residue_mask,
    dist_bins,
    w_in,
    w_out,
    w_t1,
    w_t2,
    w_dist,
    norm_params,
    dist_bias,
    m_in,
    m_out,
    m_t1,
    m_t2,
    m_dist,
    m_norm,
    m_bias,
    v_in,
    v_out,
    v_t1,
    v_t2,
    v_dist,
    v_norm,
    v_bias,
):
    tile_rows = pair_acts.shape[1]
    tile_cols = pair_acts.shape[2]
    width = w_out.shape[0]
    row_first = lax.axis_index("row") * tile_rows
    col_first = lax.axis_index("col") * tile_cols
    mask_vals = residue_mask[0].astype(jnp.float32)
    row_mask = lax.dynamic_slice_in_dim(mask_vals, row_first, tile_rows)
    col_mask = lax.dynamic_slice_in_dim(mask_vals, col_first, tile_cols)
    pair_mask = row_mask[:, None] * col_mask[None, :]
    mask_cube = pair_mask[..., None]
    pair_total = lax.psum(jnp.sum(pair_mask), ("crop", "row", "col"))
    low_in, low_out, low_t1, low_t2, low_dist = [
        weight.astype(jnp.bfloat16) for weight in (w_in, w_out, w_t1, w_t2, w_dist)
    ]
    acts = pair_acts[0].astype(jnp.float32)
    normed_one, rstd_one = standardize(acts)
    pair_norm = (normed_one * norm_params[0] + norm_params[1]).astype(jnp.bfloat16)
    projected = linear(pair_norm, low_in)
    left_proj = projected[..., :width]
    left_sig = jax.nn.sigmoid(projected[..., width : 2 * width])
    right_proj = projected[..., 2 * width : 3 * width]
    right_sig = jax.nn.sigmoid(projected[..., 3 * width : 4 * width])
    gate_sig = jax.nn.sigmoid(projected[..., 4 * width :])
    left_vals = (mask_cube * left_sig * left_proj).astype(jnp.bfloat16)
    right_vals = (mask_cube * right_sig * right_proj).astype(jnp.bfloat16)
    strips = lax.all_gather(right_vals, "row", axis=0, tiled=True)
    piece = strips
    triangle = jnp.transpose(
        lax.psum_scatter(
            jnp.einsum("jkc,ikc->jic", piece, left_vals, preferred_element_type=jnp.float32),
            "col",
            scatter_dimension=0,
            tiled=True,
        ),
        (1, 0, 2),
    )
    normed_two, rstd_two = standardize(triangle)
    tri_norm = (normed_two * norm_params[2] + norm_params[3]).astype(jnp.bfloat16)
    out_proj = linear(tri_norm, low_out)
    updated = acts + gate_sig * out_proj
    normed_three, rstd_three = standardize(updated)
    trans_in = (normed_three * norm_params[4] + norm_params[5]).astype(jnp.bfloat16)
    pre_act = linear(trans_in, low_t1)
    hidden = jax.nn.silu(pre_act).astype(jnp.bfloat16)
    final = updated + linear(hidden, low_t2)
    final_low = final.astype(jnp.bfloat16)
    logits = linear(final_low, low_dist) + dist_bias
    log_total = jax.nn.logsumexp(logits, -1)
    onehot = (dist_bins[0][..., None] == jnp.arange(w_dist.shape[1])).astype(jnp.float32)
    loss_local = jnp.sum(pair_mask * (log_total - jnp.sum(logits * onehot, -1)))
    d_logits = (mask_cube * (jnp.exp(logits - log_total[..., None]) - onehot) / pair_total).astype(
        jnp.bfloat16
    )
    grad_dist = weight_grad(final_low, d_logits)
    grad_bias = jnp.sum(d_logits.astype(jnp.float32), (0, 1))
    d_final = transposed(d_logits, low_dist)
    d_trans = d_final.astype(jnp.bfloat16)
    grad_t2 = weight_grad(hidden, d_trans)
    d_hidden = transposed(d_trans, low_t2)
    sig_pre = jax.nn.sigmoid(pre_act)
    d_pre = (d_hidden * sig_pre * (1.0 + pre_act * (1.0 - sig_pre))).astype(jnp.bfloat16)
    grad_t1 = weight_grad(trans_in, d_pre)
    d_trans_in = transposed(d_pre, low_t1)
    d_updated = d_final + standard_back(d_trans_in * norm_params[4], normed_three, rstd_three)
    d_out = (d_updated * gate_sig).astype(jnp.bfloat16)
    d_out_gate = d_updated * out_proj * gate_sig * (1.0 - gate_sig)
    grad_out = weight_grad(tri_norm, d_out)
    d_tri_norm = transposed(d_out, low_out)
    d_triangle = standard_back(d_tri_norm * norm_params[2], normed_two, rstd_two).astype(
        jnp.bfloat16
    )
    d_rows = lax.all_gather(d_triangle, "col", axis=1, tiled=True)
    d_left = jnp.einsum("ijc,jkc->ikc", d_rows, strips, preferred_element_type=jnp.float32)
    piece = d_rows
    d_right = lax.psum_scatter(
        jnp.einsum("ijc,ikc->jkc", piece, left_vals, preferred_element_type=jnp.float32).astype(
            jnp.bfloat16
        ),
        "row",
        scatter_dimension=0,
        tiled=True,
    ).astype(jnp.float32)
    d_proj = jnp.concatenate(
        [
            d_left * mask_cube * left_sig,
            d_left * mask_cube * left_proj * left_sig * (1.0 - left_sig),
            d_right * mask_cube * right_sig,
            d_right * mask_cube * right_proj * right_sig * (1.0 - right_sig),
            d_out_gate,
        ],
        -1,
    ).astype(jnp.bfloat16)
    grad_in = weight_grad(pair_norm, d_proj)
    d_pair_norm = transposed(d_proj, low_in)
    grad_norms = jnp.stack(
        [
            jnp.sum(d_pair_norm * normed_one, (0, 1)),
            jnp.sum(d_pair_norm, (0, 1)),
            jnp.sum(d_tri_norm * normed_two, (0, 1)),
            jnp.sum(d_tri_norm, (0, 1)),
            jnp.sum(d_trans_in * normed_three, (0, 1)),
            jnp.sum(d_trans_in, (0, 1)),
        ]
    )
    summed = lax.psum(
        (grad_in, grad_out, grad_t1, grad_t2, grad_dist, grad_norms, grad_bias, loss_local),
        ("crop", "row", "col"),
    )
    grads = summed[:7]
    squares = jnp.zeros((), jnp.float32)
    for grad in grads:
        squares = squares + jnp.sum(grad * grad)
    grad_norm = jnp.sqrt(squares)
    scale = CLIP_NORM / jnp.maximum(grad_norm, CLIP_NORM)
    params = (w_in, w_out, w_t1, w_t2, w_dist, norm_params, dist_bias)
    firsts = (m_in, m_out, m_t1, m_t2, m_dist, m_norm, m_bias)
    seconds = (v_in, v_out, v_t1, v_t2, v_dist, v_norm, v_bias)
    rates = (LEARN_RATE, LEARN_RATE, LEARN_RATE, LEARN_RATE, LEARN_RATE, GAIN_RATE, GAIN_RATE)
    results = [
        adamw_update(
            params[index], firsts[index], seconds[index], grads[index], scale, rates[index]
        )
        for index in range(7)
    ]
    return (
        results[0][0],
        results[1][0],
        results[2][0],
        results[3][0],
        results[4][0],
        results[5][0],
        results[6][0],
        results[0][1],
        results[1][1],
        results[2][1],
        results[3][1],
        results[4][1],
        results[5][1],
        results[6][1],
        results[0][2],
        results[1][2],
        results[2][2],
        results[3][2],
        results[4][2],
        results[5][2],
        results[6][2],
        summed[7],
        pair_total,
        grad_norm,
    )


F32 = jnp.float32
BF16 = jnp.bfloat16
NT = (((1,), (1,)), ((), ()))
NN = (((1,), (0,)), ((), ()))
TN = (((0,), (0,)), ((), ()))
MICRO = 1e3
VMEM_LIMIT = 56 * 1024 * 1024


def dot(left, right, dims=NN):
    return lax.dot_general(left, right, dims, preferred_element_type=F32)


def column_stats(values):
    center = values - jnp.mean(values, 0, keepdims=True)
    rstd = lax.rsqrt(jnp.mean(center * center, 0, keepdims=True) + NORM_EPS)
    return center * rstd, rstd


def column_back(grad, normed, rstd):
    return rstd * (
        grad
        - jnp.mean(grad, 0, keepdims=True)
        - normed * jnp.mean(grad * normed, 0, keepdims=True)
    )


def widen(param, lanes):
    return jnp.concatenate([param] * (lanes // param.shape[1]), 1)


def spread_rows(scratch, block):
    scratch[...] = jnp.swapaxes(block, 0, 1).astype(scratch.dtype)


def take_rows(scratch, start, count):
    return jnp.concatenate([scratch[start + u] for u in range(count)], 1).astype(F32)


def put_rows(scratch, start, count, values):
    lanes = values.shape[1] // count
    for u in range(count):
        scratch[start + u] = values[:, u * lanes : (u + 1) * lanes].astype(scratch.dtype)


def gather_rows(scratch, out_ref):
    out_ref[...] = jnp.swapaxes(scratch[...], 0, 1)


def call(kernel, grid, scalars, ins, outs, scratch, flops, name, aliases=None):
    return pl.pallas_call(
        kernel,
        grid_spec=pltpu.PrefetchScalarGridSpec(
            num_scalar_prefetch=len(scalars),
            grid=grid,
            in_specs=[pl.BlockSpec(block, index) for _, block, index in ins],
            out_specs=[pl.BlockSpec(block, index) for _, _, block, index in outs],
            scratch_shapes=scratch,
        ),
        out_shape=[jax.ShapeDtypeStruct(shape, dtype) for shape, dtype, _, _ in outs],
        compiler_params=pltpu.CompilerParams(vmem_limit_bytes=VMEM_LIMIT),
        cost_estimate=pl.CostEstimate(flops=int(flops), bytes_accessed=1, transcendentals=0),
        name=name,
        input_output_aliases=aliases or {},
    )(*scalars, *[a for a, _, _ in ins])


def code_rows(code_s, start, count):
    return jnp.concatenate([code_s[pl.ds(start + u, 1), :] for u in range(count)], 1)


def present_rows(code_s, start, count):
    return jnp.where(code_rows(code_s, start, count) < 0.0, 0.0, 1.0)


ROWS = 16
PROJECT_GROUP = 8
INPUT_GROUP = 16


def prepare_weights(w_in, w_out, w_t1, w_t2, w_dist, norms, bias, outs):
    projT, ogT, outT, out_w, t1T, t1, t2T, t2, distT, dist, ln_ref, bias_ref = outs
    count, chans = projT.shape
    projT[...] = (0.5 * jnp.transpose(w_in[:, :count])).astype(BF16)
    ogT[...] = (0.5 * jnp.transpose(w_in[:, count:])).astype(BF16)
    for weight, plain, turned, plain_scale, turned_scale in (
        (w_out, out_w, outT, 1.0, 1.0),
        (w_t1, t1, t1T, 1.0, 0.5),
        (w_t2, t2, t2T, 0.5, 1.0),
        (w_dist, distT, dist, 1.0, 1.0),
    ):
        plain[...] = (plain_scale * weight[...]).astype(BF16)
        turned[...] = (turned_scale * jnp.transpose(weight[...])).astype(BF16)
    for index in range(6):
        ln_ref[index] = jnp.transpose(jnp.broadcast_to(norms[index : index + 1, :], (128, chans)))
    bias_ref[...] = jnp.transpose(jnp.broadcast_to(bias[...], (128, bias.shape[1])))


def project_kernel(acts_ref, code_ref, w_ref, ln_ref, a_ref, b_ref, acts_s, a_s, b_s, code_s):
    width = a_ref.shape[0]
    code_s[...] = code_ref[0].astype(F32)
    spread_rows(acts_s, acts_ref[...])

    def some(step, carry):
        start = step * PROJECT_GROUP
        values = take_rows(acts_s, start, PROJECT_GROUP)
        lanes = values.shape[1]
        normed, _ = column_stats(values)
        low = normed * widen(ln_ref[0], lanes) + widen(ln_ref[1], lanes)
        low = (low * present_rows(code_s, start, PROJECT_GROUP)).astype(BF16)
        proj = dot(w_ref[...], low)
        left = proj[:width] * (jnp.tanh(proj[width : 2 * width]) + 1.0)
        right = proj[2 * width : 3 * width] * (jnp.tanh(proj[3 * width :]) + 1.0)
        put_rows(a_s, start, PROJECT_GROUP, left)
        put_rows(b_s, start, PROJECT_GROUP, right)
        return carry

    lax.fori_loop(0, ROWS // PROJECT_GROUP, some, 0)
    gather_rows(a_s, a_ref)
    gather_rows(b_s, b_ref)


def fixed(*zeros):
    return lambda i, *_: zeros


def project(acts, w_proj, ln_wide):
    chans, rows, lanes = acts.shape[0] - 1, acts.shape[1], acts.shape[2]
    block = (chans, ROWS, lanes)
    mid = lambda i, *_: (0, i, 0)
    out = ((chans, rows, lanes), BF16, block, mid)
    staged = pltpu.VMEM((ROWS, chans, lanes), BF16)
    return call(
        project_kernel,
        (rows // ROWS,),
        [],
        [
            (acts, block, mid),
            (acts, (1, ROWS, lanes), lambda i, *_: (chans, i, 0)),
            (w_proj, w_proj.shape, fixed(0, 0)),
            (ln_wide, ln_wide.shape, fixed(0, 0, 0)),
        ],
        [out, out],
        [staged, staged, staged, pltpu.VMEM((ROWS, lanes), F32)],
        15 * MICRO,
        "project",
    )


CHANS = 16
TRIANGLE_CHANS = 32


def ordered(flag, own, other):
    part = own.shape[0] // 2
    waves = []
    for wave in range(2):
        mine, rest = own[wave * part : (wave + 1) * part], other[wave * part : (wave + 1) * part]
        waves += [jnp.where(flag, mine, rest), jnp.where(flag, rest, mine)]
    return jnp.concatenate(waves, 0)


def kept_first(ids, q):
    return ids[2] ^ ((ids[0] ^ q) // 2) ^ (ids[1] // 2) == 0


def triangle_kernel(q, ids, a0, a1, b0, b1, keep_ref, send_ref):
    first = kept_first(ids, q)
    part = b0.shape[1] // 2
    for chan in range(TRIANGLE_CHANS):
        rows = jnp.concatenate([a0[chan], a1[chan]], 0)
        x = dot(jnp.concatenate([b0[chan], b1[chan]], 0), rows, NT)
        one = jnp.concatenate([x[:part], x[2 * part : 3 * part]], 0)
        two = jnp.concatenate([x[part : 2 * part], x[3 * part :]], 0)
        keep_ref[chan] = jnp.where(first, one, two)
        send_ref[chan] = jnp.where(first, two, one).astype(BF16)


def triangle(q, ids, a, b):
    chans, half, lanes = a[0].shape
    lead = lambda i, *_: (i, 0, 0)
    block = (TRIANGLE_CHANS, half, lanes)
    out = (chans, half, 2 * half)
    return call(
        functools.partial(triangle_kernel, q),
        (chans // TRIANGLE_CHANS,),
        [ids],
        [(v, block, lead) for v in (*a, *b)],
        [(out, F32, (TRIANGLE_CHANS, half, 2 * half), lead), (out, BF16, (TRIANGLE_CHANS, half, 2 * half), lead)],
        [],
        14 * MICRO,
        "triangle",
    )


GROUP = 16


T1_ROW, T2_ROW, OUT_ROW, OG_ROW, DIST_ROW, NORM_ROW, BIAS_ROW, LOSS_ROW, SUM_ROWS = (
    0, 512, 1024, 1152, 1280, 1344, 1350, 1351, 1352,
)


def row_sums(values):
    return jnp.sum(jnp.transpose(values), 0, keepdims=True)


def pair_kernel(
    first_call, last_call,
    ids, x_keep, x_recv, acts_ref, code_ref, ln_ref, w_outT, w_out, w_ogT, w_t1T, w_t1,
    w_t2T, w_t2, w_distT, w_dist, bias_ref, *rest,
):
    prior = () if first_call else rest[:2]
    dx_ref, sums, wide, x_s, acts_s, dx_s, code_s = rest[len(prior) :]
    chans = acts_ref.shape[0]
    lanes = 128 * GROUP
    bins = w_distT.shape[0]
    hidden_width = w_t1T.shape[0]

    @pl.when(pl.program_id(0) == 0)
    def _():
        if first_call:
            sums[...] = jnp.zeros_like(sums)
            wide[...] = jnp.zeros_like(wide)
        else:
            sums[...] = prior[0][...]
            wide[...] = prior[1][...]

    spread_rows(x_s, x_keep[...] + x_recv[...].astype(F32))
    spread_rows(acts_s, acts_ref[...])
    code_s[...] = code_ref[0].astype(F32)
    param = [widen(ln_ref[index], lanes) for index in range(6)]
    bin_index = lax.broadcasted_iota(jnp.int32, (bins, lanes), 0).astype(F32)

    def fold(values):
        return sum(values[:, 128 * part : 128 * part + 128] for part in range(GROUP))

    def add(row, values):
        sums[row : row + values.shape[0]] += values

    def group(step, carry):
        first = step * GROUP
        x = take_rows(x_s, first, GROUP)
        acts = take_rows(acts_s, first, GROUP)
        code = code_rows(code_s, first, GROUP)
        normed_two, rstd_two = column_stats(x)
        tri = (normed_two * param[2] + param[3]).astype(BF16)
        out = dot(w_outT[...], tri)
        normed_one, _ = column_stats(acts)
        low = (normed_one * param[0] + param[1]).astype(BF16)
        gate = 0.5 * jnp.tanh(dot(w_ogT[...], low)) + 0.5
        z1 = acts + gate * out
        normed_three, rstd_three = column_stats(z1)
        trans = (normed_three * param[4] + param[5]).astype(BF16)
        pre = dot(w_t1T[...], trans)
        tanh = jnp.tanh(pre)
        bent = pre * tanh
        hidden = (pre + bent).astype(BF16)
        slope = (1.0 + tanh) * (1.0 + (pre - bent))
        final = (z1 + dot(w_t2T[...], hidden)).astype(BF16)
        logits = dot(w_distT[...], final) + widen(bias_ref[...], lanes)
        top = jnp.max(logits, 0, keepdims=True)
        powers = jnp.exp(logits - top)
        total = jnp.sum(powers, 0, keepdims=True)
        present = jnp.where(code < 0.0, 0.0, 1.0)
        hot = bin_index == code
        picked = jnp.sum(jnp.where(hot, logits, 0.0), 0, keepdims=True)
        sums[LOSS_ROW : LOSS_ROW + 1] += fold(present * (jnp.log(total) + top) - picked)
        d_logits = (powers * (present / total) - jnp.where(hot, 1.0, 0.0)).astype(BF16)
        add(DIST_ROW, dot(d_logits, final, NT))
        wide[5, :bins] += fold(d_logits.astype(F32))
        d_final = dot(w_dist[...], d_logits)
        d_trans = d_final.astype(BF16)
        add(T2_ROW, dot(hidden, d_trans, NT))
        d_pre = (dot(w_t2[...], d_trans) * slope).astype(BF16)
        add(T1_ROW, dot(d_pre, trans, NT))
        d_tn = dot(w_t1[...], d_pre)
        wide[2] += fold(d_tn * normed_three)
        wide[3] += fold(d_tn)
        d_z1 = d_final + column_back(d_tn * param[4], normed_three, rstd_three)
        d_gated = d_z1 * gate
        d_out = d_gated.astype(BF16)
        d_og = (d_gated * out * (1.0 - gate)).astype(BF16)
        add(OUT_ROW, dot(d_out, tri, NT))
        g_og = dot(d_og, jnp.concatenate([low, normed_one.astype(BF16)], 0), NT)
        add(OG_ROW, g_og[:, :chans])
        wide[6] += g_og[:, chans:]
        wide[4] += fold(d_og.astype(F32))
        d_xn = dot(w_out[...], d_out)
        wide[0] += fold(d_xn * normed_two)
        wide[1] += fold(d_xn)
        d_x = column_back(d_xn * param[2], normed_two, rstd_two)
        put_rows(dx_s, first, GROUP, d_x)
        return carry

    lax.fori_loop(0, ROWS // GROUP, group, 0)
    gather_rows(dx_s, dx_ref)

    if last_call:

        @pl.when(pl.program_id(0) == pl.num_programs(0) - 1)
        def _():
            gate_w = 2.0 * w_ogT[...].astype(F32)
            for index in range(4):
                add(NORM_ROW + index, row_sums(wide[index]))
            total = jnp.sum(wide[4], 1, keepdims=True)
            add(NORM_ROW + 4, jnp.sum(gate_w * wide[6], 0, keepdims=True))
            add(NORM_ROW + 5, jnp.sum(gate_w * total, 0, keepdims=True))
            add(BIAS_ROW, row_sums(wide[5]))


def pair_block(q, ids, x_keep, x_recv, acts_kj, ln_wide, weights, bias, prior, last_call):
    chans, rows, lanes = x_keep.shape
    block = (chans, ROWS, lanes)
    mid = lambda i, *_: (0, i, 0)

    def where(i, ids):
        owner = ids[0] ^ q
        return 8 * ((i % 2) ^ (owner % 2) ^ (ids[1] % 2)) + 2 * owner + i // 2

    full = [(w, w.shape, fixed(*([0] * w.ndim))) for w in (ln_wide, *weights, bias, *prior)]
    shapes = [(SUM_ROWS, 128), (7, 128, 128)]
    return call(
        functools.partial(pair_kernel, not prior, last_call),
        (rows // ROWS,),
        [ids],
        [
            (x_keep, block, mid),
            (x_recv, block, mid),
            (acts_kj, block, lambda i, ids: (0, where(i, ids), 0)),
            (acts_kj, (1, ROWS, lanes), lambda i, ids: (chans, where(i, ids), 0)),
        ]
        + full,
        [((chans, rows, lanes), BF16, block, mid)]
        + [(s, F32, s, fixed(*([0] * len(s)))) for s in shapes],
        [pltpu.VMEM((ROWS, chans, lanes), t) for t in (F32, BF16, BF16)] + [pltpu.VMEM((ROWS, lanes), F32)],
        35 * MICRO,
        "pair",
    )


def right_back_kernel(ids, *refs):
    owns, others, firsts, seconds = refs[:4], refs[4:8], refs[8:12], refs[12:16]
    out0, out1 = refs[16:]
    half = out0.shape[1]
    own_first = kept_first(ids, 0)
    for chan in range(CHANS):
        grads = jnp.concatenate(
            [ordered(own_first, owns[q][chan], others[q][chan]) for q in range(4)], 1
        )
        values = jnp.concatenate([v[q][chan] for q in range(4) for v in (firsts, seconds)], 0)
        total = dot(grads, values).astype(BF16)
        out0[chan] = total[:half]
        out1[chan] = total[half:]


def right_back(ids, owns, others, firsts, seconds):
    chans, half, lanes = firsts[0].shape
    lead = lambda i, *_: (i, 0, 0)
    out = ((chans, half, lanes), BF16, (CHANS, half, lanes), lead)
    return call(
        right_back_kernel,
        (chans // CHANS,),
        [ids],
        [(v, (CHANS, half, 2 * half), lead) for v in (*owns, *others)]
        + [(v, (CHANS, half, lanes), lead) for v in (*firsts, *seconds)],
        [out, out],
        [],
        25 * MICRO,
        "right_back",
    )


def turn_kernel(first, second, out_ref):
    for chan in range(first.shape[0]):
        out_ref[chan] = jnp.transpose(jnp.concatenate([first[chan], second[chan]], 0))


def turn(first, second):
    chans, half, lanes = first.shape
    lead = lambda i, *_: (i, 0, 0)
    count = next(n for n in (43, 16, 8, 4, 2, 1) if chans % n == 0)
    block = (count, half, lanes)
    return call(
        turn_kernel,
        (chans // count,),
        [],
        [(first, block, lead), (second, block, lead)],
        [((chans, lanes, 2 * half), BF16, (count, lanes, 2 * half), lead)],
        [],
        12 * MICRO,
        "turn",
    )[0]


def left_back_kernel(ids, *refs):
    owns, others, firsts, seconds = refs[:4], refs[4:8], refs[8:12], refs[12:16]
    out0, out1 = refs[16:]
    half = out0.shape[1]
    for chan in range(CHANS):
        total = None
        for pair in range(2):
            own_first = kept_first(ids, 2 * pair)
            grads, values = [], []
            for q in (2 * pair, 2 * pair + 1):
                grads.append(ordered(own_first, owns[q][chan], others[q][chan]))
                values += [firsts[q][chan], seconds[q][chan]]
            term = dot(jnp.concatenate(grads, 0), jnp.concatenate(values, 0), TN)
            total = term if total is None else total + term
        total = total.astype(BF16)
        out0[chan] = total[:half]
        out1[chan] = total[half:]


def left_back(ids, owns, others, firsts, seconds):
    chans, half, lanes = firsts[0].shape
    lead = lambda i, *_: (i, 0, 0)
    out = ((chans, half, lanes), BF16, (CHANS, half, lanes), lead)
    return call(
        left_back_kernel,
        (chans // CHANS,),
        [ids],
        [(v, (CHANS, half, 2 * half), lead) for v in (*owns, *others)]
        + [(v, (CHANS, half, lanes), lead) for v in (*firsts, *seconds)],
        [out, out],
        [],
        25 * MICRO,
        "left_back",
    )


SIDE_ROWS = 272


def affine_grad(normed_grad, total, ln_ref):
    gain, shift = jnp.transpose(ln_ref[0])[:1], jnp.transpose(ln_ref[1])[:1]
    return normed_grad * gain + total * shift


def input_back_kernel(count, first_call, last_call, acts_ref, code_ref, w_ref, ln_ref, *rest):
    grads, rest = rest[:count], rest[count:]
    prior = () if first_call else rest[:3]
    out_ref, g_ref, sum_ref, acts_s, grad_s, code_s = rest[len(prior) :]
    width = grads[0].shape[0]
    chans = acts_ref.shape[0]

    @pl.when(pl.program_id(0) == 0)
    def _():
        if first_call:
            out_ref[...] = jnp.zeros_like(out_ref)
            g_ref[...] = jnp.zeros_like(g_ref)
            sum_ref[...] = jnp.zeros_like(sum_ref)
        else:
            out_ref[...] = prior[0][...]
            g_ref[...] = prior[1][...]
            sum_ref[...] = prior[2][...]

    code_s[...] = code_ref[0].astype(F32)
    spread_rows(acts_s, acts_ref[...])
    spread_rows(grad_s, grads[0][...])

    def some(step, carry):
        start = step * INPUT_GROUP
        values = take_rows(acts_s, start, INPUT_GROUP)
        lanes = values.shape[1]
        normed, _ = column_stats(values)
        low = (normed * widen(ln_ref[0], lanes) + widen(ln_ref[1], lanes)).astype(BF16)
        proj = dot(w_ref[...], low)
        tanh = jnp.tanh(proj[width:])
        d_half = take_rows(grad_s, start, INPUT_GROUP) * (0.5 * present_rows(code_s, start, INPUT_GROUP))
        d_tanh = d_half * tanh
        d_value = d_half + d_tanh
        d_gate = proj[:width] * (d_half - d_tanh * tanh)
        d_proj = jnp.concatenate([d_value.astype(BF16), d_gate.astype(BF16)], 0)
        g_ref[...] += dot(d_proj, normed.astype(BF16), NT)
        for first, part in ((0, d_value), (width, d_gate)):
            sum_ref[first : first + width] += sum(
                part[:, 128 * u : 128 * u + 128] for u in range(lanes // 128)
            )
        return carry

    lax.fori_loop(0, ROWS // INPUT_GROUP, some, 0)

    if last_call:

        @pl.when(pl.program_id(0) == pl.num_programs(0) - 1)
        def _():
            part = 2.0 * w_ref[...].astype(F32)
            total = jnp.sum(sum_ref[...], 1, keepdims=True)
            gain = jnp.sum(part * g_ref[...], 0, keepdims=True)
            shift = jnp.sum(part * total, 0, keepdims=True)
            out_ref[: 2 * width] = affine_grad(g_ref[...], total, ln_ref)
            out_ref[2 * width : 2 * width + 1] = gain
            out_ref[2 * width + 1 : 2 * width + 2] = shift


def input_back(acts, part, w_proj, ln_wide, grads, prior, last_call):
    chans, rows, lanes = acts.shape[0] - 1, acts.shape[1], acts.shape[2]
    block = (chans, ROWS, lanes)
    mid = lambda i, *_: (0, i, 0)
    depth = w_proj.shape[0] // 2
    shapes = [(SIDE_ROWS, chans), (depth, chans), (depth, 128)]
    return call(
        functools.partial(input_back_kernel, len(grads), not prior, last_call),
        (rows // ROWS,),
        [],
        [
            (acts, block, mid),
            (acts, (1, ROWS, lanes), lambda i, *_: (chans, i, 0)),
            (w_proj, (depth, chans), fixed(part, 0)),
            (ln_wide, ln_wide.shape, fixed(0, 0, 0)),
        ]
        + [(v, block, mid) for v in grads]
        + [(v, v.shape, fixed(0, 0)) for v in prior],
        [(s, F32, s, fixed(0, 0)) for s in shapes],
        [
            pltpu.VMEM((ROWS, chans, lanes), BF16),
            pltpu.VMEM((ROWS, chans, lanes), BF16),
            pltpu.VMEM((ROWS, lanes), F32),
        ],
        16 * MICRO,
        "input_back",
    )


def reduce_kernel(pair_ref, left_ref, right_ref, out_ref, full_s, core_s, crop_s, row_s, send, recv):
    side, spot, level = lax.axis_index("col"), lax.axis_index("crop"), lax.axis_index("row")
    mesh_id = pl.DeviceIdType.MESH
    sibling = {"col": 1 - side}
    crops = [{"crop": lax.rem(spot + n, 4)} for n in range(1, 4)]
    levels = [{"row": lax.rem(level + n, 4)} for n in range(1, 4)]
    barrier = pltpu.get_barrier_semaphore()
    for device in [sibling] + crops + levels:
        pl.semaphore_signal(barrier, inc=1, device_id=device, device_id_type=mesh_id)
    pl.semaphore_wait(barrier, 7)

    def copy(source, target, index, device):
        return pltpu.make_async_remote_copy(
            src_ref=source, dst_ref=target, send_sem=send.at[index], recv_sem=recv.at[index],
            device_id=device, device_id_type=mesh_id,
        )

    def run(copies):
        for one in copies:
            one.start()
        for one in copies:
            one.wait()

    half = full_s.shape[0] // 2
    quarter, share = half // 4, half // 16
    row = 0
    for ref in (pair_ref, left_ref, right_ref):
        full_s[row : row + ref.shape[0]] = ref[...]
        row += ref.shape[0]
    full_s[row:] = jnp.zeros((full_s.shape[0] - row, full_s.shape[1]), F32)
    base = pl.multiple_of(side * half, 8)
    run([copy(full_s.at[pl.ds(pl.multiple_of((1 - side) * half, 8), half)], core_s, 0, sibling)])
    full_s[pl.ds(base, half)] += core_s[...]
    def part(number):
        return pl.ds(pl.multiple_of(base + number * quarter, 8), quarter)

    run([copy(full_s.at[part(lax.rem(spot + n, 4))], crop_s.at[spot], n, crops[n - 1]) for n in range(1, 4)])
    mine = part(spot)
    crop_s[spot] = full_s[mine]
    full_s[mine] = crop_s[0] + crop_s[1] + crop_s[2] + crop_s[3]
    def slot(number):
        return pl.ds(pl.multiple_of(base + spot * quarter + number * share, 8), share)

    run([copy(full_s.at[slot(lax.rem(level + n, 4))], row_s.at[level], 3 + n, levels[n - 1]) for n in range(1, 4)])
    own = slot(level)
    row_s[level] = full_s[own]
    out_ref[own] = row_s[0] + row_s[1] + row_s[2] + row_s[3]
    run([copy(out_ref.at[own], out_ref.at[own], 6 + n, levels[n - 1]) for n in range(1, 4)])
    run([copy(out_ref.at[mine], out_ref.at[mine], 9 + n, crops[n - 1]) for n in range(1, 4)])
    run([copy(out_ref.at[pl.ds(base, half)], out_ref.at[pl.ds(base, half)], 13, sibling)])


ALL_ROWS = 2048


def reduce_all(*parts):
    lanes = parts[0].shape[1]
    return pl.pallas_call(
        reduce_kernel,
        out_shape=jax.ShapeDtypeStruct((ALL_ROWS, lanes), F32),
        scratch_shapes=[
            pltpu.VMEM((ALL_ROWS, lanes), F32),
            pltpu.VMEM((ALL_ROWS // 2, lanes), F32),
            pltpu.VMEM((4, ALL_ROWS // 8, lanes), F32),
            pltpu.VMEM((4, ALL_ROWS // 32, lanes), F32),
            pltpu.SemaphoreType.DMA((14,)),
            pltpu.SemaphoreType.DMA((14,)),
        ],
        compiler_params=pltpu.CompilerParams(
            collective_id=1, has_side_effects=True, vmem_limit_bytes=VMEM_LIMIT
        ),
        name="reduce_all",
    )(*parts)


def flip(a, b):
    return 2 * lax.rem(a // 2 + b // 2, 2) + lax.rem(a + b, 2)


def swap_bits(a):
    return 2 * lax.rem(a, 2) + a // 2


def spread_kernel(
    acts_ref, code_ref, w_in, w_out, w_t1, w_t2, w_dist, norms, bias,
    wave0_ref, wave1_ref, x_ref, y_ref, a_ref, b_ref,
    projT, ogT, outT, out_w, t1T, t1, t2T, t2, distT, dist, ln_ref, bias_ref,
    mid, taken, made, fetched, plane_send, plane_recv, share_send, share_recv, level_send, level_recv, local,
    wave_v, a_v, b_v, acts_s, a_s, b_s, code_s,
):
    spot, level = lax.axis_index("crop"), lax.axis_index("row")
    chans = mid.shape[2]
    early, middle = chans // 4, 5 * chans // 8
    cuts = [[(0, early), (early, middle - early), (middle, chans - middle)], [(0, chans)]]
    waves = (wave0_ref, wave1_ref)
    mesh_id = pl.DeviceIdType.MESH

    def block_rows(wave, distance):
        return pl.ds(pl.multiple_of(32 * flip(spot, distance) + 16 * wave, 16), 16)

    def fetch_block(wave, distance):
        return pltpu.make_async_copy(
            acts_ref.at[block_rows(wave, distance)], taken.at[wave, distance], fetched.at[4 * wave + distance]
        )

    def make_block(wave, distance):
        fetch_block(wave, distance).wait()

        def turn_row(row, carry):
            acts_s[row] = jnp.transpose(taken[wave, distance, row])
            return carry

        lax.fori_loop(0, ROWS, turn_row, 0, unroll=8)
        made[wave, distance, : chans - 1] = jnp.swapaxes(acts_s[...], 0, 1)
        made[wave, distance, chans - 1] = code_ref[block_rows(wave, distance), :]

    for wave in range(2):
        for distance in range(4):
            fetch_block(wave, distance).start()
    barrier = pltpu.get_barrier_semaphore()
    for n in range(1, 4):
        for device in ({"crop": lax.rem(spot + n, 4)}, {"row": lax.rem(level + n, 4)}):
            pl.semaphore_signal(barrier, inc=1, device_id=device, device_id_type=mesh_id)
    pl.semaphore_wait(barrier, 6)

    def plane_copy(wave, cut, distance):
        first, count = cuts[wave][cut]
        target = flip(spot, distance)
        source = made.at[wave, distance, pl.ds(first, count)]
        landing = mid.at[wave, distance, pl.ds(first, count)]
        index = 12 * wave + 4 * cut + distance
        if distance == 0:
            return pltpu.make_async_copy(source, landing, plane_recv.at[index])
        return pltpu.make_async_remote_copy(
            src_ref=source, dst_ref=landing, send_sem=plane_send.at[index], recv_sem=plane_recv.at[index],
            device_id={"crop": target}, device_id_type=mesh_id,
        )

    def landed(wave, cut, label):
        first, count = cuts[wave][cut]
        return waves[wave].at[pl.ds(first, count), pl.ds(16 * label, 16)]

    def level_copy(wave, cut, label, distance):
        first, count = cuts[wave][cut]
        source = mid.at[wave, distance, pl.ds(first, count)]
        target = swap_bits(flip(spot, distance))
        index = 12 * wave + 4 * cut + label
        remote = pltpu.make_async_remote_copy(
            src_ref=source, dst_ref=landed(wave, cut, label),
            send_sem=level_send.at[index], recv_sem=level_recv.at[index],
            device_id={"row": target}, device_id_type=mesh_id,
        )
        return target, remote, pltpu.make_async_copy(source, landed(wave, cut, label), local.at[3 * wave + cut])

    def each_level(action, wave, cut):
        for label in range(4):
            for distance in range(4):

                @pl.when(flip(level, label) == distance)
                def _(label=label, distance=distance):
                    action(wave, cut, label, distance)

    def shares(cut, label):
        first, count = cuts[0][cut]
        index = 8 * cut + 2 * label
        return [
            pltpu.make_async_remote_copy(
                src_ref=landed(0, cut, label),
                dst_ref=ref.at[pl.ds(first, count), pl.ds(16 * label, 16)],
                send_sem=share_send.at[index + n], recv_sem=share_recv.at[index + n],
                device_id={"crop": flip(spot, 1 + n)}, device_id_type=mesh_id,
            )
            for n, ref in enumerate((x_ref, y_ref))
        ]

    plane = [
        [[plane_copy(wave, cut, distance) for distance in range(4)] for cut in range(len(cuts[wave]))]
        for wave in range(2)
    ]
    for distance in (1, 3, 2, 0):
        make_block(0, distance)
        plane[0][0][distance].start()
    for copies in plane[0][1:]:
        for one in copies:
            one.start()
    for distance in (1, 3, 2, 0):
        make_block(1, distance)
        plane[1][0][distance].start()

    def begin(wave, cut, label, distance):
        one = plane[wave][cut][distance]
        one.wait() if distance == 0 else one.wait_recv()
        target, remote, stay = level_copy(wave, cut, label, distance)

        @pl.when(target == level)
        def _():
            stay.start()

        @pl.when(target != level)
        def _():
            remote.start()

    def arrive(wave, cut, label, distance):
        target, remote, stay = level_copy(wave, cut, label, distance)

        @pl.when(target == level)
        def _():
            stay.wait()

        @pl.when(target != level)
        def _():
            remote.wait_recv()
            remote.wait_send()

    def pass_on(cut):
        each_level(arrive, 0, cut)
        for label in range(4):
            for one in shares(cut, label):
                one.start()

    each_level(begin, 0, 0)
    prepare_weights(
        w_in, w_out, w_t1, w_t2, w_dist, norms, bias,
        (projT, ogT, outT, out_w, t1T, t1, t2T, t2, distT, dist, ln_ref, bias_ref),
    )
    each_level(begin, 0, 1)
    each_level(begin, 0, 2)
    each_level(begin, 1, 0)
    for cut in range(3):
        pass_on(cut)
    fetch = pltpu.make_async_copy(wave0_ref, wave_v, local.at[4])
    fetch.start()
    fetch.wait()
    width = a_v.shape[0]

    def project_rows(step, carry):
        rows = pl.ds(pl.multiple_of(step * ROWS, ROWS), ROWS)
        project_kernel(
            wave_v.at[pl.ds(0, width), rows], wave_v.at[pl.ds(width, 1), rows], projT, ln_ref,
            a_v.at[:, rows], b_v.at[:, rows], acts_s, a_s, b_s, code_s,
        )
        return carry

    lax.fori_loop(0, wave_v.shape[1] // ROWS, project_rows, 0)
    results = [
        pltpu.make_async_copy(a_v, a_ref, local.at[5]), pltpu.make_async_copy(b_v, b_ref, local.at[6])
    ]
    for one in results:
        one.start()
    for copies in plane[0] + plane[1]:
        for one in copies[1:]:
            one.wait_send()
    for cut in range(3):
        for label in range(4):
            for one in shares(cut, label):
                one.wait()
    for one in results:
        one.wait()
    each_level(arrive, 1, 0)


def spread(acts, code, w_in, w_out, w_t1, w_t2, w_dist, norms, bias):
    rows, lanes, width = acts.shape
    chans, half = width + 1, rows // 2
    anywhere = pl.BlockSpec(memory_space=pl.ANY)
    whole = pl.BlockSpec(memory_space=pltpu.VMEM)
    staged = pltpu.VMEM((ROWS, width, lanes), BF16)
    shapes = [(4 * width, width), (width, width)]
    for weight in (w_out, w_t1, w_t2, w_dist):
        shapes += [(weight.shape[1], weight.shape[0]), weight.shape]
    shapes = [jax.ShapeDtypeStruct(shape, BF16) for shape in shapes]
    shapes += [jax.ShapeDtypeStruct((6, width, 128), F32), jax.ShapeDtypeStruct((bias.shape[0], 128), F32)]
    return pl.pallas_call(
        spread_kernel,
        in_specs=[anywhere] + [whole] * 8,
        out_specs=[anywhere] * 6 + [whole] * len(shapes),
        out_shape=[jax.ShapeDtypeStruct((chans, half, lanes), BF16)] * 4
        + [jax.ShapeDtypeStruct((width, half, lanes), BF16)] * 2
        + shapes,
        scratch_shapes=[pltpu.VMEM((2, 4, chans, ROWS, lanes), BF16)]
        + [pltpu.VMEM((2, 4, ROWS, lanes, width), BF16)]
        + [pltpu.VMEM((2, 4, chans, ROWS, lanes), BF16)]
        + [pltpu.SemaphoreType.DMA((8,))]
        + [pltpu.SemaphoreType.DMA((16,)) for _ in range(2)]
        + [pltpu.SemaphoreType.DMA((24,)) for _ in range(2)]
        + [pltpu.SemaphoreType.DMA((16,)) for _ in range(2)]
        + [pltpu.SemaphoreType.DMA((7,))]
        + [pltpu.VMEM((chans, half, lanes), BF16)]
        + [pltpu.VMEM((width, half, lanes), BF16)] * 2
        + [staged] * 3
        + [pltpu.VMEM((ROWS, lanes), F32)],
        compiler_params=pltpu.CompilerParams(
            collective_id=2, has_side_effects=True, vmem_limit_bytes=VMEM_LIMIT
        ),
        name="spread",
    )(acts, code, w_in, w_out, w_t1, w_t2, w_dist.T, norms, bias.reshape(1, -1))


def update_kernel(early_ref, *refs):
    ins, outs = refs[:21], refs[21:]
    left_ref = early_ref.at[pl.ds(SUM_ROWS, SIDE_ROWS)]
    right_ref = early_ref.at[pl.ds(SUM_ROWS + SIDE_ROWS, SIDE_ROWS)]
    loss_ref, total_ref, norm_ref = outs[21:]
    total = early_ref[LOSS_ROW - 1, 127]
    inverse = 1.0 / total
    half = SIDE_ROWS - 16
    grads = [
        jnp.concatenate(
            [
                jnp.transpose(left_ref[:half]),
                jnp.transpose(right_ref[:half]),
                jnp.transpose(early_ref[OG_ROW : OG_ROW + 128]),
            ],
            1,
        ),
        jnp.transpose(early_ref[OUT_ROW : OUT_ROW + 128]),
        jnp.transpose(early_ref[T1_ROW : T1_ROW + 512]),
        early_ref[T2_ROW : T2_ROW + 512],
        early_ref[DIST_ROW : DIST_ROW + 64],
        jnp.concatenate(
            [
                left_ref[half : half + 2] + right_ref[half : half + 2] + early_ref[NORM_ROW + 4 : NORM_ROW + 6],
                early_ref[NORM_ROW : NORM_ROW + 4],
            ],
            0,
        ),
        early_ref[BIAS_ROW : BIAS_ROW + 1, :64],
    ]
    grads = [grad * inverse for grad in grads]
    squares = sum(jnp.sum(grad * grad, keepdims=True).reshape(1, 1) for grad in grads)
    grad_norm = jnp.sqrt(squares)
    scale = CLIP_NORM / jnp.maximum(grad_norm, CLIP_NORM)
    rates = (LEARN_RATE,) * 5 + (GAIN_RATE,) * 2
    for index in range(7):
        new = adamw_update(
            *[ins[7 * part + index][...].reshape(grads[index].shape) for part in range(3)],
            grads[index], scale, rates[index],
        )
        for part in range(3):
            outs[7 * part + index][...] = new[part].reshape(outs[7 * part + index].shape)
    norm_ref[...] = grad_norm
    loss_ref[...] = jnp.sum(early_ref[LOSS_ROW : LOSS_ROW + 1], keepdims=True).reshape(1, 1)
    total_ref[...] = jnp.full((1, 1), total, F32)


def update(early, params, firsts, seconds):
    flat = [v.T if index % 7 == 4 else v for index, v in enumerate((*params, *firsts, *seconds))]
    shapes = [v.shape for v in flat] + [(1, 1)] * 3
    outs = pl.pallas_call(
        update_kernel,
        out_shape=[jax.ShapeDtypeStruct(s, F32) for s in shapes],
        compiler_params=pltpu.CompilerParams(vmem_limit_bytes=VMEM_LIMIT),
        name="update",
    )(early, *flat)
    outs = [v.T if index in (4, 11, 18) else v for index, v in enumerate(outs)]
    return (*outs[:21], *[v[0, 0] for v in outs[21:]])


def after(value, *earlier):
    return lax.optimization_barrier((value, *earlier))[0]


def on_device_planes(
    pair_acts, residue_mask, dist_bins, w_in, w_out, w_t1, w_t2, w_dist, norm_params, dist_bias, *moments
):
    firsts, seconds = moments[:7], moments[7:]
    spot = lax.axis_index("crop")
    level = lax.axis_index("row")
    side = lax.axis_index("col")
    rows, cols, chans = pair_acts.shape[1:]
    width = w_out.shape[0]
    sub = rows // 4
    plane_of = (0, 2, 1, 3)
    crop = (level % 2) * 2 + level // 2

    def over_x(v):
        return lax.ppermute(v, "crop", [(g, g ^ 1) for g in range(4)])

    def over_y(v):
        return lax.ppermute(v, "crop", [(g, g ^ 2) for g in range(4)])

    def over_both(v):
        return lax.ppermute(v, "crop", [(g, g ^ 3) for g in range(4)])

    def over_core(v):
        return lax.ppermute(v, "col", [(0, 1), (1, 0)])

    own_mask = residue_mask[0]
    row_own = lax.dynamic_slice_in_dim(own_mask, rows * level, rows)
    col_own = lax.dynamic_slice_in_dim(own_mask, cols * side, cols)
    code_own = jnp.where((row_own[:, None] * col_own[None, :]) > 0, dist_bins[0], -1).astype(BF16)

    wave0, wave1, wave0_x, wave0_y, left_own, right_own, proj_w, *weights, ln_wide, bias_wide = spread(
        pair_acts[0], code_own, w_in, w_out, w_t1, w_t2, w_dist, norm_params, dist_bias
    )
    og_T, out_T, out_w, t1_T, t1_w, t2_T, t2_w, dist_T, dist_w = weights
    weights = (out_T, out_w, og_T, t1_T, t1_w, t2_T, t2_w, dist_T, dist_w)

    count = jnp.sum(own_mask).astype(F32)
    share_count = lax.axis_size("row") * lax.axis_size("col")
    acts, left, right = {}, {}, {}

    def share(q, source, shift, half):
        acts[q, half] = shift(acts[source, half])

    def values(q, half, *earlier):
        left[q, half], right[q, half] = project(after(acts[q, half], *earlier), proj_w, ln_wide)
        return right[q, half]

    acts[0, 0], acts[0, 1], acts[1, 0], acts[2, 0] = wave0, wave1, wave0_x, wave0_y
    share(1, 0, over_x, 1)
    share(2, 0, over_y, 1)
    left[0, 0], right[0, 0] = left_own, right_own
    done = values(0, 1)

    ids = jnp.stack([spot, crop, side]).astype(jnp.int32)
    keeps, recvs, dx_own, dx_other, seen, seen_other = {}, {}, {}, {}, {}, {}
    sums = []

    def forward(q, *earlier):
        keeps[q], send = triangle(
            q, after(ids, *earlier), [left[0, h] for h in range(2)], [right[q, h] for h in range(2)]
        )
        recvs[q] = over_core(send)
        return send

    def middle(q, *earlier):
        dx_own[q], *sums[:] = pair_block(
            q, after(ids, *earlier), keeps[q], recvs[q], acts_kj, ln_wide, weights, bias_wide, list(sums), q == 3
        )
        dx_other[q] = over_core(dx_own[q])
        seen[q] = (lambda v: v, over_x, over_y, over_both)[q](dx_own[q])
        seen_other[q] = over_core(seen[q]) if q in (1, 2) else dx_other[q]
        return dx_own[q]

    done = forward(0, done)
    acts_kj = turn(after(acts[0, 0], done), acts[0, 1])
    done = values(1, 0, acts_kj)
    done = values(2, 0, done)
    done = middle(0, done)
    acts[1, 1], acts[2, 1] = after(acts[1, 1], done), after(acts[2, 1], done)
    acts[3, 0] = over_y(after(acts[1, 0], done))
    acts[3, 1] = over_x(acts[2, 1])
    done = values(1, 1, done)
    done = forward(1, done)
    done = values(2, 1, done)
    done = forward(2, done)
    done = middle(1, done)
    done = middle(2, done)
    done = values(3, 0, done)
    done = values(3, 1, done)
    done = forward(3, done)
    done = middle(3, done, seen[1], seen[2])
    d_left = left_back(
        after(ids, done, seen_other[1]),
        [dx_own[q] for q in range(4)],
        [dx_other[q] for q in range(4)],
        [right[q, 0] for q in range(4)],
        [right[q, 1] for q in range(4)],
    )
    pair_sums = sums[0].at[LOSS_ROW - 1, 127].set(count * count / share_count)
    left_sum, right_sum = [], []
    for h in range(2):
        left_sum = input_back(acts[0, h], 0, proj_w, ln_wide, [d_left[h]], left_sum, h == 1)
        if h == 0:
            seen_other[3] = over_core(after(seen[3], left_sum[0]))
    d_right = right_back(
        after(ids, left_sum[0], seen_other[2]),
        [seen[q] for q in range(4)],
        [seen_other[q] for q in range(4)],
        [left[q, 0] for q in range(4)],
        [left[q, 1] for q in range(4)],
    )
    for h in range(2):
        right_sum = input_back(acts[0, h], 1, proj_w, ln_wide, [d_right[h]], right_sum, h == 1)
    params = (w_in, w_out, w_t1, w_t2, w_dist, norm_params, dist_bias)
    return update(reduce_all(pair_sums, left_sum[0], right_sum[0]), params, firsts, seconds)


def solution(mesh):
    planes = mesh.shape["crop"] == 4 and mesh.shape["row"] == 4 and mesh.shape["col"] == 2
    body = on_device_planes if planes else on_device_general
    in_specs = (
        P("crop", "row", "col", None),
        P("crop", None),
        P("crop", "row", "col"),
    ) + (P(),) * 21
    return jax.shard_map(
        body, mesh=mesh, in_specs=in_specs, out_specs=(P(),) * 24, check_vma=False
    )
```

```python
import functools

import jax
import jax.numpy as jnp
from jax import lax
from jax.experimental import pallas as pl
from jax.experimental.pallas import tpu as pltpu
from jax.sharding import PartitionSpec as P

STEP = 10


NORM_EPS = 1e-05
CLIP_NORM = 0.02
LEARN_RATE = 0.03
GAIN_RATE = 0.3
BETA_ONE = 0.9
BETA_TWO = 0.999
ADAM_EPS = 1e-08
WEIGHT_DECAY = 0.01


def standardize(values):
    center = values - jnp.mean(values, -1, keepdims=True)
    rstd = lax.rsqrt(jnp.mean(center * center, -1, keepdims=True) + NORM_EPS)
    return (center * rstd, rstd)


def standard_back(grad, normed, rstd):
    return rstd * (
        grad
        - jnp.mean(grad, -1, keepdims=True)
        - normed * jnp.mean(grad * normed, -1, keepdims=True)
    )


def linear(values, weight):
    return jnp.einsum("ijc,cd->ijd", values, weight, preferred_element_type=jnp.float32)


def weight_grad(values, grad):
    return jnp.einsum("ijc,ijd->cd", values, grad, preferred_element_type=jnp.float32)


def transposed(grad, weight):
    return jnp.einsum("ijd,cd->ijc", grad, weight, preferred_element_type=jnp.float32)


def adamw_update(weight, first, second, grad, scale, rate):
    clipped = grad * scale
    first_new = BETA_ONE * first + (1.0 - BETA_ONE) * clipped
    second_new = BETA_TWO * second + (1.0 - BETA_TWO) * clipped * clipped
    first_hat = first_new / (1.0 - BETA_ONE**STEP)
    second_hat = second_new / (1.0 - BETA_TWO**STEP)
    stepped = weight - rate * (
        first_hat / (jnp.sqrt(second_hat) + ADAM_EPS) + WEIGHT_DECAY * weight
    )
    return (stepped, first_new, second_new)


def on_device_general(
    pair_acts,
    residue_mask,
    dist_bins,
    w_in,
    w_out,
    w_t1,
    w_t2,
    w_dist,
    norm_params,
    dist_bias,
    m_in,
    m_out,
    m_t1,
    m_t2,
    m_dist,
    m_norm,
    m_bias,
    v_in,
    v_out,
    v_t1,
    v_t2,
    v_dist,
    v_norm,
    v_bias,
):
    tile_rows = pair_acts.shape[1]
    tile_cols = pair_acts.shape[2]
    width = w_out.shape[0]
    row_first = lax.axis_index("row") * tile_rows
    col_first = lax.axis_index("col") * tile_cols
    mask_vals = residue_mask[0].astype(jnp.float32)
    row_mask = lax.dynamic_slice_in_dim(mask_vals, row_first, tile_rows)
    col_mask = lax.dynamic_slice_in_dim(mask_vals, col_first, tile_cols)
    pair_mask = row_mask[:, None] * col_mask[None, :]
    mask_cube = pair_mask[..., None]
    pair_total = lax.psum(jnp.sum(pair_mask), ("crop", "row", "col"))
    low_in, low_out, low_t1, low_t2, low_dist = [
        weight.astype(jnp.bfloat16) for weight in (w_in, w_out, w_t1, w_t2, w_dist)
    ]
    acts = pair_acts[0].astype(jnp.float32)
    normed_one, rstd_one = standardize(acts)
    pair_norm = (normed_one * norm_params[0] + norm_params[1]).astype(jnp.bfloat16)
    projected = linear(pair_norm, low_in)
    left_proj = projected[..., :width]
    left_sig = jax.nn.sigmoid(projected[..., width : 2 * width])
    right_proj = projected[..., 2 * width : 3 * width]
    right_sig = jax.nn.sigmoid(projected[..., 3 * width : 4 * width])
    gate_sig = jax.nn.sigmoid(projected[..., 4 * width :])
    left_vals = (mask_cube * left_sig * left_proj).astype(jnp.bfloat16)
    right_vals = (mask_cube * right_sig * right_proj).astype(jnp.bfloat16)
    strips = lax.all_gather(right_vals, "row", axis=0, tiled=True)
    piece = strips
    triangle = jnp.transpose(
        lax.psum_scatter(
            jnp.einsum("jkc,ikc->jic", piece, left_vals, preferred_element_type=jnp.float32),
            "col",
            scatter_dimension=0,
            tiled=True,
        ),
        (1, 0, 2),
    )
    normed_two, rstd_two = standardize(triangle)
    tri_norm = (normed_two * norm_params[2] + norm_params[3]).astype(jnp.bfloat16)
    out_proj = linear(tri_norm, low_out)
    updated = acts + gate_sig * out_proj
    normed_three, rstd_three = standardize(updated)
    trans_in = (normed_three * norm_params[4] + norm_params[5]).astype(jnp.bfloat16)
    pre_act = linear(trans_in, low_t1)
    hidden = jax.nn.silu(pre_act).astype(jnp.bfloat16)
    final = updated + linear(hidden, low_t2)
    final_low = final.astype(jnp.bfloat16)
    logits = linear(final_low, low_dist) + dist_bias
    log_total = jax.nn.logsumexp(logits, -1)
    onehot = (dist_bins[0][..., None] == jnp.arange(w_dist.shape[1])).astype(jnp.float32)
    loss_local = jnp.sum(pair_mask * (log_total - jnp.sum(logits * onehot, -1)))
    d_logits = (mask_cube * (jnp.exp(logits - log_total[..., None]) - onehot) / pair_total).astype(
        jnp.bfloat16
    )
    grad_dist = weight_grad(final_low, d_logits)
    grad_bias = jnp.sum(d_logits.astype(jnp.float32), (0, 1))
    d_final = transposed(d_logits, low_dist)
    d_trans = d_final.astype(jnp.bfloat16)
    grad_t2 = weight_grad(hidden, d_trans)
    d_hidden = transposed(d_trans, low_t2)
    sig_pre = jax.nn.sigmoid(pre_act)
    d_pre = (d_hidden * sig_pre * (1.0 + pre_act * (1.0 - sig_pre))).astype(jnp.bfloat16)
    grad_t1 = weight_grad(trans_in, d_pre)
    d_trans_in = transposed(d_pre, low_t1)
    d_updated = d_final + standard_back(d_trans_in * norm_params[4], normed_three, rstd_three)
    d_out = (d_updated * gate_sig).astype(jnp.bfloat16)
    d_out_gate = d_updated * out_proj * gate_sig * (1.0 - gate_sig)
    grad_out = weight_grad(tri_norm, d_out)
    d_tri_norm = transposed(d_out, low_out)
    d_triangle = standard_back(d_tri_norm * norm_params[2], normed_two, rstd_two).astype(
        jnp.bfloat16
    )
    d_rows = lax.all_gather(d_triangle, "col", axis=1, tiled=True)
    d_left = jnp.einsum("ijc,jkc->ikc", d_rows, strips, preferred_element_type=jnp.float32)
    piece = d_rows
    d_right = lax.psum_scatter(
        jnp.einsum("ijc,ikc->jkc", piece, left_vals, preferred_element_type=jnp.float32).astype(
            jnp.bfloat16
        ),
        "row",
        scatter_dimension=0,
        tiled=True,
    ).astype(jnp.float32)
    d_proj = jnp.concatenate(
        [
            d_left * mask_cube * left_sig,
            d_left * mask_cube * left_proj * left_sig * (1.0 - left_sig),
            d_right * mask_cube * right_sig,
            d_right * mask_cube * right_proj * right_sig * (1.0 - right_sig),
            d_out_gate,
        ],
        -1,
    ).astype(jnp.bfloat16)
    grad_in = weight_grad(pair_norm, d_proj)
    d_pair_norm = transposed(d_proj, low_in)
    grad_norms = jnp.stack(
        [
            jnp.sum(d_pair_norm * normed_one, (0, 1)),
            jnp.sum(d_pair_norm, (0, 1)),
            jnp.sum(d_tri_norm * normed_two, (0, 1)),
            jnp.sum(d_tri_norm, (0, 1)),
            jnp.sum(d_trans_in * normed_three, (0, 1)),
            jnp.sum(d_trans_in, (0, 1)),
        ]
    )
    summed = lax.psum(
        (grad_in, grad_out, grad_t1, grad_t2, grad_dist, grad_norms, grad_bias, loss_local),
        ("crop", "row", "col"),
    )
    grads = summed[:7]
    squares = jnp.zeros((), jnp.float32)
    for grad in grads:
        squares = squares + jnp.sum(grad * grad)
    grad_norm = jnp.sqrt(squares)
    scale = CLIP_NORM / jnp.maximum(grad_norm, CLIP_NORM)
    params = (w_in, w_out, w_t1, w_t2, w_dist, norm_params, dist_bias)
    firsts = (m_in, m_out, m_t1, m_t2, m_dist, m_norm, m_bias)
    seconds = (v_in, v_out, v_t1, v_t2, v_dist, v_norm, v_bias)
    rates = (LEARN_RATE, LEARN_RATE, LEARN_RATE, LEARN_RATE, LEARN_RATE, GAIN_RATE, GAIN_RATE)
    results = [
        adamw_update(
            params[index], firsts[index], seconds[index], grads[index], scale, rates[index]
        )
        for index in range(7)
    ]
    return (
        results[0][0],
        results[1][0],
        results[2][0],
        results[3][0],
        results[4][0],
        results[5][0],
        results[6][0],
        results[0][1],
        results[1][1],
        results[2][1],
        results[3][1],
        results[4][1],
        results[5][1],
        results[6][1],
        results[0][2],
        results[1][2],
        results[2][2],
        results[3][2],
        results[4][2],
        results[5][2],
        results[6][2],
        summed[7],
        pair_total,
        grad_norm,
    )


F32 = jnp.float32
BF16 = jnp.bfloat16
NT = (((1,), (1,)), ((), ()))
NN = (((1,), (0,)), ((), ()))
TN = (((0,), (0,)), ((), ()))
MICRO = 1e3
VMEM_LIMIT = 56 * 1024 * 1024


def dot(left, right, dims=NN):
    return lax.dot_general(left, right, dims, preferred_element_type=F32)


def column_stats(values):
    center = values - jnp.mean(values, 0, keepdims=True)
    rstd = lax.rsqrt(jnp.mean(center * center, 0, keepdims=True) + NORM_EPS)
    return center * rstd, rstd


def column_back(grad, normed, rstd):
    return rstd * (
        grad
        - jnp.mean(grad, 0, keepdims=True)
        - normed * jnp.mean(grad * normed, 0, keepdims=True)
    )


def widen(param, lanes):
    return jnp.concatenate([param] * (lanes // param.shape[1]), 1)


def spread_rows(scratch, block):
    scratch[...] = jnp.swapaxes(block, 0, 1).astype(scratch.dtype)


def take_rows(scratch, start, count):
    return jnp.concatenate([scratch[start + u] for u in range(count)], 1).astype(F32)


def put_rows(scratch, start, count, values):
    lanes = values.shape[1] // count
    for u in range(count):
        scratch[start + u] = values[:, u * lanes : (u + 1) * lanes].astype(scratch.dtype)


def gather_rows(scratch, out_ref):
    out_ref[...] = jnp.swapaxes(scratch[...], 0, 1)


def call(kernel, grid, scalars, ins, outs, scratch, flops, name, aliases=None):
    return pl.pallas_call(
        kernel,
        grid_spec=pltpu.PrefetchScalarGridSpec(
            num_scalar_prefetch=len(scalars),
            grid=grid,
            in_specs=[pl.BlockSpec(block, index) for _, block, index in ins],
            out_specs=[pl.BlockSpec(block, index) for _, _, block, index in outs],
            scratch_shapes=scratch,
        ),
        out_shape=[jax.ShapeDtypeStruct(shape, dtype) for shape, dtype, _, _ in outs],
        compiler_params=pltpu.CompilerParams(vmem_limit_bytes=VMEM_LIMIT),
        cost_estimate=pl.CostEstimate(flops=int(flops), bytes_accessed=1, transcendentals=0),
        name=name,
        input_output_aliases=aliases or {},
    )(*scalars, *[a for a, _, _ in ins])


def code_rows(code_s, start, count):
    return jnp.concatenate([code_s[pl.ds(start + u, 1), :] for u in range(count)], 1)


def present_rows(code_s, start, count):
    return jnp.where(code_rows(code_s, start, count) < 0.0, 0.0, 1.0)


ROWS = 16
PROJECT_GROUP = 8
INPUT_GROUP = 16


def prepare_weights(w_in, w_out, w_t1, w_t2, w_dist, norms, bias, outs):
    projT, ogT, outT, out_w, t1T, t1, t2T, t2, distT, dist, ln_ref, bias_ref = outs
    count, chans = projT.shape
    projT[...] = (0.5 * jnp.transpose(w_in[:, :count])).astype(BF16)
    ogT[...] = (0.5 * jnp.transpose(w_in[:, count:])).astype(BF16)
    for weight, plain, turned, plain_scale, turned_scale in (
        (w_out, out_w, outT, 1.0, 1.0),
        (w_t1, t1, t1T, 1.0, 0.5),
        (w_t2, t2, t2T, 0.5, 1.0),
        (w_dist, distT, dist, 1.0, 1.0),
    ):
        plain[...] = (plain_scale * weight[...]).astype(BF16)
        turned[...] = (turned_scale * jnp.transpose(weight[...])).astype(BF16)
    for index in range(6):
        ln_ref[index] = jnp.transpose(jnp.broadcast_to(norms[index : index + 1, :], (128, chans)))
    bias_ref[...] = jnp.transpose(jnp.broadcast_to(bias[...], (128, bias.shape[1])))


def project_kernel(acts_ref, code_ref, w_ref, ln_ref, a_ref, b_ref, acts_s, a_s, b_s, code_s):
    width = a_ref.shape[0]
    code_s[...] = code_ref[0].astype(F32)
    spread_rows(acts_s, acts_ref[...])

    def some(step, carry):
        start = step * PROJECT_GROUP
        values = take_rows(acts_s, start, PROJECT_GROUP)
        lanes = values.shape[1]
        normed, _ = column_stats(values)
        low = normed * widen(ln_ref[0], lanes) + widen(ln_ref[1], lanes)
        low = (low * present_rows(code_s, start, PROJECT_GROUP)).astype(BF16)
        proj = dot(w_ref[...], low)
        left = proj[:width] * (jnp.tanh(proj[width : 2 * width]) + 1.0)
        right = proj[2 * width : 3 * width] * (jnp.tanh(proj[3 * width :]) + 1.0)
        put_rows(a_s, start, PROJECT_GROUP, left)
        put_rows(b_s, start, PROJECT_GROUP, right)
        return carry

    lax.fori_loop(0, ROWS // PROJECT_GROUP, some, 0)
    gather_rows(a_s, a_ref)
    gather_rows(b_s, b_ref)


def project_two_kernel(acts0, code0, acts1, code1, w_ref, ln_ref, a0, b0, a1, b1, *scratch):
    steps = pl.num_programs(0) // 2

    @pl.when(pl.program_id(0) < steps)
    def _():
        project_kernel(acts0, code0, w_ref, ln_ref, a0, b0, *scratch)

    @pl.when(pl.program_id(0) >= steps)
    def _():
        project_kernel(acts1, code1, w_ref, ln_ref, a1, b1, *scratch)


def project_two(first, second, w_proj, ln_wide):
    chans, rows, lanes = first.shape[0] - 1, first.shape[1], first.shape[2]
    block = (chans, ROWS, lanes)
    steps = rows // ROWS
    spots = [lambda i: jnp.minimum(i, steps - 1), lambda i: jnp.maximum(i - steps, 0)]
    staged = pltpu.VMEM((ROWS, chans, lanes), BF16)
    ins, outs = [], []
    for acts, spot in zip((first, second), spots):
        ins.append((acts, block, lambda i, *_, spot=spot: (0, spot(i), 0)))
        ins.append((acts, (1, ROWS, lanes), lambda i, *_, spot=spot: (chans, spot(i), 0)))
        outs += [((chans, rows, lanes), BF16, block, lambda i, *_, spot=spot: (0, spot(i), 0))] * 2
    return call(
        project_two_kernel,
        (2 * steps,),
        [],
        ins + [(w_proj, w_proj.shape, fixed(0, 0)), (ln_wide, ln_wide.shape, fixed(0, 0, 0))],
        outs,
        [staged, staged, staged, pltpu.VMEM((ROWS, lanes), F32)],
        30 * MICRO,
        "project_two",
    )


def fixed(*zeros):
    return lambda i, *_: zeros


def project(acts, w_proj, ln_wide):
    chans, rows, lanes = acts.shape[0] - 1, acts.shape[1], acts.shape[2]
    block = (chans, ROWS, lanes)
    mid = lambda i, *_: (0, i, 0)
    out = ((chans, rows, lanes), BF16, block, mid)
    staged = pltpu.VMEM((ROWS, chans, lanes), BF16)
    return call(
        project_kernel,
        (rows // ROWS,),
        [],
        [
            (acts, block, mid),
            (acts, (1, ROWS, lanes), lambda i, *_: (chans, i, 0)),
            (w_proj, w_proj.shape, fixed(0, 0)),
            (ln_wide, ln_wide.shape, fixed(0, 0, 0)),
        ],
        [out, out],
        [staged, staged, staged, pltpu.VMEM((ROWS, lanes), F32)],
        15 * MICRO,
        "project",
    )


CHANS = 16
TRIANGLE_CHANS = 32


def ordered(flag, own, other):
    part = own.shape[0] // 2
    waves = []
    for wave in range(2):
        mine, rest = own[wave * part : (wave + 1) * part], other[wave * part : (wave + 1) * part]
        waves += [jnp.where(flag, mine, rest), jnp.where(flag, rest, mine)]
    return jnp.concatenate(waves, 0)


def kept_first(ids, q):
    return ids[2] ^ ((ids[0] ^ q) // 2) ^ (ids[1] // 2) == 0


def triangle_kernel(q, ids, a0, a1, b0, b1, keep_ref, send_ref):
    first = kept_first(ids, q)
    part = b0.shape[1] // 2
    for chan in range(TRIANGLE_CHANS):
        rows = jnp.concatenate([a0[chan], a1[chan]], 0)
        x = dot(jnp.concatenate([b0[chan], b1[chan]], 0), rows, NT)
        one = jnp.concatenate([x[:part], x[2 * part : 3 * part]], 0)
        two = jnp.concatenate([x[part : 2 * part], x[3 * part :]], 0)
        keep_ref[chan] = jnp.where(first, one, two)
        send_ref[chan] = jnp.where(first, two, one).astype(BF16)


def triangle(q, ids, a, b):
    chans, half, lanes = a[0].shape
    lead = lambda i, *_: (i, 0, 0)
    block = (TRIANGLE_CHANS, half, lanes)
    out = (chans, half, 2 * half)
    return call(
        functools.partial(triangle_kernel, q),
        (chans // TRIANGLE_CHANS,),
        [ids],
        [(v, block, lead) for v in (*a, *b)],
        [(out, F32, (TRIANGLE_CHANS, half, 2 * half), lead), (out, BF16, (TRIANGLE_CHANS, half, 2 * half), lead)],
        [],
        14 * MICRO,
        "triangle",
    )


GROUP = 16


T1_ROW, T2_ROW, OUT_ROW, OG_ROW, DIST_ROW, NORM_ROW, BIAS_ROW, LOSS_ROW, SUM_ROWS = (
    0, 512, 1024, 1152, 1280, 1344, 1350, 1351, 1352,
)


def row_sums(values):
    return jnp.sum(jnp.transpose(values), 0, keepdims=True)


def pair_kernel(
    first_call, last_call,
    ids, x_keep, x_recv, acts_ref, code_ref, ln_ref, w_outT, w_out, w_ogT, w_t1T, w_t1,
    w_t2T, w_t2, w_distT, w_dist, bias_ref, *rest,
):
    prior = () if first_call else rest[:2]
    dx_ref, sums, wide, x_s, acts_s, dx_s, code_s = rest[len(prior) :]
    chans = acts_ref.shape[0]
    lanes = 128 * GROUP
    bins = w_distT.shape[0]
    hidden_width = w_t1T.shape[0]

    @pl.when(pl.program_id(0) == 0)
    def _():
        if first_call:
            sums[...] = jnp.zeros_like(sums)
            wide[...] = jnp.zeros_like(wide)
        else:
            sums[...] = prior[0][...]
            wide[...] = prior[1][...]

    spread_rows(x_s, x_keep[...] + x_recv[...].astype(F32))
    spread_rows(acts_s, acts_ref[...])
    code_s[...] = code_ref[0].astype(F32)
    param = [widen(ln_ref[index], lanes) for index in range(6)]
    bin_index = lax.broadcasted_iota(jnp.int32, (bins, lanes), 0).astype(F32)

    def fold(values):
        return sum(values[:, 128 * part : 128 * part + 128] for part in range(GROUP))

    def add(row, values):
        sums[row : row + values.shape[0]] += values

    def group(step, carry):
        first = step * GROUP
        x = take_rows(x_s, first, GROUP)
        acts = take_rows(acts_s, first, GROUP)
        code = code_rows(code_s, first, GROUP)
        normed_two, rstd_two = column_stats(x)
        tri = (normed_two * param[2] + param[3]).astype(BF16)
        out = dot(w_outT[...], tri)
        normed_one, _ = column_stats(acts)
        low = (normed_one * param[0] + param[1]).astype(BF16)
        gate = 0.5 * jnp.tanh(dot(w_ogT[...], low)) + 0.5
        z1 = acts + gate * out
        normed_three, rstd_three = column_stats(z1)
        trans = (normed_three * param[4] + param[5]).astype(BF16)
        pre = dot(w_t1T[...], trans)
        tanh = jnp.tanh(pre)
        bent = pre * tanh
        hidden = (pre + bent).astype(BF16)
        slope = (1.0 + tanh) * (1.0 + (pre - bent))
        final = (z1 + dot(w_t2T[...], hidden)).astype(BF16)
        logits = dot(w_distT[...], final) + widen(bias_ref[...], lanes)
        top = jnp.max(logits, 0, keepdims=True)
        powers = jnp.exp(logits - top)
        total = jnp.sum(powers, 0, keepdims=True)
        present = jnp.where(code < 0.0, 0.0, 1.0)
        hot = bin_index == code
        picked = jnp.sum(jnp.where(hot, logits, 0.0), 0, keepdims=True)
        sums[LOSS_ROW : LOSS_ROW + 1] += fold(present * (jnp.log(total) + top) - picked)
        d_logits = (powers * (present / total) - jnp.where(hot, 1.0, 0.0)).astype(BF16)
        add(DIST_ROW, dot(d_logits, final, NT))
        wide[5, :bins] += fold(d_logits.astype(F32))
        d_final = dot(w_dist[...], d_logits)
        d_trans = d_final.astype(BF16)
        add(T2_ROW, dot(hidden, d_trans, NT))
        d_pre = (dot(w_t2[...], d_trans) * slope).astype(BF16)
        add(T1_ROW, dot(d_pre, trans, NT))
        d_tn = dot(w_t1[...], d_pre)
        wide[2] += fold(d_tn * normed_three)
        wide[3] += fold(d_tn)
        d_z1 = d_final + column_back(d_tn * param[4], normed_three, rstd_three)
        d_gated = d_z1 * gate
        d_out = d_gated.astype(BF16)
        d_og = (d_gated * out * (1.0 - gate)).astype(BF16)
        add(OUT_ROW, dot(d_out, tri, NT))
        g_og = dot(d_og, jnp.concatenate([low, normed_one.astype(BF16)], 0), NT)
        add(OG_ROW, g_og[:, :chans])
        wide[6] += g_og[:, chans:]
        wide[4] += fold(d_og.astype(F32))
        d_xn = dot(w_out[...], d_out)
        wide[0] += fold(d_xn * normed_two)
        wide[1] += fold(d_xn)
        d_x = column_back(d_xn * param[2], normed_two, rstd_two)
        put_rows(dx_s, first, GROUP, d_x)
        return carry

    lax.fori_loop(0, ROWS // GROUP, group, 0)
    gather_rows(dx_s, dx_ref)

    if last_call:

        @pl.when(pl.program_id(0) == pl.num_programs(0) - 1)
        def _():
            gate_w = 2.0 * w_ogT[...].astype(F32)
            for index in range(4):
                add(NORM_ROW + index, row_sums(wide[index]))
            total = jnp.sum(wide[4], 1, keepdims=True)
            add(NORM_ROW + 4, jnp.sum(gate_w * wide[6], 0, keepdims=True))
            add(NORM_ROW + 5, jnp.sum(gate_w * total, 0, keepdims=True))
            add(BIAS_ROW, row_sums(wide[5]))


def pair_block(q, ids, x_keep, x_recv, acts_kj, ln_wide, weights, bias, prior, last_call):
    chans, rows, lanes = x_keep.shape
    block = (chans, ROWS, lanes)
    mid = lambda i, *_: (0, i, 0)

    def where(i, ids):
        owner = ids[0] ^ q
        return 8 * ((i % 2) ^ (owner % 2) ^ (ids[1] % 2)) + 2 * owner + i // 2

    full = [(w, w.shape, fixed(*([0] * w.ndim))) for w in (ln_wide, *weights, bias, *prior)]
    shapes = [(SUM_ROWS, 128), (7, 128, 128)]
    return call(
        functools.partial(pair_kernel, not prior, last_call),
        (rows // ROWS,),
        [ids],
        [
            (x_keep, block, mid),
            (x_recv, block, mid),
            (acts_kj, block, lambda i, ids: (0, where(i, ids), 0)),
            (acts_kj, (1, ROWS, lanes), lambda i, ids: (chans, where(i, ids), 0)),
        ]
        + full,
        [((chans, rows, lanes), BF16, block, mid)]
        + [(s, F32, s, fixed(*([0] * len(s)))) for s in shapes],
        [pltpu.VMEM((ROWS, chans, lanes), t) for t in (F32, BF16, BF16)] + [pltpu.VMEM((ROWS, lanes), F32)],
        35 * MICRO,
        "pair",
    )


def right_back_kernel(ids, *refs):
    owns, others, firsts, seconds = refs[:4], refs[4:8], refs[8:12], refs[12:16]
    out0, out1 = refs[16:]
    half = out0.shape[1]
    own_first = kept_first(ids, 0)
    for chan in range(CHANS):
        grads = jnp.concatenate(
            [ordered(own_first, owns[q][chan], others[q][chan]) for q in range(4)], 1
        )
        values = jnp.concatenate([v[q][chan] for q in range(4) for v in (firsts, seconds)], 0)
        total = dot(grads, values).astype(BF16)
        out0[chan] = total[:half]
        out1[chan] = total[half:]


def right_back(ids, owns, others, firsts, seconds):
    chans, half, lanes = firsts[0].shape
    lead = lambda i, *_: (i, 0, 0)
    out = ((chans, half, lanes), BF16, (CHANS, half, lanes), lead)
    return call(
        right_back_kernel,
        (chans // CHANS,),
        [ids],
        [(v, (CHANS, half, 2 * half), lead) for v in (*owns, *others)]
        + [(v, (CHANS, half, lanes), lead) for v in (*firsts, *seconds)],
        [out, out],
        [],
        25 * MICRO,
        "right_back",
    )


def turn_kernel(first, second, out_ref):
    for chan in range(first.shape[0]):
        out_ref[chan] = jnp.transpose(jnp.concatenate([first[chan], second[chan]], 0))


def turn(first, second):
    chans, half, lanes = first.shape
    lead = lambda i, *_: (i, 0, 0)
    count = (chans + 1) // 2
    block = (count, half, lanes)
    return call(
        turn_kernel,
        (2,),
        [],
        [(first, block, lead), (second, block, lead)],
        [((chans, lanes, 2 * half), BF16, (count, lanes, 2 * half), lead)],
        [],
        12 * MICRO,
        "turn",
    )[0]


def left_back_kernel(ids, *refs):
    owns, others, firsts, seconds = refs[:4], refs[4:8], refs[8:12], refs[12:16]
    out0, out1 = refs[16:]
    half = out0.shape[1]
    for chan in range(CHANS):
        total = None
        for pair in range(2):
            own_first = kept_first(ids, 2 * pair)
            grads, values = [], []
            for q in (2 * pair, 2 * pair + 1):
                grads.append(ordered(own_first, owns[q][chan], others[q][chan]))
                values += [firsts[q][chan], seconds[q][chan]]
            term = dot(jnp.concatenate(grads, 0), jnp.concatenate(values, 0), TN)
            total = term if total is None else total + term
        total = total.astype(BF16)
        out0[chan] = total[:half]
        out1[chan] = total[half:]


def left_back(ids, owns, others, firsts, seconds):
    chans, half, lanes = firsts[0].shape
    lead = lambda i, *_: (i, 0, 0)
    out = ((chans, half, lanes), BF16, (CHANS, half, lanes), lead)
    return call(
        left_back_kernel,
        (chans // CHANS,),
        [ids],
        [(v, (CHANS, half, 2 * half), lead) for v in (*owns, *others)]
        + [(v, (CHANS, half, lanes), lead) for v in (*firsts, *seconds)],
        [out, out],
        [],
        25 * MICRO,
        "left_back",
    )


SIDE_ROWS = 272


def affine_grad(normed_grad, total, ln_ref):
    gain, shift = jnp.transpose(ln_ref[0])[:1], jnp.transpose(ln_ref[1])[:1]
    return normed_grad * gain + total * shift


def input_back_kernel(count, first_call, last_call, w_ref, ln_ref, *rest):
    halves, rest = [rest[3 * n : 3 * n + 3] for n in range(count)], rest[3 * count :]
    prior = () if first_call else rest[:3]
    out_ref, g_ref, sum_ref, acts_s, grad_s, code_s = rest[len(prior) :]
    width = halves[0][2].shape[0]

    @pl.when(pl.program_id(0) == 0)
    def _():
        if first_call:
            out_ref[...] = jnp.zeros_like(out_ref)
            g_ref[...] = jnp.zeros_like(g_ref)
            sum_ref[...] = jnp.zeros_like(sum_ref)
        else:
            out_ref[...] = prior[0][...]
            g_ref[...] = prior[1][...]
            sum_ref[...] = prior[2][...]

    steps = pl.num_programs(0) // count
    for number, (acts_ref, code_ref, grad_ref) in enumerate(halves):

        @pl.when(pl.program_id(0) // steps == number)
        def _(acts_ref=acts_ref, code_ref=code_ref, grad_ref=grad_ref):
            code_s[...] = code_ref[0].astype(F32)
            spread_rows(acts_s, acts_ref[...])
            spread_rows(grad_s, grad_ref[...])

    def some(step, carry):
        start = step * INPUT_GROUP
        values = take_rows(acts_s, start, INPUT_GROUP)
        lanes = values.shape[1]
        normed, _ = column_stats(values)
        low = (normed * widen(ln_ref[0], lanes) + widen(ln_ref[1], lanes)).astype(BF16)
        proj = dot(w_ref[...], low)
        tanh = jnp.tanh(proj[width:])
        d_half = take_rows(grad_s, start, INPUT_GROUP) * (0.5 * present_rows(code_s, start, INPUT_GROUP))
        d_tanh = d_half * tanh
        d_value = d_half + d_tanh
        d_gate = proj[:width] * (d_half - d_tanh * tanh)
        d_proj = jnp.concatenate([d_value.astype(BF16), d_gate.astype(BF16)], 0)
        g_ref[...] += dot(d_proj, normed.astype(BF16), NT)
        for first, part in ((0, d_value), (width, d_gate)):
            sum_ref[first : first + width] += sum(
                part[:, 128 * u : 128 * u + 128] for u in range(lanes // 128)
            )
        return carry

    lax.fori_loop(0, ROWS // INPUT_GROUP, some, 0)

    if last_call:

        @pl.when(pl.program_id(0) == pl.num_programs(0) - 1)
        def _():
            part = 2.0 * w_ref[...].astype(F32)
            total = jnp.sum(sum_ref[...], 1, keepdims=True)
            gain = jnp.sum(part * g_ref[...], 0, keepdims=True)
            shift = jnp.sum(part * total, 0, keepdims=True)
            out_ref[: 2 * width] = affine_grad(g_ref[...], total, ln_ref)
            out_ref[2 * width : 2 * width + 1] = gain
            out_ref[2 * width + 1 : 2 * width + 2] = shift


def input_back(halves, part, w_proj, ln_wide, prior, last_call):
    chans, rows, lanes = halves[0][1].shape
    block = (chans, ROWS, lanes)
    steps = rows // ROWS
    depth = w_proj.shape[0] // 2
    shapes = [(SIDE_ROWS, chans), (depth, chans), (depth, 128)]
    ins = []
    for number, (acts, grad) in enumerate(halves):
        spot = lambda i, number=number: jnp.clip(i - number * steps, 0, steps - 1)
        mid = lambda i, *_, spot=spot: (0, spot(i), 0)
        ins += [
            (acts, block, mid),
            (acts, (1, ROWS, lanes), lambda i, *_, spot=spot: (chans, spot(i), 0)),
            (grad, block, mid),
        ]
    return call(
        functools.partial(input_back_kernel, len(halves), not prior, last_call),
        (len(halves) * steps,),
        [],
        [(w_proj, (depth, chans), fixed(part, 0)), (ln_wide, ln_wide.shape, fixed(0, 0, 0))]
        + ins
        + [(v, v.shape, fixed(0, 0)) for v in prior],
        [(s, F32, s, fixed(0, 0)) for s in shapes],
        [
            pltpu.VMEM((ROWS, chans, lanes), BF16),
            pltpu.VMEM((ROWS, chans, lanes), BF16),
            pltpu.VMEM((ROWS, lanes), F32),
        ],
        16 * MICRO,
        "input_back",
    )


def reduce_kernel(pair_ref, left_ref, right_ref, out_ref, full_s, core_s, crop_s, row_s, send, recv):
    side, spot, level = lax.axis_index("col"), lax.axis_index("crop"), lax.axis_index("row")
    mesh_id = pl.DeviceIdType.MESH
    sibling = {"col": 1 - side}
    crops = [{"crop": lax.rem(spot + n, 4)} for n in range(1, 4)]
    levels = [{"row": lax.rem(level + n, 4)} for n in range(1, 4)]
    barrier = pltpu.get_barrier_semaphore()
    for device in [sibling] + crops + levels:
        pl.semaphore_signal(barrier, inc=1, device_id=device, device_id_type=mesh_id)
    pl.semaphore_wait(barrier, 7)

    def copy(source, target, index, device):
        return pltpu.make_async_remote_copy(
            src_ref=source, dst_ref=target, send_sem=send.at[index], recv_sem=recv.at[index],
            device_id=device, device_id_type=mesh_id,
        )

    def run(copies):
        for one in copies:
            one.start()
        for one in copies:
            one.wait()

    half = full_s.shape[0] // 2
    quarter, share = half // 4, half // 16
    row = 0
    for ref in (pair_ref, left_ref, right_ref):
        full_s[row : row + ref.shape[0]] = ref[...]
        row += ref.shape[0]
    full_s[row:] = jnp.zeros((full_s.shape[0] - row, full_s.shape[1]), F32)
    base = pl.multiple_of(side * half, 8)
    run([copy(full_s.at[pl.ds(pl.multiple_of((1 - side) * half, 8), half)], core_s, 0, sibling)])
    full_s[pl.ds(base, half)] += core_s[...]
    def part(number):
        return pl.ds(pl.multiple_of(base + number * quarter, 8), quarter)

    run([copy(full_s.at[part(lax.rem(spot + n, 4))], crop_s.at[spot], n, crops[n - 1]) for n in range(1, 4)])
    mine = part(spot)
    crop_s[spot] = full_s[mine]
    full_s[mine] = crop_s[0] + crop_s[1] + crop_s[2] + crop_s[3]
    def slot(number):
        return pl.ds(pl.multiple_of(base + spot * quarter + number * share, 8), share)

    run([copy(full_s.at[slot(lax.rem(level + n, 4))], row_s.at[level], 3 + n, levels[n - 1]) for n in range(1, 4)])
    own = slot(level)
    row_s[level] = full_s[own]
    out_ref[own] = row_s[0] + row_s[1] + row_s[2] + row_s[3]
    run([copy(out_ref.at[own], out_ref.at[own], 6 + n, levels[n - 1]) for n in range(1, 4)])
    run([copy(out_ref.at[mine], out_ref.at[mine], 9 + n, crops[n - 1]) for n in range(1, 4)])
    run([copy(out_ref.at[pl.ds(base, half)], out_ref.at[pl.ds(base, half)], 13, sibling)])


ALL_ROWS = 2048


def reduce_all(*parts):
    lanes = parts[0].shape[1]
    return pl.pallas_call(
        reduce_kernel,
        out_shape=jax.ShapeDtypeStruct((ALL_ROWS, lanes), F32),
        scratch_shapes=[
            pltpu.VMEM((ALL_ROWS, lanes), F32),
            pltpu.VMEM((ALL_ROWS // 2, lanes), F32),
            pltpu.VMEM((4, ALL_ROWS // 8, lanes), F32),
            pltpu.VMEM((4, ALL_ROWS // 32, lanes), F32),
            pltpu.SemaphoreType.DMA((14,)),
            pltpu.SemaphoreType.DMA((14,)),
        ],
        compiler_params=pltpu.CompilerParams(
            collective_id=1, has_side_effects=True, vmem_limit_bytes=VMEM_LIMIT
        ),
        name="reduce_all",
    )(*parts)


def flip(a, b):
    return 2 * lax.rem(a // 2 + b // 2, 2) + lax.rem(a + b, 2)


def swap_bits(a):
    return 2 * lax.rem(a, 2) + a // 2


def spread_kernel(
    acts_ref, code_ref, w_in, w_out, w_t1, w_t2, w_dist, norms, bias,
    wave0_ref, wave1_ref, x_ref, y_ref, a_ref, b_ref,
    projT, ogT, outT, out_w, t1T, t1, t2T, t2, distT, dist, ln_ref, bias_ref,
    mid, taken, made, fetched, plane_send, plane_recv, share_send, share_recv, level_send, level_recv, local,
    wave_v, a_v, b_v, acts_s, a_s, b_s, code_s,
):
    spot, level = lax.axis_index("crop"), lax.axis_index("row")
    chans = mid.shape[2]
    early, middle = chans // 4, 5 * chans // 8
    cuts = [[(0, early), (early, middle - early), (middle, chans - middle)], [(0, chans)]]
    waves = (wave0_ref, wave1_ref)
    mesh_id = pl.DeviceIdType.MESH

    def block_rows(wave, distance):
        return pl.ds(pl.multiple_of(32 * flip(spot, distance) + 16 * wave, 16), 16)

    def fetch_block(wave, distance):
        return pltpu.make_async_copy(
            acts_ref.at[block_rows(wave, distance)], taken.at[wave, distance], fetched.at[4 * wave + distance]
        )

    def make_block(wave, distance):
        fetch_block(wave, distance).wait()

        def turn_row(row, carry):
            acts_s[row] = jnp.transpose(taken[wave, distance, row])
            return carry

        lax.fori_loop(0, ROWS, turn_row, 0, unroll=8)
        made[wave, distance, : chans - 1] = jnp.swapaxes(acts_s[...], 0, 1)
        made[wave, distance, chans - 1] = code_ref[block_rows(wave, distance), :]

    for wave in range(2):
        for distance in range(4):
            fetch_block(wave, distance).start()
    barrier = pltpu.get_barrier_semaphore()
    for n in range(1, 4):
        for device in ({"crop": lax.rem(spot + n, 4)}, {"row": lax.rem(level + n, 4)}):
            pl.semaphore_signal(barrier, inc=1, device_id=device, device_id_type=mesh_id)
    pl.semaphore_wait(barrier, 6)

    def plane_copy(wave, cut, distance):
        first, count = cuts[wave][cut]
        target = flip(spot, distance)
        source = made.at[wave, distance, pl.ds(first, count)]
        landing = mid.at[wave, distance, pl.ds(first, count)]
        index = 12 * wave + 4 * cut + distance
        if distance == 0:
            return pltpu.make_async_copy(source, landing, plane_recv.at[index])
        return pltpu.make_async_remote_copy(
            src_ref=source, dst_ref=landing, send_sem=plane_send.at[index], recv_sem=plane_recv.at[index],
            device_id={"crop": target}, device_id_type=mesh_id,
        )

    def landed(wave, cut, label):
        first, count = cuts[wave][cut]
        return waves[wave].at[pl.ds(first, count), pl.ds(16 * label, 16)]

    def level_copy(wave, cut, label, distance):
        first, count = cuts[wave][cut]
        source = mid.at[wave, distance, pl.ds(first, count)]
        target = swap_bits(flip(spot, distance))
        index = 12 * wave + 4 * cut + label
        remote = pltpu.make_async_remote_copy(
            src_ref=source, dst_ref=landed(wave, cut, label),
            send_sem=level_send.at[index], recv_sem=level_recv.at[index],
            device_id={"row": target}, device_id_type=mesh_id,
        )
        return target, remote, pltpu.make_async_copy(source, landed(wave, cut, label), local.at[3 * wave + cut])

    def each_level(action, wave, cut):
        for label in range(4):
            for distance in range(4):

                @pl.when(flip(level, label) == distance)
                def _(label=label, distance=distance):
                    action(wave, cut, label, distance)

    def shares(cut, label):
        first, count = cuts[0][cut]
        index = 8 * cut + 2 * label
        return [
            pltpu.make_async_remote_copy(
                src_ref=landed(0, cut, label),
                dst_ref=ref.at[pl.ds(first, count), pl.ds(16 * label, 16)],
                send_sem=share_send.at[index + n], recv_sem=share_recv.at[index + n],
                device_id={"crop": flip(spot, 1 + n)}, device_id_type=mesh_id,
            )
            for n, ref in enumerate((x_ref, y_ref))
        ]

    plane = [
        [[plane_copy(wave, cut, distance) for distance in range(4)] for cut in range(len(cuts[wave]))]
        for wave in range(2)
    ]
    for distance in (1, 3, 2, 0):
        make_block(0, distance)
        plane[0][0][distance].start()
    for copies in plane[0][1:]:
        for one in copies:
            one.start()
    for distance in (1, 3, 2, 0):
        make_block(1, distance)
        plane[1][0][distance].start()

    def begin(wave, cut, label, distance):
        one = plane[wave][cut][distance]
        one.wait() if distance == 0 else one.wait_recv()
        target, remote, stay = level_copy(wave, cut, label, distance)

        @pl.when(target == level)
        def _():
            stay.start()

        @pl.when(target != level)
        def _():
            remote.start()

    def arrive(wave, cut, label, distance):
        target, remote, stay = level_copy(wave, cut, label, distance)

        @pl.when(target == level)
        def _():
            stay.wait()

        @pl.when(target != level)
        def _():
            remote.wait_recv()
            remote.wait_send()

    def pass_on(cut):
        each_level(arrive, 0, cut)
        for label in range(4):
            for one in shares(cut, label):
                one.start()

    each_level(begin, 0, 0)
    prepare_weights(
        w_in, w_out, w_t1, w_t2, w_dist, norms, bias,
        (projT, ogT, outT, out_w, t1T, t1, t2T, t2, distT, dist, ln_ref, bias_ref),
    )
    each_level(begin, 0, 1)
    each_level(begin, 0, 2)
    each_level(begin, 1, 0)
    for cut in range(3):
        pass_on(cut)
    fetch = pltpu.make_async_copy(wave0_ref, wave_v, local.at[4])
    fetch.start()
    fetch.wait()
    width = a_v.shape[0]

    def project_rows(step, carry):
        rows = pl.ds(pl.multiple_of(step * ROWS, ROWS), ROWS)
        project_kernel(
            wave_v.at[pl.ds(0, width), rows], wave_v.at[pl.ds(width, 1), rows], projT, ln_ref,
            a_v.at[:, rows], b_v.at[:, rows], acts_s, a_s, b_s, code_s,
        )
        return carry

    lax.fori_loop(0, wave_v.shape[1] // ROWS, project_rows, 0)
    results = [
        pltpu.make_async_copy(a_v, a_ref, local.at[5]), pltpu.make_async_copy(b_v, b_ref, local.at[6])
    ]
    for one in results:
        one.start()
    for copies in plane[0] + plane[1]:
        for one in copies[1:]:
            one.wait_send()
    for cut in range(3):
        for label in range(4):
            for one in shares(cut, label):
                one.wait()
    for one in results:
        one.wait()
    each_level(arrive, 1, 0)


def spread(acts, code, w_in, w_out, w_t1, w_t2, w_dist, norms, bias):
    rows, lanes, width = acts.shape
    chans, half = width + 1, rows // 2
    anywhere = pl.BlockSpec(memory_space=pl.ANY)
    whole = pl.BlockSpec(memory_space=pltpu.VMEM)
    staged = pltpu.VMEM((ROWS, width, lanes), BF16)
    shapes = [(4 * width, width), (width, width)]
    for weight in (w_out, w_t1, w_t2, w_dist):
        shapes += [(weight.shape[1], weight.shape[0]), weight.shape]
    shapes = [jax.ShapeDtypeStruct(shape, BF16) for shape in shapes]
    shapes += [jax.ShapeDtypeStruct((6, width, 128), F32), jax.ShapeDtypeStruct((bias.shape[0], 128), F32)]
    return pl.pallas_call(
        spread_kernel,
        in_specs=[anywhere] + [whole] * 8,
        out_specs=[anywhere] * 6 + [whole] * len(shapes),
        out_shape=[jax.ShapeDtypeStruct((chans, half, lanes), BF16)] * 4
        + [jax.ShapeDtypeStruct((width, half, lanes), BF16)] * 2
        + shapes,
        scratch_shapes=[pltpu.VMEM((2, 4, chans, ROWS, lanes), BF16)]
        + [pltpu.VMEM((2, 4, ROWS, lanes, width), BF16)]
        + [pltpu.VMEM((2, 4, chans, ROWS, lanes), BF16)]
        + [pltpu.SemaphoreType.DMA((8,))]
        + [pltpu.SemaphoreType.DMA((16,)) for _ in range(2)]
        + [pltpu.SemaphoreType.DMA((24,)) for _ in range(2)]
        + [pltpu.SemaphoreType.DMA((16,)) for _ in range(2)]
        + [pltpu.SemaphoreType.DMA((7,))]
        + [pltpu.VMEM((chans, half, lanes), BF16)]
        + [pltpu.VMEM((width, half, lanes), BF16)] * 2
        + [staged] * 3
        + [pltpu.VMEM((ROWS, lanes), F32)],
        compiler_params=pltpu.CompilerParams(
            collective_id=2, has_side_effects=True, vmem_limit_bytes=VMEM_LIMIT
        ),
        name="spread",
    )(acts, code, w_in, w_out, w_t1, w_t2, w_dist.T, norms, bias.reshape(1, -1))


def update_kernel(early_ref, *refs):
    ins, outs = refs[:21], refs[21:]
    left_ref = early_ref.at[pl.ds(SUM_ROWS, SIDE_ROWS)]
    right_ref = early_ref.at[pl.ds(SUM_ROWS + SIDE_ROWS, SIDE_ROWS)]
    loss_ref, total_ref, norm_ref = outs[21:]
    total = early_ref[LOSS_ROW - 1, 127]
    inverse = 1.0 / total
    half = SIDE_ROWS - 16
    grads = [
        jnp.concatenate(
            [
                jnp.transpose(left_ref[:half]),
                jnp.transpose(right_ref[:half]),
                jnp.transpose(early_ref[OG_ROW : OG_ROW + 128]),
            ],
            1,
        ),
        jnp.transpose(early_ref[OUT_ROW : OUT_ROW + 128]),
        jnp.transpose(early_ref[T1_ROW : T1_ROW + 512]),
        early_ref[T2_ROW : T2_ROW + 512],
        early_ref[DIST_ROW : DIST_ROW + 64],
        jnp.concatenate(
            [
                left_ref[half : half + 2] + right_ref[half : half + 2] + early_ref[NORM_ROW + 4 : NORM_ROW + 6],
                early_ref[NORM_ROW : NORM_ROW + 4],
            ],
            0,
        ),
        early_ref[BIAS_ROW : BIAS_ROW + 1, :64],
    ]
    grads = [grad * inverse for grad in grads]
    squares = sum(jnp.sum(grad * grad, keepdims=True).reshape(1, 1) for grad in grads)
    grad_norm = jnp.sqrt(squares)
    scale = CLIP_NORM / jnp.maximum(grad_norm, CLIP_NORM)
    rates = (LEARN_RATE,) * 5 + (GAIN_RATE,) * 2
    for index in range(7):
        new = adamw_update(
            *[ins[7 * part + index][...].reshape(grads[index].shape) for part in range(3)],
            grads[index], scale, rates[index],
        )
        for part in range(3):
            outs[7 * part + index][...] = new[part].reshape(outs[7 * part + index].shape)
    norm_ref[...] = grad_norm
    loss_ref[...] = jnp.sum(early_ref[LOSS_ROW : LOSS_ROW + 1], keepdims=True).reshape(1, 1)
    total_ref[...] = jnp.full((1, 1), total, F32)


def update(early, params, firsts, seconds):
    flat = [v.T if index % 7 == 4 else v for index, v in enumerate((*params, *firsts, *seconds))]
    shapes = [v.shape for v in flat] + [(1, 1)] * 3
    outs = pl.pallas_call(
        update_kernel,
        out_shape=[jax.ShapeDtypeStruct(s, F32) for s in shapes],
        compiler_params=pltpu.CompilerParams(vmem_limit_bytes=VMEM_LIMIT),
        name="update",
    )(early, *flat)
    outs = [v.T if index in (4, 11, 18) else v for index, v in enumerate(outs)]
    return (*outs[:21], *[v[0, 0] for v in outs[21:]])


def after(value, *earlier):
    return lax.optimization_barrier((value, *earlier))[0]


def on_device_planes(
    pair_acts, residue_mask, dist_bins, w_in, w_out, w_t1, w_t2, w_dist, norm_params, dist_bias, *moments
):
    firsts, seconds = moments[:7], moments[7:]
    spot = lax.axis_index("crop")
    level = lax.axis_index("row")
    side = lax.axis_index("col")
    rows, cols, chans = pair_acts.shape[1:]
    width = w_out.shape[0]
    sub = rows // 4
    plane_of = (0, 2, 1, 3)
    crop = (level % 2) * 2 + level // 2

    def over_x(v):
        return lax.ppermute(v, "crop", [(g, g ^ 1) for g in range(4)])

    def over_y(v):
        return lax.ppermute(v, "crop", [(g, g ^ 2) for g in range(4)])

    def over_both(v):
        return lax.ppermute(v, "crop", [(g, g ^ 3) for g in range(4)])

    def over_core(v):
        return lax.ppermute(v, "col", [(0, 1), (1, 0)])

    own_mask = residue_mask[0]
    row_own = lax.dynamic_slice_in_dim(own_mask, rows * level, rows)
    col_own = lax.dynamic_slice_in_dim(own_mask, cols * side, cols)
    code_own = jnp.where((row_own[:, None] * col_own[None, :]) > 0, dist_bins[0], -1).astype(BF16)

    wave0, wave1, wave0_x, wave0_y, left_own, right_own, proj_w, *weights, ln_wide, bias_wide = spread(
        pair_acts[0], code_own, w_in, w_out, w_t1, w_t2, w_dist, norm_params, dist_bias
    )
    og_T, out_T, out_w, t1_T, t1_w, t2_T, t2_w, dist_T, dist_w = weights
    weights = (out_T, out_w, og_T, t1_T, t1_w, t2_T, t2_w, dist_T, dist_w)

    count = jnp.sum(own_mask).astype(F32)
    share_count = lax.axis_size("row") * lax.axis_size("col")
    acts, left, right = {}, {}, {}

    def share(q, source, shift, half):
        acts[q, half] = shift(acts[source, half])

    def values(q, half, *earlier):
        left[q, half], right[q, half] = project(after(acts[q, half], *earlier), proj_w, ln_wide)
        return right[q, half]

    acts[0, 0], acts[0, 1], acts[1, 0], acts[2, 0] = wave0, wave1, wave0_x, wave0_y
    share(1, 0, over_x, 1)
    share(2, 0, over_y, 1)
    left[0, 0], right[0, 0] = left_own, right_own
    done = values(0, 1)

    ids = jnp.stack([spot, crop, side]).astype(jnp.int32)
    def values_two(one, two, *earlier):
        results = project_two(after(acts[one], *earlier), acts[two], proj_w, ln_wide)
        left[one], right[one], left[two], right[two] = results
        return results[0]

    keeps, recvs, dx_own, dx_other, seen, seen_other = {}, {}, {}, {}, {}, {}
    sums = []

    def forward(q, *earlier):
        keeps[q], send = triangle(
            q, after(ids, *earlier), [left[0, h] for h in range(2)], [right[q, h] for h in range(2)]
        )
        recvs[q] = over_core(send)
        return send

    def middle(q, *earlier):
        dx_own[q], *sums[:] = pair_block(
            q, after(ids, *earlier), keeps[q], recvs[q], acts_kj, ln_wide, weights, bias_wide, list(sums), q == 3
        )
        dx_other[q] = over_core(dx_own[q])
        seen[q] = (lambda v: v, over_x, over_y, over_both)[q](dx_own[q])
        seen_other[q] = over_core(seen[q]) if q in (1, 2) else dx_other[q]
        return dx_own[q]

    done = forward(0, done)
    acts_kj = turn(after(acts[0, 0], done), acts[0, 1])
    done = values_two((1, 0), (2, 0), acts_kj)
    done = middle(0, done)
    acts[1, 1], acts[2, 1] = after(acts[1, 1], done), after(acts[2, 1], done)
    acts[3, 0] = over_y(after(acts[1, 0], done))
    acts[3, 1] = over_x(acts[2, 1])
    done = values(1, 1, done)
    done = forward(1, done)
    done = values(2, 1, done)
    done = forward(2, done)
    done = middle(1, done)
    done = middle(2, done)
    done = values_two((3, 0), (3, 1), done)
    done = forward(3, done)
    done = middle(3, done, seen[1], seen[2])
    d_left = left_back(
        after(ids, done, seen_other[1]),
        [dx_own[q] for q in range(4)],
        [dx_other[q] for q in range(4)],
        [right[q, 0] for q in range(4)],
        [right[q, 1] for q in range(4)],
    )
    pair_sums = sums[0].at[LOSS_ROW - 1, 127].set(count * count / share_count)
    left_sum = []
    for h in range(2):
        left_sum = input_back([(acts[0, h], d_left[h])], 0, proj_w, ln_wide, left_sum, h == 1)
        if h == 0:
            seen_other[3] = over_core(after(seen[3], left_sum[0]))
    d_right = right_back(
        after(ids, left_sum[0], seen_other[2]),
        [seen[q] for q in range(4)],
        [seen_other[q] for q in range(4)],
        [left[q, 0] for q in range(4)],
        [left[q, 1] for q in range(4)],
    )
    right_sum = input_back([(acts[0, h], d_right[h]) for h in range(2)], 1, proj_w, ln_wide, [], True)
    params = (w_in, w_out, w_t1, w_t2, w_dist, norm_params, dist_bias)
    return update(reduce_all(pair_sums, left_sum[0], right_sum[0]), params, firsts, seconds)


def solution(mesh):
    planes = mesh.shape["crop"] == 4 and mesh.shape["row"] == 4 and mesh.shape["col"] == 2
    body = on_device_planes if planes else on_device_general
    in_specs = (
        P("crop", "row", "col", None),
        P("crop", None),
        P("crop", "row", "col"),
    ) + (P(),) * 21
    return jax.shard_map(
        body, mesh=mesh, in_specs=in_specs, out_specs=(P(),) * 24, check_vma=False
    )
```

```python
import functools

import jax
import jax.numpy as jnp
from jax import lax
from jax.experimental import pallas as pl
from jax.experimental.pallas import tpu as pltpu
from jax.sharding import PartitionSpec as P

STEP = 10


NORM_EPS = 1e-05
CLIP_NORM = 0.02
LEARN_RATE = 0.03
GAIN_RATE = 0.3
BETA_ONE = 0.9
BETA_TWO = 0.999
ADAM_EPS = 1e-08
WEIGHT_DECAY = 0.01


def standardize(values):
    center = values - jnp.mean(values, -1, keepdims=True)
    rstd = lax.rsqrt(jnp.mean(center * center, -1, keepdims=True) + NORM_EPS)
    return (center * rstd, rstd)


def standard_back(grad, normed, rstd):
    return rstd * (
        grad
        - jnp.mean(grad, -1, keepdims=True)
        - normed * jnp.mean(grad * normed, -1, keepdims=True)
    )


def linear(values, weight):
    return jnp.einsum("ijc,cd->ijd", values, weight, preferred_element_type=jnp.float32)


def weight_grad(values, grad):
    return jnp.einsum("ijc,ijd->cd", values, grad, preferred_element_type=jnp.float32)


def transposed(grad, weight):
    return jnp.einsum("ijd,cd->ijc", grad, weight, preferred_element_type=jnp.float32)


def adamw_update(weight, first, second, grad, scale, rate):
    clipped = grad * scale
    first_new = BETA_ONE * first + (1.0 - BETA_ONE) * clipped
    second_new = BETA_TWO * second + (1.0 - BETA_TWO) * clipped * clipped
    first_hat = first_new / (1.0 - BETA_ONE**STEP)
    second_hat = second_new / (1.0 - BETA_TWO**STEP)
    stepped = weight - rate * (
        first_hat / (jnp.sqrt(second_hat) + ADAM_EPS) + WEIGHT_DECAY * weight
    )
    return (stepped, first_new, second_new)


def on_device_general(
    pair_acts,
    residue_mask,
    dist_bins,
    w_in,
    w_out,
    w_t1,
    w_t2,
    w_dist,
    norm_params,
    dist_bias,
    m_in,
    m_out,
    m_t1,
    m_t2,
    m_dist,
    m_norm,
    m_bias,
    v_in,
    v_out,
    v_t1,
    v_t2,
    v_dist,
    v_norm,
    v_bias,
):
    tile_rows = pair_acts.shape[1]
    tile_cols = pair_acts.shape[2]
    width = w_out.shape[0]
    row_first = lax.axis_index("row") * tile_rows
    col_first = lax.axis_index("col") * tile_cols
    mask_vals = residue_mask[0].astype(jnp.float32)
    row_mask = lax.dynamic_slice_in_dim(mask_vals, row_first, tile_rows)
    col_mask = lax.dynamic_slice_in_dim(mask_vals, col_first, tile_cols)
    pair_mask = row_mask[:, None] * col_mask[None, :]
    mask_cube = pair_mask[..., None]
    pair_total = lax.psum(jnp.sum(pair_mask), ("crop", "row", "col"))
    low_in, low_out, low_t1, low_t2, low_dist = [
        weight.astype(jnp.bfloat16) for weight in (w_in, w_out, w_t1, w_t2, w_dist)
    ]
    acts = pair_acts[0].astype(jnp.float32)
    normed_one, rstd_one = standardize(acts)
    pair_norm = (normed_one * norm_params[0] + norm_params[1]).astype(jnp.bfloat16)
    projected = linear(pair_norm, low_in)
    left_proj = projected[..., :width]
    left_sig = jax.nn.sigmoid(projected[..., width : 2 * width])
    right_proj = projected[..., 2 * width : 3 * width]
    right_sig = jax.nn.sigmoid(projected[..., 3 * width : 4 * width])
    gate_sig = jax.nn.sigmoid(projected[..., 4 * width :])
    left_vals = (mask_cube * left_sig * left_proj).astype(jnp.bfloat16)
    right_vals = (mask_cube * right_sig * right_proj).astype(jnp.bfloat16)
    strips = lax.all_gather(right_vals, "row", axis=0, tiled=True)
    piece = strips
    triangle = jnp.transpose(
        lax.psum_scatter(
            jnp.einsum("jkc,ikc->jic", piece, left_vals, preferred_element_type=jnp.float32),
            "col",
            scatter_dimension=0,
            tiled=True,
        ),
        (1, 0, 2),
    )
    normed_two, rstd_two = standardize(triangle)
    tri_norm = (normed_two * norm_params[2] + norm_params[3]).astype(jnp.bfloat16)
    out_proj = linear(tri_norm, low_out)
    updated = acts + gate_sig * out_proj
    normed_three, rstd_three = standardize(updated)
    trans_in = (normed_three * norm_params[4] + norm_params[5]).astype(jnp.bfloat16)
    pre_act = linear(trans_in, low_t1)
    hidden = jax.nn.silu(pre_act).astype(jnp.bfloat16)
    final = updated + linear(hidden, low_t2)
    final_low = final.astype(jnp.bfloat16)
    logits = linear(final_low, low_dist) + dist_bias
    log_total = jax.nn.logsumexp(logits, -1)
    onehot = (dist_bins[0][..., None] == jnp.arange(w_dist.shape[1])).astype(jnp.float32)
    loss_local = jnp.sum(pair_mask * (log_total - jnp.sum(logits * onehot, -1)))
    d_logits = (mask_cube * (jnp.exp(logits - log_total[..., None]) - onehot) / pair_total).astype(
        jnp.bfloat16
    )
    grad_dist = weight_grad(final_low, d_logits)
    grad_bias = jnp.sum(d_logits.astype(jnp.float32), (0, 1))
    d_final = transposed(d_logits, low_dist)
    d_trans = d_final.astype(jnp.bfloat16)
    grad_t2 = weight_grad(hidden, d_trans)
    d_hidden = transposed(d_trans, low_t2)
    sig_pre = jax.nn.sigmoid(pre_act)
    d_pre = (d_hidden * sig_pre * (1.0 + pre_act * (1.0 - sig_pre))).astype(jnp.bfloat16)
    grad_t1 = weight_grad(trans_in, d_pre)
    d_trans_in = transposed(d_pre, low_t1)
    d_updated = d_final + standard_back(d_trans_in * norm_params[4], normed_three, rstd_three)
    d_out = (d_updated * gate_sig).astype(jnp.bfloat16)
    d_out_gate = d_updated * out_proj * gate_sig * (1.0 - gate_sig)
    grad_out = weight_grad(tri_norm, d_out)
    d_tri_norm = transposed(d_out, low_out)
    d_triangle = standard_back(d_tri_norm * norm_params[2], normed_two, rstd_two).astype(
        jnp.bfloat16
    )
    d_rows = lax.all_gather(d_triangle, "col", axis=1, tiled=True)
    d_left = jnp.einsum("ijc,jkc->ikc", d_rows, strips, preferred_element_type=jnp.float32)
    piece = d_rows
    d_right = lax.psum_scatter(
        jnp.einsum("ijc,ikc->jkc", piece, left_vals, preferred_element_type=jnp.float32).astype(
            jnp.bfloat16
        ),
        "row",
        scatter_dimension=0,
        tiled=True,
    ).astype(jnp.float32)
    d_proj = jnp.concatenate(
        [
            d_left * mask_cube * left_sig,
            d_left * mask_cube * left_proj * left_sig * (1.0 - left_sig),
            d_right * mask_cube * right_sig,
            d_right * mask_cube * right_proj * right_sig * (1.0 - right_sig),
            d_out_gate,
        ],
        -1,
    ).astype(jnp.bfloat16)
    grad_in = weight_grad(pair_norm, d_proj)
    d_pair_norm = transposed(d_proj, low_in)
    grad_norms = jnp.stack(
        [
            jnp.sum(d_pair_norm * normed_one, (0, 1)),
            jnp.sum(d_pair_norm, (0, 1)),
            jnp.sum(d_tri_norm * normed_two, (0, 1)),
            jnp.sum(d_tri_norm, (0, 1)),
            jnp.sum(d_trans_in * normed_three, (0, 1)),
            jnp.sum(d_trans_in, (0, 1)),
        ]
    )
    summed = lax.psum(
        (grad_in, grad_out, grad_t1, grad_t2, grad_dist, grad_norms, grad_bias, loss_local),
        ("crop", "row", "col"),
    )
    grads = summed[:7]
    squares = jnp.zeros((), jnp.float32)
    for grad in grads:
        squares = squares + jnp.sum(grad * grad)
    grad_norm = jnp.sqrt(squares)
    scale = CLIP_NORM / jnp.maximum(grad_norm, CLIP_NORM)
    params = (w_in, w_out, w_t1, w_t2, w_dist, norm_params, dist_bias)
    firsts = (m_in, m_out, m_t1, m_t2, m_dist, m_norm, m_bias)
    seconds = (v_in, v_out, v_t1, v_t2, v_dist, v_norm, v_bias)
    rates = (LEARN_RATE, LEARN_RATE, LEARN_RATE, LEARN_RATE, LEARN_RATE, GAIN_RATE, GAIN_RATE)
    results = [
        adamw_update(
            params[index], firsts[index], seconds[index], grads[index], scale, rates[index]
        )
        for index in range(7)
    ]
    return (
        results[0][0],
        results[1][0],
        results[2][0],
        results[3][0],
        results[4][0],
        results[5][0],
        results[6][0],
        results[0][1],
        results[1][1],
        results[2][1],
        results[3][1],
        results[4][1],
        results[5][1],
        results[6][1],
        results[0][2],
        results[1][2],
        results[2][2],
        results[3][2],
        results[4][2],
        results[5][2],
        results[6][2],
        summed[7],
        pair_total,
        grad_norm,
    )


F32 = jnp.float32
BF16 = jnp.bfloat16
NT = (((1,), (1,)), ((), ()))
NN = (((1,), (0,)), ((), ()))
TN = (((0,), (0,)), ((), ()))
MICRO = 1e3
VMEM_LIMIT = 56 * 1024 * 1024


def dot(left, right, dims=NN):
    return lax.dot_general(left, right, dims, preferred_element_type=F32)


def column_stats(values):
    center = values - jnp.mean(values, 0, keepdims=True)
    rstd = lax.rsqrt(jnp.mean(center * center, 0, keepdims=True) + NORM_EPS)
    return center * rstd, rstd


def column_back(grad, normed, rstd):
    return rstd * (
        grad
        - jnp.mean(grad, 0, keepdims=True)
        - normed * jnp.mean(grad * normed, 0, keepdims=True)
    )


def widen(param, lanes):
    return jnp.concatenate([param] * (lanes // param.shape[1]), 1)


def spread_rows(scratch, block):
    scratch[...] = jnp.swapaxes(block, 0, 1).astype(scratch.dtype)


def take_rows(scratch, start, count):
    return jnp.concatenate([scratch[start + u] for u in range(count)], 1).astype(F32)


def put_rows(scratch, start, count, values):
    lanes = values.shape[1] // count
    for u in range(count):
        scratch[start + u] = values[:, u * lanes : (u + 1) * lanes].astype(scratch.dtype)


def gather_rows(scratch, out_ref):
    out_ref[...] = jnp.swapaxes(scratch[...], 0, 1)


def call(kernel, grid, scalars, ins, outs, scratch, flops, name, aliases=None):
    return pl.pallas_call(
        kernel,
        grid_spec=pltpu.PrefetchScalarGridSpec(
            num_scalar_prefetch=len(scalars),
            grid=grid,
            in_specs=[pl.BlockSpec(block, index) for _, block, index in ins],
            out_specs=[pl.BlockSpec(block, index) for _, _, block, index in outs],
            scratch_shapes=scratch,
        ),
        out_shape=[jax.ShapeDtypeStruct(shape, dtype) for shape, dtype, _, _ in outs],
        compiler_params=pltpu.CompilerParams(vmem_limit_bytes=VMEM_LIMIT),
        cost_estimate=pl.CostEstimate(flops=int(flops), bytes_accessed=1, transcendentals=0),
        name=name,
        input_output_aliases=aliases or {},
    )(*scalars, *[a for a, _, _ in ins])


def code_rows(code_s, start, count):
    return jnp.concatenate([code_s[pl.ds(start + u, 1), :] for u in range(count)], 1)


def present_rows(code_s, start, count):
    return jnp.where(code_rows(code_s, start, count) < 0.0, 0.0, 1.0)


ROWS = 16
PROJECT_GROUP = 8
INPUT_GROUP = 16


def prepare_weights(w_in, w_out, w_t1, w_t2, w_dist, norms, bias, outs):
    projT, ogT, outT, out_w, t1T, t1, t2T, t2, distT, dist, ln_ref, bias_ref = outs
    count, chans = projT.shape
    projT[...] = (0.5 * jnp.transpose(w_in[:, :count])).astype(BF16)
    ogT[...] = (0.5 * jnp.transpose(w_in[:, count:])).astype(BF16)
    for weight, plain, turned, plain_scale, turned_scale in (
        (w_out, out_w, outT, 1.0, 1.0),
        (w_t1, t1, t1T, 1.0, 0.5),
        (w_t2, t2, t2T, 0.5, 1.0),
        (w_dist, distT, dist, 1.0, 1.0),
    ):
        plain[...] = (plain_scale * weight[...]).astype(BF16)
        turned[...] = (turned_scale * jnp.transpose(weight[...])).astype(BF16)
    for index in range(6):
        ln_ref[index] = jnp.transpose(jnp.broadcast_to(norms[index : index + 1, :], (128, chans)))
    bias_ref[...] = jnp.transpose(jnp.broadcast_to(bias[...], (128, bias.shape[1])))


def project_kernel(acts_ref, code_ref, w_ref, ln_ref, a_ref, b_ref, acts_s, a_s, b_s, code_s):
    width = a_ref.shape[0]
    code_s[...] = code_ref[0].astype(F32)
    spread_rows(acts_s, acts_ref[...])

    def some(step, carry):
        start = step * PROJECT_GROUP
        values = take_rows(acts_s, start, PROJECT_GROUP)
        lanes = values.shape[1]
        normed, _ = column_stats(values)
        low = normed * widen(ln_ref[0], lanes) + widen(ln_ref[1], lanes)
        low = (low * present_rows(code_s, start, PROJECT_GROUP)).astype(BF16)
        proj = dot(w_ref[...], low)
        left = proj[:width] * (jnp.tanh(proj[width : 2 * width]) + 1.0)
        right = proj[2 * width : 3 * width] * (jnp.tanh(proj[3 * width :]) + 1.0)
        put_rows(a_s, start, PROJECT_GROUP, left)
        put_rows(b_s, start, PROJECT_GROUP, right)
        return carry

    lax.fori_loop(0, ROWS // PROJECT_GROUP, some, 0)
    gather_rows(a_s, a_ref)
    gather_rows(b_s, b_ref)


def project_two_kernel(acts0, code0, acts1, code1, w_ref, ln_ref, a0, b0, a1, b1, *scratch):
    steps = pl.num_programs(0) // 2

    @pl.when(pl.program_id(0) < steps)
    def _():
        project_kernel(acts0, code0, w_ref, ln_ref, a0, b0, *scratch)

    @pl.when(pl.program_id(0) >= steps)
    def _():
        project_kernel(acts1, code1, w_ref, ln_ref, a1, b1, *scratch)


def project_two(first, second, w_proj, ln_wide):
    chans, rows, lanes = first.shape[0] - 1, first.shape[1], first.shape[2]
    block = (chans, ROWS, lanes)
    steps = rows // ROWS
    spots = [lambda i: jnp.minimum(i, steps - 1), lambda i: jnp.maximum(i - steps, 0)]
    staged = pltpu.VMEM((ROWS, chans, lanes), BF16)
    ins, outs = [], []
    for acts, spot in zip((first, second), spots):
        ins.append((acts, block, lambda i, *_, spot=spot: (0, spot(i), 0)))
        ins.append((acts, (1, ROWS, lanes), lambda i, *_, spot=spot: (chans, spot(i), 0)))
        outs += [((chans, rows, lanes), BF16, block, lambda i, *_, spot=spot: (0, spot(i), 0))] * 2
    return call(
        project_two_kernel,
        (2 * steps,),
        [],
        ins + [(w_proj, w_proj.shape, fixed(0, 0)), (ln_wide, ln_wide.shape, fixed(0, 0, 0))],
        outs,
        [staged, staged, staged, pltpu.VMEM((ROWS, lanes), F32)],
        30 * MICRO,
        "project_two",
    )


def fixed(*zeros):
    return lambda i, *_: zeros


def project(acts, w_proj, ln_wide):
    chans, rows, lanes = acts.shape[0] - 1, acts.shape[1], acts.shape[2]
    block = (chans, ROWS, lanes)
    mid = lambda i, *_: (0, i, 0)
    out = ((chans, rows, lanes), BF16, block, mid)
    staged = pltpu.VMEM((ROWS, chans, lanes), BF16)
    return call(
        project_kernel,
        (rows // ROWS,),
        [],
        [
            (acts, block, mid),
            (acts, (1, ROWS, lanes), lambda i, *_: (chans, i, 0)),
            (w_proj, w_proj.shape, fixed(0, 0)),
            (ln_wide, ln_wide.shape, fixed(0, 0, 0)),
        ],
        [out, out],
        [staged, staged, staged, pltpu.VMEM((ROWS, lanes), F32)],
        15 * MICRO,
        "project",
    )


CHANS = 16
TRIANGLE_CHANS = 32


def ordered(flag, own, other):
    part = own.shape[0] // 2
    waves = []
    for wave in range(2):
        mine, rest = own[wave * part : (wave + 1) * part], other[wave * part : (wave + 1) * part]
        waves += [jnp.where(flag, mine, rest), jnp.where(flag, rest, mine)]
    return jnp.concatenate(waves, 0)


def kept_first(ids, q):
    return ids[2] ^ ((ids[0] ^ q) // 2) ^ (ids[1] // 2) == 0


def triangle_kernel(q, ids, a0, a1, b0, b1, keep_ref, send_ref):
    first = kept_first(ids, q)
    part = b0.shape[1] // 2
    for chan in range(TRIANGLE_CHANS):
        rows = jnp.concatenate([a0[chan], a1[chan]], 0)
        x = dot(jnp.concatenate([b0[chan], b1[chan]], 0), rows, NT)
        one = jnp.concatenate([x[:part], x[2 * part : 3 * part]], 0)
        two = jnp.concatenate([x[part : 2 * part], x[3 * part :]], 0)
        keep_ref[chan] = jnp.where(first, one, two)
        send_ref[chan] = jnp.where(first, two, one).astype(BF16)


def triangle(q, ids, a, b):
    chans, half, lanes = a[0].shape
    lead = lambda i, *_: (i, 0, 0)
    block = (TRIANGLE_CHANS, half, lanes)
    out = (chans, half, 2 * half)
    return call(
        functools.partial(triangle_kernel, q),
        (chans // TRIANGLE_CHANS,),
        [ids],
        [(v, block, lead) for v in (*a, *b)],
        [(out, F32, (TRIANGLE_CHANS, half, 2 * half), lead), (out, BF16, (TRIANGLE_CHANS, half, 2 * half), lead)],
        [],
        14 * MICRO,
        "triangle",
    )


GROUP = 16


T1_ROW, T2_ROW, OUT_ROW, OG_ROW, DIST_ROW, NORM_ROW, BIAS_ROW, LOSS_ROW, SUM_ROWS = (
    0, 512, 1024, 1152, 1280, 1344, 1350, 1351, 1352,
)


def row_sums(values):
    return jnp.sum(jnp.transpose(values), 0, keepdims=True)


def pair_kernel(
    first_call, last_call,
    ids, x_keep, x_recv, acts_ref, code_ref, ln_ref, w_outT, w_out, w_ogT, w_t1T, w_t1,
    w_t2T, w_t2, w_distT, w_dist, bias_ref, *rest,
):
    prior = () if first_call else rest[:2]
    dx_ref, sums, wide, x_s, acts_s, dx_s, code_s = rest[len(prior) :]
    chans = acts_ref.shape[0]
    lanes = 128 * GROUP
    bins = w_distT.shape[0]
    hidden_width = w_t1T.shape[0]

    @pl.when(pl.program_id(0) == 0)
    def _():
        if first_call:
            sums[...] = jnp.zeros_like(sums)
            wide[...] = jnp.zeros_like(wide)
        else:
            sums[...] = prior[0][...]
            wide[...] = prior[1][...]

    spread_rows(x_s, x_keep[...] + x_recv[...].astype(F32))
    spread_rows(acts_s, acts_ref[...])
    code_s[...] = code_ref[0].astype(F32)
    param = [widen(ln_ref[index], lanes) for index in range(6)]
    bin_index = lax.broadcasted_iota(jnp.int32, (bins, lanes), 0).astype(F32)

    def fold(values):
        return sum(values[:, 128 * part : 128 * part + 128] for part in range(GROUP))

    def add(row, values):
        sums[row : row + values.shape[0]] += values

    def group(step, carry):
        first = step * GROUP
        x = take_rows(x_s, first, GROUP)
        acts = take_rows(acts_s, first, GROUP)
        code = code_rows(code_s, first, GROUP)
        normed_two, rstd_two = column_stats(x)
        tri = (normed_two * param[2] + param[3]).astype(BF16)
        out = dot(w_outT[...], tri)
        normed_one, _ = column_stats(acts)
        low = (normed_one * param[0] + param[1]).astype(BF16)
        gate = 0.5 * jnp.tanh(dot(w_ogT[...], low)) + 0.5
        z1 = acts + gate * out
        normed_three, rstd_three = column_stats(z1)
        trans = (normed_three * param[4] + param[5]).astype(BF16)
        pre = dot(w_t1T[...], trans)
        tanh = jnp.tanh(pre)
        bent = pre * tanh
        hidden = (pre + bent).astype(BF16)
        slope = (1.0 + tanh) * (1.0 + (pre - bent))
        final = (z1 + dot(w_t2T[...], hidden)).astype(BF16)
        logits = dot(w_distT[...], final) + widen(bias_ref[...], lanes)
        top = jnp.max(logits, 0, keepdims=True)
        powers = jnp.exp(logits - top)
        total = jnp.sum(powers, 0, keepdims=True)
        present = jnp.where(code < 0.0, 0.0, 1.0)
        hot = bin_index == code
        picked = jnp.sum(jnp.where(hot, logits, 0.0), 0, keepdims=True)
        sums[LOSS_ROW : LOSS_ROW + 1] += fold(present * (jnp.log(total) + top) - picked)
        d_logits = (powers * (present / total) - jnp.where(hot, 1.0, 0.0)).astype(BF16)
        add(DIST_ROW, dot(d_logits, final, NT))
        wide[5, :bins] += fold(d_logits.astype(F32))
        d_final = dot(w_dist[...], d_logits)
        d_trans = d_final.astype(BF16)
        add(T2_ROW, dot(hidden, d_trans, NT))
        d_pre = (dot(w_t2[...], d_trans) * slope).astype(BF16)
        add(T1_ROW, dot(d_pre, trans, NT))
        d_tn = dot(w_t1[...], d_pre)
        wide[2] += fold(d_tn * normed_three)
        wide[3] += fold(d_tn)
        d_z1 = d_final + column_back(d_tn * param[4], normed_three, rstd_three)
        d_gated = d_z1 * gate
        d_out = d_gated.astype(BF16)
        d_og = (d_gated * out * (1.0 - gate)).astype(BF16)
        add(OUT_ROW, dot(d_out, tri, NT))
        g_og = dot(d_og, jnp.concatenate([low, normed_one.astype(BF16)], 0), NT)
        add(OG_ROW, g_og[:, :chans])
        wide[6] += g_og[:, chans:]
        wide[4] += fold(d_og.astype(F32))
        d_xn = dot(w_out[...], d_out)
        wide[0] += fold(d_xn * normed_two)
        wide[1] += fold(d_xn)
        d_x = column_back(d_xn * param[2], normed_two, rstd_two)
        put_rows(dx_s, first, GROUP, d_x)
        return carry

    lax.fori_loop(0, ROWS // GROUP, group, 0)
    gather_rows(dx_s, dx_ref)

    if last_call:

        @pl.when(pl.program_id(0) == pl.num_programs(0) - 1)
        def _():
            gate_w = 2.0 * w_ogT[...].astype(F32)
            for index in range(4):
                add(NORM_ROW + index, row_sums(wide[index]))
            total = jnp.sum(wide[4], 1, keepdims=True)
            add(NORM_ROW + 4, jnp.sum(gate_w * wide[6], 0, keepdims=True))
            add(NORM_ROW + 5, jnp.sum(gate_w * total, 0, keepdims=True))
            add(BIAS_ROW, row_sums(wide[5]))


def pair_block(q, ids, x_keep, x_recv, acts_kj, ln_wide, weights, bias, prior, last_call):
    chans, rows, lanes = x_keep.shape
    block = (chans, ROWS, lanes)
    mid = lambda i, *_: (0, i, 0)

    def where(i, ids):
        owner = ids[0] ^ q
        return 8 * ((i % 2) ^ (owner % 2) ^ (ids[1] % 2)) + 2 * owner + i // 2

    full = [(w, w.shape, fixed(*([0] * w.ndim))) for w in (ln_wide, *weights, bias, *prior)]
    shapes = [(SUM_ROWS, 128), (7, 128, 128)]
    return call(
        functools.partial(pair_kernel, not prior, last_call),
        (rows // ROWS,),
        [ids],
        [
            (x_keep, block, mid),
            (x_recv, block, mid),
            (acts_kj, block, lambda i, ids: (0, where(i, ids), 0)),
            (acts_kj, (1, ROWS, lanes), lambda i, ids: (chans, where(i, ids), 0)),
        ]
        + full,
        [((chans, rows, lanes), BF16, block, mid)]
        + [(s, F32, s, fixed(*([0] * len(s)))) for s in shapes],
        [pltpu.VMEM((ROWS, chans, lanes), t) for t in (F32, BF16, BF16)] + [pltpu.VMEM((ROWS, lanes), F32)],
        35 * MICRO,
        "pair",
    )


def right_back_kernel(ids, *refs):
    owns, others, firsts, seconds = refs[:4], refs[4:8], refs[8:12], refs[12:16]
    out0, out1 = refs[16:]
    half = out0.shape[1]
    own_first = kept_first(ids, 0)
    for chan in range(CHANS):
        grads = jnp.concatenate(
            [ordered(own_first, owns[q][chan], others[q][chan]) for q in range(4)], 1
        )
        values = jnp.concatenate([v[q][chan] for q in range(4) for v in (firsts, seconds)], 0)
        total = dot(grads, values).astype(BF16)
        out0[chan] = total[:half]
        out1[chan] = total[half:]


def right_back(ids, owns, others, firsts, seconds):
    chans, half, lanes = firsts[0].shape
    lead = lambda i, *_: (i, 0, 0)
    out = ((chans, half, lanes), BF16, (CHANS, half, lanes), lead)
    return call(
        right_back_kernel,
        (chans // CHANS,),
        [ids],
        [(v, (CHANS, half, 2 * half), lead) for v in (*owns, *others)]
        + [(v, (CHANS, half, lanes), lead) for v in (*firsts, *seconds)],
        [out, out],
        [],
        25 * MICRO,
        "right_back",
    )


def turn_kernel(first, second, out_ref):
    for chan in range(first.shape[0]):
        out_ref[chan] = jnp.transpose(jnp.concatenate([first[chan], second[chan]], 0))


def turn(first, second):
    chans, half, lanes = first.shape
    lead = lambda i, *_: (i, 0, 0)
    count = next(n for n in (43, 16, 8, 4, 2, 1) if chans % n == 0)
    block = (count, half, lanes)
    return call(
        turn_kernel,
        (chans // count,),
        [],
        [(first, block, lead), (second, block, lead)],
        [((chans, lanes, 2 * half), BF16, (count, lanes, 2 * half), lead)],
        [],
        12 * MICRO,
        "turn",
    )[0]


def left_back_kernel(ids, *refs):
    owns, others, firsts, seconds = refs[:4], refs[4:8], refs[8:12], refs[12:16]
    out0, out1 = refs[16:]
    half = out0.shape[1]
    for chan in range(CHANS):
        total = None
        for pair in range(2):
            own_first = kept_first(ids, 2 * pair)
            grads, values = [], []
            for q in (2 * pair, 2 * pair + 1):
                grads.append(ordered(own_first, owns[q][chan], others[q][chan]))
                values += [firsts[q][chan], seconds[q][chan]]
            term = dot(jnp.concatenate(grads, 0), jnp.concatenate(values, 0), TN)
            total = term if total is None else total + term
        total = total.astype(BF16)
        out0[chan] = total[:half]
        out1[chan] = total[half:]


def left_back(ids, owns, others, firsts, seconds):
    chans, half, lanes = firsts[0].shape
    lead = lambda i, *_: (i, 0, 0)
    out = ((chans, half, lanes), BF16, (CHANS, half, lanes), lead)
    return call(
        left_back_kernel,
        (chans // CHANS,),
        [ids],
        [(v, (CHANS, half, 2 * half), lead) for v in (*owns, *others)]
        + [(v, (CHANS, half, lanes), lead) for v in (*firsts, *seconds)],
        [out, out],
        [],
        25 * MICRO,
        "left_back",
    )


SIDE_ROWS = 272


def affine_grad(normed_grad, total, ln_ref):
    gain, shift = jnp.transpose(ln_ref[0])[:1], jnp.transpose(ln_ref[1])[:1]
    return normed_grad * gain + total * shift


def input_back_kernel(count, first_call, last_call, w_ref, ln_ref, *rest):
    halves, rest = [rest[3 * n : 3 * n + 3] for n in range(count)], rest[3 * count :]
    prior = () if first_call else rest[:3]
    out_ref, g_ref, sum_ref, acts_s, grad_s, code_s = rest[len(prior) :]
    width = halves[0][2].shape[0]

    @pl.when(pl.program_id(0) == 0)
    def _():
        if first_call:
            out_ref[...] = jnp.zeros_like(out_ref)
            g_ref[...] = jnp.zeros_like(g_ref)
            sum_ref[...] = jnp.zeros_like(sum_ref)
        else:
            out_ref[...] = prior[0][...]
            g_ref[...] = prior[1][...]
            sum_ref[...] = prior[2][...]

    steps = pl.num_programs(0) // count
    for number, (acts_ref, code_ref, grad_ref) in enumerate(halves):

        @pl.when(pl.program_id(0) // steps == number)
        def _(acts_ref=acts_ref, code_ref=code_ref, grad_ref=grad_ref):
            code_s[...] = code_ref[0].astype(F32)
            spread_rows(acts_s, acts_ref[...])
            spread_rows(grad_s, grad_ref[...])

    def some(step, carry):
        start = step * INPUT_GROUP
        values = take_rows(acts_s, start, INPUT_GROUP)
        lanes = values.shape[1]
        normed, _ = column_stats(values)
        low = (normed * widen(ln_ref[0], lanes) + widen(ln_ref[1], lanes)).astype(BF16)
        proj = dot(w_ref[...], low)
        tanh = jnp.tanh(proj[width:])
        d_half = take_rows(grad_s, start, INPUT_GROUP) * (0.5 * present_rows(code_s, start, INPUT_GROUP))
        d_tanh = d_half * tanh
        d_value = d_half + d_tanh
        d_gate = proj[:width] * (d_half - d_tanh * tanh)
        d_proj = jnp.concatenate([d_value.astype(BF16), d_gate.astype(BF16)], 0)
        g_ref[...] += dot(d_proj, normed.astype(BF16), NT)
        for first, part in ((0, d_value), (width, d_gate)):
            sum_ref[first : first + width] += sum(
                part[:, 128 * u : 128 * u + 128] for u in range(lanes // 128)
            )
        return carry

    lax.fori_loop(0, ROWS // INPUT_GROUP, some, 0)

    if last_call:

        @pl.when(pl.program_id(0) == pl.num_programs(0) - 1)
        def _():
            part = 2.0 * w_ref[...].astype(F32)
            total = jnp.sum(sum_ref[...], 1, keepdims=True)
            gain = jnp.sum(part * g_ref[...], 0, keepdims=True)
            shift = jnp.sum(part * total, 0, keepdims=True)
            out_ref[: 2 * width] = affine_grad(g_ref[...], total, ln_ref)
            out_ref[2 * width : 2 * width + 1] = gain
            out_ref[2 * width + 1 : 2 * width + 2] = shift


def input_back(halves, part, w_proj, ln_wide, prior, last_call):
    chans, rows, lanes = halves[0][1].shape
    block = (chans, ROWS, lanes)
    steps = rows // ROWS
    depth = w_proj.shape[0] // 2
    shapes = [(SIDE_ROWS, chans), (depth, chans), (depth, 128)]
    ins = []
    for number, (acts, grad) in enumerate(halves):
        spot = lambda i, number=number: jnp.clip(i - number * steps, 0, steps - 1)
        mid = lambda i, *_, spot=spot: (0, spot(i), 0)
        ins += [
            (acts, block, mid),
            (acts, (1, ROWS, lanes), lambda i, *_, spot=spot: (chans, spot(i), 0)),
            (grad, block, mid),
        ]
    return call(
        functools.partial(input_back_kernel, len(halves), not prior, last_call),
        (len(halves) * steps,),
        [],
        [(w_proj, (depth, chans), fixed(part, 0)), (ln_wide, ln_wide.shape, fixed(0, 0, 0))]
        + ins
        + [(v, v.shape, fixed(0, 0)) for v in prior],
        [(s, F32, s, fixed(0, 0)) for s in shapes],
        [
            pltpu.VMEM((ROWS, chans, lanes), BF16),
            pltpu.VMEM((ROWS, chans, lanes), BF16),
            pltpu.VMEM((ROWS, lanes), F32),
        ],
        16 * MICRO,
        "input_back",
    )


def reduce_kernel(share_ref, pair_ref, left_ref, right_ref, out_ref, full_s, core_s, crop_s, row_s, send, recv):
    side, spot, level = lax.axis_index("col"), lax.axis_index("crop"), lax.axis_index("row")
    mesh_id = pl.DeviceIdType.MESH
    sibling = {"col": 1 - side}
    crops = [{"crop": lax.rem(spot + n, 4)} for n in range(1, 4)]
    levels = [{"row": lax.rem(level + n, 4)} for n in range(1, 4)]
    barrier = pltpu.get_barrier_semaphore()
    for device in [sibling] + crops + levels:
        pl.semaphore_signal(barrier, inc=1, device_id=device, device_id_type=mesh_id)
    pl.semaphore_wait(barrier, 7)

    def copy(source, target, index, device):
        return pltpu.make_async_remote_copy(
            src_ref=source, dst_ref=target, send_sem=send.at[index], recv_sem=recv.at[index],
            device_id=device, device_id_type=mesh_id,
        )

    def run(copies):
        for one in copies:
            one.start()
        for one in copies:
            one.wait()

    half = full_s.shape[0] // 2
    quarter, share = half // 4, half // 16
    row = 0
    for ref in (pair_ref, left_ref, right_ref):
        full_s[row : row + ref.shape[0]] = ref[...]
        row += ref.shape[0]
    full_s[row:] = jnp.zeros((full_s.shape[0] - row, full_s.shape[1]), F32)
    full_s[BIAS_ROW : BIAS_ROW + 1] += share_ref[...]
    base = pl.multiple_of(side * half, 8)
    run([copy(full_s.at[pl.ds(pl.multiple_of((1 - side) * half, 8), half)], core_s, 0, sibling)])
    full_s[pl.ds(base, half)] += core_s[...]
    def part(number):
        return pl.ds(pl.multiple_of(base + number * quarter, 8), quarter)

    run([copy(full_s.at[part(lax.rem(spot + n, 4))], crop_s.at[spot], n, crops[n - 1]) for n in range(1, 4)])
    mine = part(spot)
    crop_s[spot] = full_s[mine]
    full_s[mine] = crop_s[0] + crop_s[1] + crop_s[2] + crop_s[3]
    def slot(number):
        return pl.ds(pl.multiple_of(base + spot * quarter + number * share, 8), share)

    run([copy(full_s.at[slot(lax.rem(level + n, 4))], row_s.at[level], 3 + n, levels[n - 1]) for n in range(1, 4)])
    own = slot(level)
    row_s[level] = full_s[own]
    out_ref[own] = row_s[0] + row_s[1] + row_s[2] + row_s[3]
    run([copy(out_ref.at[own], out_ref.at[own], 6 + n, levels[n - 1]) for n in range(1, 4)])
    run([copy(out_ref.at[mine], out_ref.at[mine], 9 + n, crops[n - 1]) for n in range(1, 4)])
    run([copy(out_ref.at[pl.ds(base, half)], out_ref.at[pl.ds(base, half)], 13, sibling)])


ALL_ROWS = 2048


def reduce_all(share, *parts):
    lanes = share.shape[1]
    return pl.pallas_call(
        reduce_kernel,
        out_shape=jax.ShapeDtypeStruct((ALL_ROWS, lanes), F32),
        scratch_shapes=[
            pltpu.VMEM((ALL_ROWS, lanes), F32),
            pltpu.VMEM((ALL_ROWS // 2, lanes), F32),
            pltpu.VMEM((4, ALL_ROWS // 8, lanes), F32),
            pltpu.VMEM((4, ALL_ROWS // 32, lanes), F32),
            pltpu.SemaphoreType.DMA((14,)),
            pltpu.SemaphoreType.DMA((14,)),
        ],
        compiler_params=pltpu.CompilerParams(
            collective_id=1, has_side_effects=True, vmem_limit_bytes=VMEM_LIMIT
        ),
        name="reduce_all",
    )(share, *parts)


def flip(a, b):
    return 2 * lax.rem(a // 2 + b // 2, 2) + lax.rem(a + b, 2)


def swap_bits(a):
    return 2 * lax.rem(a, 2) + a // 2


def spread_kernel(
    acts_ref, code_ref, w_in, w_out, w_t1, w_t2, w_dist, norms, bias,
    wave0_ref, wave1_ref, x_ref, y_ref, a_ref, b_ref,
    projT, ogT, outT, out_w, t1T, t1, t2T, t2, distT, dist, ln_ref, bias_ref,
    mid, taken, made, fetched, plane_send, plane_recv, share_send, share_recv, level_send, level_recv, local,
    wave_v, a_v, b_v, acts_s, a_s, b_s, code_s,
):
    spot, level = lax.axis_index("crop"), lax.axis_index("row")
    chans = mid.shape[2]
    early, middle = chans // 4, 5 * chans // 8
    cuts = [[(0, early), (early, middle - early), (middle, chans - middle)], [(0, chans)]]
    waves = (wave0_ref, wave1_ref)
    mesh_id = pl.DeviceIdType.MESH

    def block_rows(wave, distance):
        return pl.ds(pl.multiple_of(32 * flip(spot, distance) + 16 * wave, 16), 16)

    def fetch_block(wave, distance):
        return pltpu.make_async_copy(
            acts_ref.at[block_rows(wave, distance)], taken.at[wave, distance], fetched.at[4 * wave + distance]
        )

    def make_block(wave, distance):
        fetch_block(wave, distance).wait()

        def turn_row(row, carry):
            acts_s[row] = jnp.transpose(taken[wave, distance, row])
            return carry

        lax.fori_loop(0, ROWS, turn_row, 0, unroll=8)
        made[wave, distance, : chans - 1] = jnp.swapaxes(acts_s[...], 0, 1)
        made[wave, distance, chans - 1] = code_ref[block_rows(wave, distance), :]

    for wave in range(2):
        for distance in range(4):
            fetch_block(wave, distance).start()
    barrier = pltpu.get_barrier_semaphore()
    for n in range(1, 4):
        for device in ({"crop": lax.rem(spot + n, 4)}, {"row": lax.rem(level + n, 4)}):
            pl.semaphore_signal(barrier, inc=1, device_id=device, device_id_type=mesh_id)
    pl.semaphore_wait(barrier, 6)

    def plane_copy(wave, cut, distance):
        first, count = cuts[wave][cut]
        target = flip(spot, distance)
        source = made.at[wave, distance, pl.ds(first, count)]
        landing = mid.at[wave, distance, pl.ds(first, count)]
        index = 12 * wave + 4 * cut + distance
        if distance == 0:
            return pltpu.make_async_copy(source, landing, plane_recv.at[index])
        return pltpu.make_async_remote_copy(
            src_ref=source, dst_ref=landing, send_sem=plane_send.at[index], recv_sem=plane_recv.at[index],
            device_id={"crop": target}, device_id_type=mesh_id,
        )

    def landed(wave, cut, label):
        first, count = cuts[wave][cut]
        return waves[wave].at[pl.ds(first, count), pl.ds(16 * label, 16)]

    def level_copy(wave, cut, label, distance):
        first, count = cuts[wave][cut]
        source = mid.at[wave, distance, pl.ds(first, count)]
        target = swap_bits(flip(spot, distance))
        index = 12 * wave + 4 * cut + label
        remote = pltpu.make_async_remote_copy(
            src_ref=source, dst_ref=landed(wave, cut, label),
            send_sem=level_send.at[index], recv_sem=level_recv.at[index],
            device_id={"row": target}, device_id_type=mesh_id,
        )
        return target, remote, pltpu.make_async_copy(source, landed(wave, cut, label), local.at[3 * wave + cut])

    def each_level(action, wave, cut):
        for label in range(4):
            for distance in range(4):

                @pl.when(flip(level, label) == distance)
                def _(label=label, distance=distance):
                    action(wave, cut, label, distance)

    def shares(cut, label):
        first, count = cuts[0][cut]
        index = 8 * cut + 2 * label
        return [
            pltpu.make_async_remote_copy(
                src_ref=landed(0, cut, label),
                dst_ref=ref.at[pl.ds(first, count), pl.ds(16 * label, 16)],
                send_sem=share_send.at[index + n], recv_sem=share_recv.at[index + n],
                device_id={"crop": flip(spot, 1 + n)}, device_id_type=mesh_id,
            )
            for n, ref in enumerate((x_ref, y_ref))
        ]

    plane = [
        [[plane_copy(wave, cut, distance) for distance in range(4)] for cut in range(len(cuts[wave]))]
        for wave in range(2)
    ]
    for distance in (1, 3, 2, 0):
        make_block(0, distance)
        plane[0][0][distance].start()
    for copies in plane[0][1:]:
        for one in copies:
            one.start()
    for distance in (1, 3, 2, 0):
        make_block(1, distance)
        plane[1][0][distance].start()

    def begin(wave, cut, label, distance):
        one = plane[wave][cut][distance]
        one.wait() if distance == 0 else one.wait_recv()
        target, remote, stay = level_copy(wave, cut, label, distance)

        @pl.when(target == level)
        def _():
            stay.start()

        @pl.when(target != level)
        def _():
            remote.start()

    def arrive(wave, cut, label, distance):
        target, remote, stay = level_copy(wave, cut, label, distance)

        @pl.when(target == level)
        def _():
            stay.wait()

        @pl.when(target != level)
        def _():
            remote.wait_recv()
            remote.wait_send()

    def pass_on(cut):
        each_level(arrive, 0, cut)
        for label in range(4):
            for one in shares(cut, label):
                one.start()

    each_level(begin, 0, 0)
    prepare_weights(
        w_in, w_out, w_t1, w_t2, w_dist, norms, bias,
        (projT, ogT, outT, out_w, t1T, t1, t2T, t2, distT, dist, ln_ref, bias_ref),
    )
    each_level(begin, 0, 1)
    each_level(begin, 0, 2)
    each_level(begin, 1, 0)
    for cut in range(3):
        pass_on(cut)
    fetch = pltpu.make_async_copy(wave0_ref, wave_v, local.at[4])
    fetch.start()
    fetch.wait()
    width = a_v.shape[0]

    def project_rows(step, carry):
        rows = pl.ds(pl.multiple_of(step * ROWS, ROWS), ROWS)
        project_kernel(
            wave_v.at[pl.ds(0, width), rows], wave_v.at[pl.ds(width, 1), rows], projT, ln_ref,
            a_v.at[:, rows], b_v.at[:, rows], acts_s, a_s, b_s, code_s,
        )
        return carry

    lax.fori_loop(0, wave_v.shape[1] // ROWS, project_rows, 0)
    results = [
        pltpu.make_async_copy(a_v, a_ref, local.at[5]), pltpu.make_async_copy(b_v, b_ref, local.at[6])
    ]
    for one in results:
        one.start()
    for copies in plane[0] + plane[1]:
        for one in copies[1:]:
            one.wait_send()
    for cut in range(3):
        for label in range(4):
            for one in shares(cut, label):
                one.wait()
    for one in results:
        one.wait()
    each_level(arrive, 1, 0)


def spread(acts, code, w_in, w_out, w_t1, w_t2, w_dist, norms, bias):
    rows, lanes, width = acts.shape
    chans, half = width + 1, rows // 2
    anywhere = pl.BlockSpec(memory_space=pl.ANY)
    whole = pl.BlockSpec(memory_space=pltpu.VMEM)
    staged = pltpu.VMEM((ROWS, width, lanes), BF16)
    shapes = [(4 * width, width), (width, width)]
    for weight in (w_out, w_t1, w_t2, w_dist):
        shapes += [(weight.shape[1], weight.shape[0]), weight.shape]
    shapes = [jax.ShapeDtypeStruct(shape, BF16) for shape in shapes]
    shapes += [jax.ShapeDtypeStruct((6, width, 128), F32), jax.ShapeDtypeStruct((bias.shape[0], 128), F32)]
    return pl.pallas_call(
        spread_kernel,
        in_specs=[anywhere] + [whole] * 8,
        out_specs=[anywhere] * 6 + [whole] * len(shapes),
        out_shape=[jax.ShapeDtypeStruct((chans, half, lanes), BF16)] * 4
        + [jax.ShapeDtypeStruct((width, half, lanes), BF16)] * 2
        + shapes,
        scratch_shapes=[pltpu.VMEM((2, 4, chans, ROWS, lanes), BF16)]
        + [pltpu.VMEM((2, 4, ROWS, lanes, width), BF16)]
        + [pltpu.VMEM((2, 4, chans, ROWS, lanes), BF16)]
        + [pltpu.SemaphoreType.DMA((8,))]
        + [pltpu.SemaphoreType.DMA((16,)) for _ in range(2)]
        + [pltpu.SemaphoreType.DMA((24,)) for _ in range(2)]
        + [pltpu.SemaphoreType.DMA((16,)) for _ in range(2)]
        + [pltpu.SemaphoreType.DMA((7,))]
        + [pltpu.VMEM((chans, half, lanes), BF16)]
        + [pltpu.VMEM((width, half, lanes), BF16)] * 2
        + [staged] * 3
        + [pltpu.VMEM((ROWS, lanes), F32)],
        compiler_params=pltpu.CompilerParams(
            collective_id=2, has_side_effects=True, vmem_limit_bytes=VMEM_LIMIT
        ),
        name="spread",
    )(acts, code, w_in, w_out, w_t1, w_t2, w_dist.T, norms, bias.reshape(1, -1))


def update_kernel(early_ref, *refs):
    ins, outs = refs[:21], refs[21:]
    left_ref = early_ref.at[pl.ds(SUM_ROWS, SIDE_ROWS)]
    right_ref = early_ref.at[pl.ds(SUM_ROWS + SIDE_ROWS, SIDE_ROWS)]
    loss_ref, total_ref, norm_ref = outs[21:]
    total = early_ref[LOSS_ROW - 1, 127]
    inverse = 1.0 / total
    half = SIDE_ROWS - 16
    grads = [
        jnp.concatenate(
            [
                jnp.transpose(left_ref[:half]),
                jnp.transpose(right_ref[:half]),
                jnp.transpose(early_ref[OG_ROW : OG_ROW + 128]),
            ],
            1,
        ),
        jnp.transpose(early_ref[OUT_ROW : OUT_ROW + 128]),
        jnp.transpose(early_ref[T1_ROW : T1_ROW + 512]),
        early_ref[T2_ROW : T2_ROW + 512],
        early_ref[DIST_ROW : DIST_ROW + 64],
        jnp.concatenate(
            [
                left_ref[half : half + 2] + right_ref[half : half + 2] + early_ref[NORM_ROW + 4 : NORM_ROW + 6],
                early_ref[NORM_ROW : NORM_ROW + 4],
            ],
            0,
        ),
        early_ref[BIAS_ROW : BIAS_ROW + 1, :64],
    ]
    grads = [grad * inverse for grad in grads]
    squares = sum(jnp.sum(grad * grad, keepdims=True).reshape(1, 1) for grad in grads)
    grad_norm = jnp.sqrt(squares)
    scale = CLIP_NORM / jnp.maximum(grad_norm, CLIP_NORM)
    rates = (LEARN_RATE,) * 5 + (GAIN_RATE,) * 2
    for index in range(7):
        new = adamw_update(
            *[ins[7 * part + index][...].reshape(grads[index].shape) for part in range(3)],
            grads[index], scale, rates[index],
        )
        for part in range(3):
            outs[7 * part + index][...] = new[part].reshape(outs[7 * part + index].shape)
    norm_ref[...] = grad_norm
    loss_ref[...] = jnp.sum(early_ref[LOSS_ROW : LOSS_ROW + 1], keepdims=True).reshape(1, 1)
    total_ref[...] = jnp.full((1, 1), total, F32)


def update(early, params, firsts, seconds):
    flat = [v.T if index % 7 == 4 else v for index, v in enumerate((*params, *firsts, *seconds))]
    shapes = [v.shape for v in flat] + [(1, 1)] * 3
    outs = pl.pallas_call(
        update_kernel,
        out_shape=[jax.ShapeDtypeStruct(s, F32) for s in shapes],
        compiler_params=pltpu.CompilerParams(vmem_limit_bytes=VMEM_LIMIT),
        name="update",
    )(early, *flat)
    outs = [v.T if index in (4, 11, 18) else v for index, v in enumerate(outs)]
    return (*outs[:21], *[v[0, 0] for v in outs[21:]])


def after(value, *earlier):
    return lax.optimization_barrier((value, *earlier))[0]


def on_device_planes(
    pair_acts, residue_mask, dist_bins, w_in, w_out, w_t1, w_t2, w_dist, norm_params, dist_bias, *moments
):
    firsts, seconds = moments[:7], moments[7:]
    spot = lax.axis_index("crop")
    level = lax.axis_index("row")
    side = lax.axis_index("col")
    rows, cols, chans = pair_acts.shape[1:]
    width = w_out.shape[0]
    sub = rows // 4
    plane_of = (0, 2, 1, 3)
    crop = (level % 2) * 2 + level // 2

    def over_x(v):
        return lax.ppermute(v, "crop", [(g, g ^ 1) for g in range(4)])

    def over_y(v):
        return lax.ppermute(v, "crop", [(g, g ^ 2) for g in range(4)])

    def over_both(v):
        return lax.ppermute(v, "crop", [(g, g ^ 3) for g in range(4)])

    def over_core(v):
        return lax.ppermute(v, "col", [(0, 1), (1, 0)])

    own_mask = residue_mask[0]
    row_own = lax.dynamic_slice_in_dim(own_mask, rows * level, rows)
    col_own = lax.dynamic_slice_in_dim(own_mask, cols * side, cols)
    code_own = jnp.where((row_own[:, None] * col_own[None, :]) > 0, dist_bins[0], -1).astype(BF16)

    wave0, wave1, wave0_x, wave0_y, left_own, right_own, proj_w, *weights, ln_wide, bias_wide = spread(
        pair_acts[0], code_own, w_in, w_out, w_t1, w_t2, w_dist, norm_params, dist_bias
    )
    og_T, out_T, out_w, t1_T, t1_w, t2_T, t2_w, dist_T, dist_w = weights
    weights = (out_T, out_w, og_T, t1_T, t1_w, t2_T, t2_w, dist_T, dist_w)

    count = jnp.sum(own_mask).astype(F32)
    share_count = lax.axis_size("row") * lax.axis_size("col")
    acts, left, right = {}, {}, {}

    def share(q, source, shift, half):
        acts[q, half] = shift(acts[source, half])

    def values(q, half, *earlier):
        left[q, half], right[q, half] = project(after(acts[q, half], *earlier), proj_w, ln_wide)
        return right[q, half]

    acts[0, 0], acts[0, 1], acts[1, 0], acts[2, 0] = wave0, wave1, wave0_x, wave0_y
    share(1, 0, over_x, 1)
    share(2, 0, over_y, 1)
    left[0, 0], right[0, 0] = left_own, right_own
    done = values(0, 1)

    ids = jnp.stack([spot, crop, side]).astype(jnp.int32)
    def values_two(one, two, *earlier):
        results = project_two(after(acts[one], *earlier), acts[two], proj_w, ln_wide)
        left[one], right[one], left[two], right[two] = results
        return results[0]

    keeps, recvs, dx_own, dx_other, seen, seen_other = {}, {}, {}, {}, {}, {}
    sums = []

    def forward(q, *earlier):
        keeps[q], send = triangle(
            q, after(ids, *earlier), [left[0, h] for h in range(2)], [right[q, h] for h in range(2)]
        )
        recvs[q] = over_core(send)
        return send

    def middle(q, *earlier):
        dx_own[q], *sums[:] = pair_block(
            q, after(ids, *earlier), keeps[q], recvs[q], acts_kj, ln_wide, weights, bias_wide, list(sums), q == 3
        )
        dx_other[q] = over_core(dx_own[q])
        seen[q] = (lambda v: v, over_x, over_y, over_both)[q](dx_own[q])
        seen_other[q] = over_core(seen[q]) if q in (1, 2) else dx_other[q]
        return dx_own[q]

    done = forward(0, done)
    acts_kj = turn(after(acts[0, 0], done), acts[0, 1])
    done = values_two((1, 0), (2, 0), acts_kj)
    done = middle(0, done)
    acts[1, 1], acts[2, 1] = after(acts[1, 1], done), after(acts[2, 1], done)
    acts[3, 0] = over_y(after(acts[1, 0], done))
    acts[3, 1] = over_x(acts[2, 1])
    done = values(1, 1, done)
    done = forward(1, done)
    done = values(2, 1, done)
    done = forward(2, done)
    done = middle(1, done)
    done = middle(2, done)
    done = values_two((3, 0), (3, 1), done)
    done = forward(3, done)
    done = middle(3, done, seen[1], seen[2])
    d_left = left_back(
        after(ids, done, seen_other[1]),
        [dx_own[q] for q in range(4)],
        [dx_other[q] for q in range(4)],
        [right[q, 0] for q in range(4)],
        [right[q, 1] for q in range(4)],
    )
    share = jnp.where(jnp.arange(128) == 127, count * count / share_count, 0.0)[None]
    left_sum = []
    for h in range(2):
        left_sum = input_back([(acts[0, h], d_left[h])], 0, proj_w, ln_wide, left_sum, h == 1)
        if h == 0:
            seen_other[3] = over_core(after(seen[3], left_sum[0]))
    d_right = right_back(
        after(ids, left_sum[0], seen_other[2]),
        [seen[q] for q in range(4)],
        [seen_other[q] for q in range(4)],
        [left[q, 0] for q in range(4)],
        [left[q, 1] for q in range(4)],
    )
    right_sum = input_back([(acts[0, h], d_right[h]) for h in range(2)], 1, proj_w, ln_wide, [], True)
    params = (w_in, w_out, w_t1, w_t2, w_dist, norm_params, dist_bias)
    return update(reduce_all(share, sums[0], left_sum[0], right_sum[0]), params, firsts, seconds)


def solution(mesh):
    planes = mesh.shape["crop"] == 4 and mesh.shape["row"] == 4 and mesh.shape["col"] == 2
    body = on_device_planes if planes else on_device_general
    in_specs = (
        P("crop", "row", "col", None),
        P("crop", None),
        P("crop", "row", "col"),
    ) + (P(),) * 21
    return jax.shard_map(
        body, mesh=mesh, in_specs=in_specs, out_specs=(P(),) * 24, check_vma=False
    )
```
